32 devices in a mesh: clus: 4 (over y, x), blk: 8 (over z, core).
Axes of the slice: x: 2, y: 2, z: 4, core: 2. Of those that a mesh axis runs over, the one named last changes fastest.
Arguments:
- leaf_basis: bfloat16 [256, 256, 128], P(('clus', 'blk')), may hold values from -6 to 6
- transfer: float32 [256, 128, 256], P(('clus', 'blk')), may hold values from -0.08 to 1.68
- block_rows: bfloat16 [512, 256, 192], P(('clus', 'blk')), may hold values from -6 to 6
- block_cols: bfloat16 [512, 256, 192], P(('clus', 'blk')), may hold values from -0.4375 to 0.4375
- rank_slabs: int32 [512], P(('clus', 'blk')), may hold values from 1 to 3, as said below
- row_leaf: int32 [512], P(('clus', 'blk')), may hold values from 0 to 63
- col_group: int32 [512, 1], P(('clus', 'blk')), may hold values from 0 to 3; in each aligned block of 16 rows (0 to 15, 16 to 31, ...) at most 8 rows name the same one
- col_leaf: int32 [512], P(('clus', 'blk')), may hold values from 0 to 63
Outputs:
- coupling: float32 [512, 128, 128], P(('clus', 'blk'))
- transfer_new: float32 [256, 128, 256], P(('clus', 'blk'))
The draws below stay inside these ranges and needn't reach their ends.
Inputs may be any that keep to these rules, and one draw needn't show every extreme that they name: `col_group`: among the 16 blocks of one device at most 8 have the same column group. `rank_slabs`: some block has 3 granules and some has one.
All inputs are finite; a program needn't handle non-finite values.
Results may differ from the reference program's by a relative error of at most 0.0058.
Values may be sent and summed in bfloat16 or wider, within the bound.
No kernel may reach another device: no remote copies, remote signals or barrier semaphores. Data moves between devices by JAX's collectives and lax.ppermute only.
A program may use at most 128 MiB of HBM per device.

```python
import math
import jax
import jax.numpy as jnp
import numpy as np
from jax import lax

LEAF_RANK = 128
PARENT_RANK = 256
POINTS = 256
SLAB = 64
SLABS = 3
LEAF_DEV = 8
BLOCK_DEV = 16
RANK_MAX = 192
LEAVES = 256
GROUP_LEAVES = 64
BLOCKS = 512
CAPACITY = 8
N_CLUS = 4
N_BLK = 8


def draw_transfer(key, part):
    key_diag, key_jitter = jax.random.split(key)
    diag_gain = jnp.exp(jax.random.uniform(key_diag, (LEAVES, LEAF_RANK), jnp.float32, 0.0, jnp.log(1.6)))
    jitter = jax.random.truncated_normal(key_jitter, -3.0, 3.0, (LEAVES, LEAF_RANK, PARENT_RANK), jnp.float32)
    jitter = jitter * 0.025
    slot_index = jnp.arange(LEAVES, dtype=jnp.int32) % LEAF_DEV
    upper_half = (slot_index >= LEAF_DEV // 2).astype(jnp.int32)
    row_index = lax.broadcasted_iota(jnp.int32, (LEAVES, LEAF_RANK, PARENT_RANK), 1)
    column = lax.broadcasted_iota(jnp.int32, (LEAVES, LEAF_RANK, PARENT_RANK), 2)
    on_diag = column == row_index + upper_half[:, None, None] * LEAF_RANK
    return jitter + jnp.where(on_diag, diag_gain[:, :, None], 0.0)


def draw_rank_slabs(key, part):
    key_base, key_top, key_low = jax.random.split(key, 3)
    slab_counts = jax.random.randint(key_base, (BLOCKS,), 1, SLABS + 1, dtype=jnp.int32)
    top_at = jax.random.randint(key_top, (), 0, BLOCKS, dtype=jnp.int32)
    low_at = (top_at + jax.random.randint(key_low, (), 1, BLOCKS, dtype=jnp.int32)) % BLOCKS
    places = jnp.arange(BLOCKS, dtype=jnp.int32)
    slab_counts = jnp.where(places == top_at, SLABS, slab_counts)
    return jnp.where(places == low_at, 1, slab_counts).astype(jnp.int32)


def place_ends(entries, key, smallest, top_value):
    longest = entries.shape.index(max(entries.shape))
    spots = []
    for shift in (0, 1):
        where = [jax.random.randint(jax.random.fold_in(key, axis), (), 0, length) for axis, length in enumerate(entries.shape)]
        where[longest] = (where[longest] + shift) % entries.shape[longest]
        spots.append(tuple(where))
    return entries.at[spots[0]].set(smallest).at[spots[1]].set(top_value)


def steps_of(stream_key, extent, cuts, low, high):
    loudness = 1.0
    for position, blocks in cuts:
        steps = jax.random.uniform(jax.random.fold_in(jax.random.fold_in(stream_key, 6), position), (blocks,), jnp.float32, low / len(cuts), high / len(cuts))
        loudness = loudness * jnp.repeat(jnp.exp(steps), extent[position] // blocks).reshape((-1,) + (1,) * (len(extent) - 1 - position))
    return loudness


def assign_block(rng, own, number, rows, amount, top, reach, slope):
    sequence = jax.random.permutation(rng, amount)
    crowded, usual = portions_of(amount, rows * top, reach, slope, True), portions_of(amount, rows * top, reach, slope, False)
    places = jnp.arange(amount)

    def named(sizes, rotation):
        used = int((sizes > 0).sum())
        fixed = max(1, used // 4)
        shifted = fixed + (places - fixed + rotation * (used - fixed)) % max(1, amount - fixed)
        return jnp.zeros((amount,), jnp.int32).at[sequence[jnp.where(places < fixed, places, shifted)]].set(jnp.asarray(sizes, jnp.int32))

    sizes = jnp.where(number % 4 == 0, named(crowded, number // 4), named(usual, number - number // 4 - 1))
    mixed = jax.random.permutation(jax.random.fold_in(own, 3), amount)
    source_of, taker = mixed[0:amount // 2 * 2:2], mixed[1:amount // 2 * 2:2]
    margin = jnp.minimum(sizes[source_of] - 1, reach - sizes[taker]) // 2
    margin = jnp.where((source_of == sequence[0]) | (taker == sequence[0]) | (sizes[taker] == 0), 0, jnp.maximum(margin, 0))
    shifted = jax.random.randint(jax.random.fold_in(own, 4), (amount // 2,), 0, 1 << 20) % (margin + 1)
    sizes = sizes.at[source_of].add(-shifted).at[taker].add(shifted)
    labels = jnp.searchsorted(jnp.cumsum(sizes), jnp.arange(rows * top), side="right").astype(jnp.int32)
    grid = labels.reshape(top, rows).T
    grid = grid[jax.random.permutation(jax.random.fold_in(own, 1), rows)]
    rotation = jax.random.randint(jax.random.fold_in(own, 2), (rows, 1), 0, top)
    return jnp.take_along_axis(grid, (jnp.arange(top)[None, :] + rotation) % top, axis=1)


def portions_of(amount, total, limit, lean, full):
    loads = [(1 << 20) // math.isqrt(rank ** lean) + 1 for rank in range(1, amount + 1)]
    largest = limit if full else min(limit, max(-(-total // amount), total * loads[0] // sum(loads)))
    least = 1 if total - largest >= amount - 1 else 0
    counts, surplus = [largest] + [least] * (amount - 1), total - largest - least * (amount - 1)
    while surplus > 0:
        candidates = [i for i in range(1, amount) if counts[i] < largest] or [i for i in range(1, amount) if counts[i] < limit]
        whole, remaining = sum([loads[i] for i in candidates]), surplus
        for i in candidates:
            more = min(limit - counts[i], max(1, remaining * loads[i] // whole), surplus)
            counts[i] = counts[i] + more
            surplus = surplus - more
    return np.array(counts)


def normal_values(own_key, extent, width, bound, cuts=(), held_as=jnp.bfloat16):
    result = jax.random.normal(own_key, extent, jnp.float32) * width
    if len(cuts) > 0:
        result = steps_of(own_key, extent, cuts, -0.22, 0.18) * result
    return jnp.clip(result, min=-bound, max=bound).astype(held_as)


def setup_inputs(seed: int = 0) -> dict:
    streams_of = jax.random.split(jax.random.key(seed), 9)
    leaf_basis = normal_values(streams_of[0], (LEAVES, POINTS, LEAF_RANK), 1.0, 6.0, ((0, 32),))
    transfer = draw_transfer(jax.random.fold_in(streams_of[8], 71), 0)
    block_rows = normal_values(streams_of[2], (BLOCKS, POINTS, RANK_MAX), 1.0, 6.0, ((0, 32),))
    block_cols = normal_values(streams_of[3], (BLOCKS, POINTS, RANK_MAX), RANK_MAX ** -0.5, 0.4375, ((0, 32),))
    rank_slabs = draw_rank_slabs(jax.random.fold_in(streams_of[8], 71), 0)
    row_leaf = place_ends(jax.random.randint(streams_of[5], (BLOCKS,), 0, GROUP_LEAVES), jax.random.fold_in(streams_of[5], 1), 0, GROUP_LEAVES - 1).astype(jnp.int32)
    col_group_keys = jax.random.split(jax.random.fold_in(streams_of[6], 1), BLOCKS // BLOCK_DEV)
    col_group_turns = jax.random.permutation(jax.random.fold_in(streams_of[6], 3), BLOCKS // BLOCK_DEV)
    col_group = jax.vmap(lambda own, number: assign_block(jax.random.fold_in(streams_of[6], 2), own, number, BLOCK_DEV, N_CLUS, 1, CAPACITY, 2))(col_group_keys, col_group_turns).reshape((BLOCKS, 1))
    col_leaf = place_ends(jax.random.randint(streams_of[7], (BLOCKS,), 0, GROUP_LEAVES), jax.random.fold_in(streams_of[7], 1), 0, GROUP_LEAVES - 1).astype(jnp.int32)
    return {"leaf_basis": leaf_basis, "transfer": transfer, "block_rows": block_rows, "block_cols": block_cols, "rank_slabs": rank_slabs, "row_leaf": row_leaf, "col_group": col_group, "col_leaf": col_leaf}


def reference(leaf_basis, transfer, block_rows, block_cols, rank_slabs, row_leaf, col_group, col_leaf):
    leaf_float = leaf_basis.astype(jnp.float32)
    gram_leaf = jnp.einsum('npk,npq->nkq', leaf_float, leaf_float, precision=lax.Precision.HIGHEST)
    lower_leaf = jnp.linalg.cholesky(gram_leaf)
    basis_rows = jax.scipy.linalg.solve_triangular(lower_leaf, jnp.swapaxes(leaf_float, 1, 2), lower=True)
    basis_rows = basis_rows.astype(jnp.bfloat16)
    stacked = jnp.einsum('nqk,nqj->nkj', lower_leaf, transfer, precision=lax.Precision.HIGHEST)
    devices = LEAVES // LEAF_DEV
    half_count = LEAF_DEV // 2
    per_device = stacked.reshape(devices, LEAF_DEV, LEAF_RANK, PARENT_RANK)
    partner = per_device.reshape(devices // 2, 2, LEAF_DEV, LEAF_RANK, PARENT_RANK)[:, ::-1].reshape(per_device.shape)
    first_child = per_device[:, :half_count]
    second_child = partner[:, half_count:]
    gram_parent = jnp.einsum('dmkj,dmki->dmji', first_child, first_child, precision=lax.Precision.HIGHEST)
    gram_parent = gram_parent + jnp.einsum('dmkj,dmki->dmji', second_child, second_child, precision=lax.Precision.HIGHEST)
    lower_parent = jnp.linalg.cholesky(gram_parent)
    swapped = lower_parent.reshape(devices // 2, 2, half_count, PARENT_RANK, PARENT_RANK)[:, ::-1].reshape(lower_parent.shape)
    lower_all = jnp.concatenate([lower_parent, swapped], axis=1)
    new_rows = jax.scipy.linalg.solve_triangular(lower_all, jnp.swapaxes(per_device, 2, 3), lower=True)
    transfer_new = jnp.swapaxes(new_rows, 2, 3).reshape(LEAVES, LEAF_RANK, PARENT_RANK)
    block_ids = jnp.arange(BLOCKS, dtype=jnp.int32)
    row_cluster = (block_ids // (BLOCK_DEV * N_BLK) * GROUP_LEAVES + row_leaf).astype(jnp.int32)
    col_cluster = (col_group[:, 0] * GROUP_LEAVES + col_leaf).astype(jnp.int32)
    widths = (rank_slabs * SLAB).astype(jnp.int32)
    batches = BLOCKS // BLOCK_DEV

    def one_batch(pieces):
        rows_part, cols_part, row_ids, col_ids, width_part = pieces
        live_cols = jnp.arange(RANK_MAX, dtype=jnp.int32)[None, None, :] < width_part[:, None, None]
        rows_live = jnp.where(live_cols, rows_part, jnp.zeros_like(rows_part)).astype(jnp.float32)
        cols_live = jnp.where(live_cols, cols_part, jnp.zeros_like(cols_part)).astype(jnp.float32)
        row_basis = basis_rows[row_ids].astype(jnp.float32)
        col_basis = basis_rows[col_ids].astype(jnp.float32)
        near_proj = jnp.einsum('bkp,bpr->bkr', row_basis, rows_live, precision=lax.Precision.HIGHEST).astype(jnp.bfloat16)
        far_proj = jnp.einsum('bkp,bpr->bkr', col_basis, cols_live, precision=lax.Precision.HIGHEST).astype(jnp.bfloat16)
        near_proj = lax.optimization_barrier(near_proj)
        far_proj = lax.optimization_barrier(far_proj)
        return jnp.einsum('bkr,bjr->bkj', near_proj.astype(jnp.float32), far_proj.astype(jnp.float32), precision=lax.Precision.HIGHEST)
    coupling = lax.map(one_batch, (block_rows.reshape(batches, BLOCK_DEV, POINTS, RANK_MAX), block_cols.reshape(batches, BLOCK_DEV, POINTS, RANK_MAX), row_cluster.reshape(batches, BLOCK_DEV), col_cluster.reshape(batches, BLOCK_DEV), widths.reshape(batches, BLOCK_DEV)))
    coupling = coupling.reshape(BLOCKS, LEAF_RANK, LEAF_RANK)
    return (coupling, transfer_new)
```

```python
import functools

import jax
import jax.numpy as jnp
from jax import lax
from jax.experimental import pallas as pl
from jax.experimental.pallas import tpu as pltpu
from jax.sharding import PartitionSpec as P

SLAB = 64
PANEL = 8
STRIP = 32
VMEM_LIMIT = 40 * 1024 * 1024

NN = (((1,), (0,)), ((), ()))
NT = (((1,), (1,)), ((), ()))
TN = (((0,), (0,)), ((), ()))


def params():
    return pltpu.CompilerParams(vmem_limit_bytes=VMEM_LIMIT)


def cost(flops, moved):
    return pl.CostEstimate(flops=flops, bytes_accessed=moved, transcendentals=0)


def dot(left, right, dims):
    return lax.dot_general(left, right, dims, preferred_element_type=jnp.float32)


def split(value):
    high = value.astype(jnp.bfloat16)
    low = (value - high.astype(jnp.float32)).astype(jnp.bfloat16)
    return high, low


def dot_split(left, right, dims):
    (lh, ll), (rh, rl) = left, right
    return dot(lh, rh, dims) + (dot(lh, rl, dims) + dot(ll, rh, dims))


def lower_part(value):
    rows = lax.broadcasted_iota(jnp.int32, value.shape, 0)
    cols = lax.broadcasted_iota(jnp.int32, value.shape, 1)
    return jnp.where(cols <= rows, value, 0.0)


def factor(work, batch, size):
    lane = lax.broadcasted_iota(jnp.int32, (batch, size), 1)

    def spread(row, column):
        return jnp.broadcast_to(row[:, column : column + 1], (batch, size))

    for top in range(0, size, STRIP):
        rows = [work[pl.ds(top + i, batch, stride=size), :] for i in range(STRIP)]
        for q in range(0, STRIP, PANEL):
            first = top + q
            inside = (lane >= first) & (lane < first + PANEL)
            diag = {
                (i, j): spread(rows[q + i], first + j) for i in range(PANEL) for j in range(i, PANEL)
            }
            scale, upper = [], {}
            for k in range(PANEL):
                inv = lax.rsqrt(diag[k, k])
                scale.append(inv)
                for j in range(k + 1, PANEL):
                    upper[k, j] = diag[k, j] * inv
                for i in range(k + 1, PANEL):
                    for j in range(i, PANEL):
                        diag[i, j] = diag[i, j] - upper[k, i] * upper[k, j]
            done = []
            for k in range(PANEL):
                row = jnp.where(inside, jnp.where(lane == first + k, 1.0, 0.0), rows[q + k])
                for m in range(k):
                    row = row - upper[m, k] * done[m]
                done.append(row * scale[k])
            rows[q : q + PANEL] = done
            for i in range(q + PANEL, STRIP):
                row = jnp.where(inside, 0.0, rows[i])
                for k in range(PANEL):
                    row = row - spread(done[k], top + i) * done[k]
                rows[i] = row
        for i in range(STRIP):
            work[pl.ds(top + i, batch, stride=size), :] = rows[i]
        below = top + STRIP
        if below < size:
            for b in range(batch):
                strip = work[b * size + top : b * size + below, :]
                row = lax.broadcasted_iota(jnp.int32, strip.shape, 0) + top
                column = lax.broadcasted_iota(jnp.int32, strip.shape, 1)
                keep = (column <= row) | (column >= below)
                high, low = split(strip)
                left = jnp.concatenate([high, high, low], axis=0)
                high, low = split(jnp.where(keep, strip, 0.0))
                right = jnp.concatenate([high, low, high], axis=0)
                rest = work[b * size + below : (b + 1) * size, :]
                column = lax.broadcasted_iota(jnp.int32, rest.shape, 1)
                rest = jnp.where((column >= top) & (column < below), 0.0, rest)
                work[b * size + below : (b + 1) * size, :] = rest - dot(left, right, TN)[below:]


def leaf_kernel(basis, rows_out, work):
    count, points, rank = basis.shape
    for b in range(count):
        leaf = basis[b]
        work[b * rank : (b + 1) * rank, :] = dot(leaf, leaf, TN)
    factor(work, count, rank)
    for b in range(count):
        high, low = split(lower_part(work[b * rank : (b + 1) * rank, :]))
        leaf = basis[b]
        rows_out[b] = (dot(high, leaf, NT) + dot(low, leaf, NT)).astype(rows_out.dtype)


def parent_top_kernel(own_basis, own_transfer, far_basis, far_transfer, weighted, top, cross, corner):
    count, points, rank = own_basis.shape
    half = own_transfer.shape[2] // 2
    for j in range(count):
        other = (j + count // 2) % count
        total = None
        for basis, transfer, c in ((own_basis, own_transfer, j), (far_basis, far_transfer, other)):
            leaf = basis[c]
            gram = split(dot(leaf, leaf, TN))
            value = transfer[c]
            moved = dot_split(gram, split(value), NN)
            if basis is own_basis:
                weighted[c] = moved
            left, right = split(value[:, :half]), split(value[:, half:])
            moved_left, moved_right = split(moved[:, :half]), split(moved[:, half:])
            parts = (
                dot_split(left, moved_left, TN),
                dot_split(right, moved_left, TN),
                dot_split(right, moved_right, TN),
            )
            total = parts if total is None else tuple(a + b for a, b in zip(total, parts))
        top[j * half : (j + 1) * half, :] = total[0]
        cross[j] = total[1]
        corner[j] = total[2]
    factor(top, count, half)


def parent_low_kernel(leaf_work, weighted, top, cross, corner, out, work, coupled):
    count, rank, columns = weighted.shape
    half = columns // 2
    for j in range(count):
        inverse = split(lower_part(top[j * half : (j + 1) * half, :]))
        lower = dot_split(split(cross[j]), inverse, NT)
        coupled[j] = lower
        lower = split(lower)
        work[j * half : (j + 1) * half, :] = corner[j] - dot_split(lower, lower, NT)
    factor(work, count, half)
    for j in range(count):
        leaf_inverse = split(lower_part(leaf_work[j * rank : (j + 1) * rank, :]))
        stacked = dot_split(leaf_inverse, split(weighted[j]), NN)
        inverse = split(lower_part(top[j * half : (j + 1) * half, :]))
        first = dot_split(split(stacked[:, :half]), inverse, NT)
        rest = stacked[:, half:] - dot_split(split(first), split(coupled[j]), NT)
        inverse = split(lower_part(work[j * half : (j + 1) * half, :]))
        out[j, :, :half] = first
        out[j, :, half:] = dot_split(split(rest), inverse, NT)


def leaf_stage(leaf_basis):
    count, points, rank = leaf_basis.shape
    return pl.pallas_call(
        leaf_kernel,
        out_shape=(
            jax.ShapeDtypeStruct((count, rank, points), jnp.bfloat16),
            jax.ShapeDtypeStruct((count * rank, rank), jnp.float32),
        ),
        compiler_params=params(),
        cost_estimate=cost(10**9, 10**7),
        name="leaf_factor",
    )(leaf_basis)


def parent_stage(leaf_basis, transfer, far_basis, far_transfer, leaf_work):
    count, points, rank = leaf_basis.shape
    columns = transfer.shape[2]
    half = columns // 2
    weighted, top, cross, corner = pl.pallas_call(
        parent_top_kernel,
        out_shape=(
            jax.ShapeDtypeStruct((count, rank, columns), jnp.float32),
            jax.ShapeDtypeStruct((count * half, half), jnp.float32),
            jax.ShapeDtypeStruct((count, half, half), jnp.float32),
            jax.ShapeDtypeStruct((count, half, half), jnp.float32),
        ),
        compiler_params=params(),
        cost_estimate=cost(10**9, 4 * 10**7),
        name="parent_top",
    )(leaf_basis, transfer, far_basis, far_transfer)
    return pl.pallas_call(
        parent_low_kernel,
        out_shape=jax.ShapeDtypeStruct(transfer.shape, jnp.float32),
        scratch_shapes=[
            pltpu.VMEM((count * half, half), jnp.float32),
            pltpu.VMEM((count, half, half), jnp.float32),
        ],
        compiler_params=params(),
        cost_estimate=cost(10**9, 4 * 10**7),
        name="parent_low",
    )(leaf_work, weighted, top, cross, corner)


def serve_kernel(groups, *refs):
    asked, table, outs = refs[: groups - 1], refs[groups - 1], refs[groups : 2 * groups - 1]
    sem, tally = refs[2 * groups - 1 :]
    me = lax.axis_index("clus")
    leaves = table.shape[0]
    count = asked[0].shape[0]
    tally[0] = 0
    for d in range(1, groups):

        def place(b, position, d=d):
            code = asked[d - 1][b]
            mine = (code // leaves) == me

            @pl.when(mine)
            def _():
                leaf = code % leaves
                pltpu.make_async_copy(table.at[leaf], outs[d - 1].at[position], sem).start()

            return position + mine.astype(jnp.int32)

        tally[0] += lax.fori_loop(0, count, place, jnp.int32(0))

    def finish(_, carry):
        pltpu.make_async_copy(table.at[0], outs[0].at[0], sem).wait()
        return carry

    lax.fori_loop(0, tally[0], finish, 0)


def partner(index, d, groups):
    if groups & (groups - 1) == 0:
        return index ^ d
    return lax.rem(index + d, groups)


def serve(asked, table, capacity):
    groups = len(asked) + 1
    return pl.pallas_call(
        functools.partial(serve_kernel, groups),
        in_specs=[pl.BlockSpec(memory_space=pltpu.SMEM)] * (groups - 1)
        + [pl.BlockSpec(memory_space=pl.ANY)],
        out_specs=[pl.BlockSpec(memory_space=pl.ANY)] * (groups - 1),
        out_shape=[jax.ShapeDtypeStruct((capacity,) + table.shape[1:], table.dtype)] * (groups - 1),
        scratch_shapes=[pltpu.SemaphoreType.DMA, pltpu.SMEM((1,), jnp.int32)],
        compiler_params=params(),
        cost_estimate=cost(0, 4 * 10**6),
        name="serve",
    )(*asked, table)


def near_kernel(leaf, slabs, table, factors, out, held, sem):
    count, width, points = factors.shape

    def begin(b, carry):
        pltpu.make_async_copy(table.at[leaf[b]], held.at[b], sem.at[b]).start()
        return carry

    lax.fori_loop(0, count, begin, 0)
    column = lax.broadcasted_iota(jnp.int32, (out.shape[1], width), 1)
    for b in range(count):
        pltpu.make_async_copy(table.at[0], held.at[b], sem.at[b]).wait()
        value = dot(held[b], factors[b], NT)
        out[b] = jnp.where(column < slabs[b] * SLAB, value, 0.0).astype(out.dtype)


def near_stage(row_leaf, rank_slabs, table, factors):
    count, width, points = factors.shape
    rank = table.shape[1]
    smem = pl.BlockSpec(memory_space=pltpu.SMEM)
    vmem = pl.BlockSpec(memory_space=pltpu.VMEM)
    return pl.pallas_call(
        near_kernel,
        in_specs=[smem, smem, pl.BlockSpec(memory_space=pl.ANY), vmem],
        out_specs=vmem,
        out_shape=jax.ShapeDtypeStruct((count, rank, width), jnp.bfloat16),
        scratch_shapes=[
            pltpu.VMEM((count,) + table.shape[1:], table.dtype),
            pltpu.SemaphoreType.DMA((count,)),
        ],
        compiler_params=params(),
        cost_estimate=cost(2 * 10**8, 4 * 10**6),
        name="near",
    )(row_leaf, rank_slabs, table, factors)


def far_kernel(groups, code, slabs, near, table, *rest):
    fetched, (factors, out, held, sem, tally) = rest[: groups - 1], rest[groups - 1 :]
    count, width, points = factors.shape
    leaves = table.shape[0]
    me = lax.axis_index("clus")
    for g in range(groups):
        tally[g] = 0

    def begin(b, carry):
        group, leaf = code[b] // leaves, code[b] % leaves
        position = tally[group]
        tally[group] = position + 1

        @pl.when(group == me)
        def _():
            pltpu.make_async_copy(table.at[leaf], held.at[b], sem.at[b]).start()

        for d in range(1, groups):

            @pl.when(group == partner(me, d, groups))
            def _():
                pltpu.make_async_copy(fetched[d - 1].at[position], held.at[b], sem.at[b]).start()

        return carry

    lax.fori_loop(0, count, begin, 0)
    column = lax.broadcasted_iota(jnp.int32, (near.shape[1], width), 1)
    for b in range(count):
        pltpu.make_async_copy(table.at[0], held.at[b], sem.at[b]).wait()
        value = dot(held[b], factors[b], NT)
        value = jnp.where(column < slabs[b] * SLAB, value, 0.0).astype(jnp.bfloat16)
        out[b] = dot(near[b], value, NT)


def far_stage(code, rank_slabs, near, table, fetched, factors):
    count, width, points = factors.shape
    rank = table.shape[1]
    groups = len(fetched) + 1
    smem = pl.BlockSpec(memory_space=pltpu.SMEM)
    vmem = pl.BlockSpec(memory_space=pltpu.VMEM)
    anywhere = pl.BlockSpec(memory_space=pl.ANY)
    return pl.pallas_call(
        functools.partial(far_kernel, groups),
        in_specs=[smem, smem, vmem] + [anywhere] * groups + [vmem],
        out_specs=vmem,
        out_shape=jax.ShapeDtypeStruct((count, rank, rank), jnp.float32),
        scratch_shapes=[
            pltpu.VMEM((count,) + table.shape[1:], table.dtype),
            pltpu.SemaphoreType.DMA((count,)),
            pltpu.SMEM((groups,), jnp.int32),
        ],
        compiler_params=params(),
        cost_estimate=cost(3 * 10**8, 6 * 10**6),
        name="far",
    )(code, rank_slabs, near, table, *fetched, factors)


def shift(value, axis, d):
    size = lax.axis_size(axis)
    pairs = [(partner_of(target, d, size), target) for target in range(size)]
    return lax.ppermute(value, axis, pairs)


def partner_of(index, d, size):
    if size & (size - 1) == 0:
        return index ^ d
    return (index + d) % size


def per_device(
    leaf_basis, transfer, block_rows, block_cols, rank_slabs, row_leaf, col_group, col_leaf
):
    groups = lax.axis_size("clus")
    block_count = block_rows.shape[0]
    capacity = max(2, 2 * block_count // groups)
    leaves = leaf_basis.shape[0] * lax.axis_size("blk")
    code = col_group[:, 0] * leaves + col_leaf
    asked = [shift(code, "clus", d) for d in range(1, groups)]
    far_basis = shift(leaf_basis, "blk", 1)
    far_transfer = shift(transfer, "blk", 1)
    basis_rows, leaf_work = leaf_stage(leaf_basis)
    table = lax.all_gather(basis_rows, "blk", axis=0, tiled=True)
    transfer_new = parent_stage(leaf_basis, transfer, far_basis, far_transfer, leaf_work)
    served = serve(asked, table, capacity)
    fetched = [shift(value, "clus", d) for d, value in zip(range(1, groups), served)]
    near = near_stage(row_leaf, rank_slabs, table, jnp.swapaxes(block_rows, 1, 2))
    coupling = far_stage(code, rank_slabs, near, table, fetched, jnp.swapaxes(block_cols, 1, 2))
    return (coupling, transfer_new)


def solution(mesh):
    placed = (
        P(("clus", "blk"), None, None),
        P(("clus", "blk"), None, None),
        P(("clus", "blk"), None, None),
        P(("clus", "blk"), None, None),
        P(("clus", "blk")),
        P(("clus", "blk")),
        P(("clus", "blk"), None),
        P(("clus", "blk")),
    )
    return jax.shard_map(
        per_device,
        mesh=mesh,
        in_specs=placed,
        out_specs=(P(("clus", "blk"), None, None), P(("clus", "blk"), None, None)),
        check_vma=False,
    )
```

```python
import functools

import jax
import jax.numpy as jnp
from jax import lax
from jax.experimental import pallas as pl
from jax.experimental.pallas import tpu as pltpu
from jax.sharding import PartitionSpec as P

SLAB = 64
PANEL = 8
STRIP = 32
CHUNKS = 2
VMEM_LIMIT = 40 * 1024 * 1024

NN = (((1,), (0,)), ((), ()))
NT = (((1,), (1,)), ((), ()))
TN = (((0,), (0,)), ((), ()))


def params():
    return pltpu.CompilerParams(vmem_limit_bytes=VMEM_LIMIT)


def cost(flops, moved):
    return pl.CostEstimate(flops=flops, bytes_accessed=moved, transcendentals=0)


def dot(left, right, dims):
    return lax.dot_general(left, right, dims, preferred_element_type=jnp.float32)


def split(value):
    high = value.astype(jnp.bfloat16)
    low = (value - high.astype(jnp.float32)).astype(jnp.bfloat16)
    return high, low


def dot_split(left, right, dims):
    (lh, ll), (rh, rl) = left, right
    return dot(lh, rh, dims) + (dot(lh, rl, dims) + dot(ll, rh, dims))


def lower_part(value):
    rows = lax.broadcasted_iota(jnp.int32, value.shape, 0)
    cols = lax.broadcasted_iota(jnp.int32, value.shape, 1)
    return jnp.where(cols <= rows, value, 0.0)


def factor(work, batch, size):
    lane = lax.broadcasted_iota(jnp.int32, (batch, size), 1)

    def spread(row, column):
        return jnp.broadcast_to(row[:, column : column + 1], (batch, size))

    for top in range(0, size, STRIP):
        rows = [work[pl.ds(top + i, batch, stride=size), :] for i in range(STRIP)]
        for q in range(0, STRIP, PANEL):
            first = top + q
            inside = (lane >= first) & (lane < first + PANEL)
            diag = {
                (i, j): spread(rows[q + i], first + j) for i in range(PANEL) for j in range(i, PANEL)
            }
            scale, upper = [], {}
            for k in range(PANEL):
                inv = lax.rsqrt(diag[k, k])
                scale.append(inv)
                for j in range(k + 1, PANEL):
                    upper[k, j] = diag[k, j] * inv
                for i in range(k + 1, PANEL):
                    for j in range(i, PANEL):
                        diag[i, j] = diag[i, j] - upper[k, i] * upper[k, j]
            done = []
            for k in range(PANEL):
                row = jnp.where(inside, jnp.where(lane == first + k, 1.0, 0.0), rows[q + k])
                for m in range(k):
                    row = row - upper[m, k] * done[m]
                done.append(row * scale[k])
            rows[q : q + PANEL] = done
            for i in range(q + PANEL, STRIP):
                row = jnp.where(inside, 0.0, rows[i])
                for k in range(PANEL):
                    row = row - spread(done[k], top + i) * done[k]
                rows[i] = row
        for i in range(STRIP):
            work[pl.ds(top + i, batch, stride=size), :] = rows[i]
        below = top + STRIP
        if below < size:
            for b in range(batch):
                strip = work[b * size + top : b * size + below, :]
                row = lax.broadcasted_iota(jnp.int32, strip.shape, 0) + top
                column = lax.broadcasted_iota(jnp.int32, strip.shape, 1)
                keep = (column <= row) | (column >= below)
                high, low = split(strip)
                left = jnp.concatenate([high, high, low], axis=0)
                high, low = split(jnp.where(keep, strip, 0.0))
                right = jnp.concatenate([high, low, high], axis=0)
                rest = work[b * size + below : (b + 1) * size, :]
                column = lax.broadcasted_iota(jnp.int32, rest.shape, 1)
                rest = jnp.where((column >= top) & (column < below), 0.0, rest)
                work[b * size + below : (b + 1) * size, :] = rest - dot(left, right, TN)[below:]


def leaf_kernel(basis, *outs):
    pieces, work = outs[:-1], outs[-1]
    count, points, rank = basis.shape
    chunk = points // len(pieces)
    for b in range(count):
        leaf = basis[b]
        work[b * rank : (b + 1) * rank, :] = dot(leaf, leaf, TN)
    factor(work, count, rank)
    for b in range(count):
        high, low = split(lower_part(work[b * rank : (b + 1) * rank, :]))
        for c, piece in enumerate(pieces):
            leaf = basis[b, c * chunk : (c + 1) * chunk, :]
            piece[b] = (dot(leaf, high, NT) + dot(leaf, low, NT)).astype(piece.dtype)


def parent_top_kernel(own_basis, own_transfer, far_basis, far_transfer, weighted, top, cross, corner):
    count, points, rank = own_basis.shape
    half = own_transfer.shape[2] // 2
    for j in range(count):
        other = (j + count // 2) % count
        total = None
        for basis, transfer, c in ((own_basis, own_transfer, j), (far_basis, far_transfer, other)):
            leaf = basis[c]
            gram = split(dot(leaf, leaf, TN))
            value = transfer[c]
            moved = dot_split(gram, split(value), NN)
            if basis is own_basis:
                weighted[c] = moved
            left, right = split(value[:, :half]), split(value[:, half:])
            moved_left, moved_right = split(moved[:, :half]), split(moved[:, half:])
            parts = (
                dot_split(left, moved_left, TN),
                dot_split(right, moved_left, TN),
                dot_split(right, moved_right, TN),
            )
            total = parts if total is None else tuple(a + b for a, b in zip(total, parts))
        top[j * half : (j + 1) * half, :] = total[0]
        cross[j] = total[1]
        corner[j] = total[2]
    factor(top, count, half)


def parent_low_kernel(leaf_work, weighted, top, cross, corner, out, work, coupled):
    count, rank, columns = weighted.shape
    half = columns // 2
    for j in range(count):
        inverse = split(lower_part(top[j * half : (j + 1) * half, :]))
        lower = dot_split(split(cross[j]), inverse, NT)
        coupled[j] = lower
        lower = split(lower)
        work[j * half : (j + 1) * half, :] = corner[j] - dot_split(lower, lower, NT)
    factor(work, count, half)
    for j in range(count):
        leaf_inverse = split(lower_part(leaf_work[j * rank : (j + 1) * rank, :]))
        stacked = dot_split(leaf_inverse, split(weighted[j]), NN)
        inverse = split(lower_part(top[j * half : (j + 1) * half, :]))
        first = dot_split(split(stacked[:, :half]), inverse, NT)
        rest = stacked[:, half:] - dot_split(split(first), split(coupled[j]), NT)
        inverse = split(lower_part(work[j * half : (j + 1) * half, :]))
        out[j, :, :half] = first
        out[j, :, half:] = dot_split(split(rest), inverse, NT)


def leaf_stage(leaf_basis):
    count, points, rank = leaf_basis.shape
    piece = jax.ShapeDtypeStruct((count, points // CHUNKS, rank), jnp.bfloat16)
    return pl.pallas_call(
        leaf_kernel,
        out_shape=[piece] * CHUNKS + [jax.ShapeDtypeStruct((count * rank, rank), jnp.float32)],
        compiler_params=params(),
        cost_estimate=cost(10**9, 25 * 10**6),
        name="leaf_factor",
    )(leaf_basis)


def parent_top(leaf_basis, transfer, far_basis, far_transfer):
    count, points, rank = leaf_basis.shape
    half = transfer.shape[2] // 2
    square = jax.ShapeDtypeStruct((count, half, half), jnp.float32)
    return pl.pallas_call(
        parent_top_kernel,
        out_shape=(
            jax.ShapeDtypeStruct(transfer.shape, jnp.float32),
            jax.ShapeDtypeStruct((count * half, half), jnp.float32),
            square,
            square,
        ),
        compiler_params=params(),
        cost_estimate=cost(10**9, 50 * 10**6),
        name="parent_top",
    )(leaf_basis, transfer, far_basis, far_transfer)


def parent_low(transfer, leaf_work, halves):
    count, rank, columns = transfer.shape
    half = columns // 2
    return pl.pallas_call(
        parent_low_kernel,
        out_shape=jax.ShapeDtypeStruct(transfer.shape, jnp.float32),
        scratch_shapes=[
            pltpu.VMEM((count * half, half), jnp.float32),
            pltpu.VMEM((count, half, half), jnp.float32),
        ],
        compiler_params=params(),
        cost_estimate=cost(10**9, 40 * 10**6),
        name="parent_low",
    )(leaf_work, *halves)


def shift(value, axis, d):
    pairs = [(index ^ d, index) for index in range(lax.axis_size(axis))]
    return lax.ppermute(value, axis, pairs)


def exchange(value):
    size = lax.axis_size("blk")
    held = {0: value}
    for d in range(2, size, 2):
        held[d] = shift(value, "blk", d)
    for d in range(0, size, 2):
        held[d + 1] = shift(held[d], "blk", 1)
    return [held[d] for d in range(size)]


def pick(table, leaf, store):
    count = table[0].shape[0]
    place = lax.div(leaf, count) ^ lax.axis_index("blk")
    for d in range(len(table)):

        @pl.when(place == d)
        def _():
            store(table[d][lax.rem(leaf, count)])


def serve_kernel(groups, size, *refs):
    asked, table, outs = refs[: groups - 1], refs[groups - 1 : groups - 1 + size], refs[1 - groups :]
    me = lax.axis_index("clus")
    leaves = size * table[0].shape[0]
    for d in range(1, groups):

        def place(b, position, d=d):
            code = asked[d - 1][b]
            mine = lax.div(code, leaves) == me

            @pl.when(mine)
            def _():
                def store(value):
                    outs[d - 1][position] = value

                pick(table, lax.rem(code, leaves), store)

            return position + mine.astype(jnp.int32)

        lax.fori_loop(0, asked[0].shape[0], place, jnp.int32(0))


def serve(asked, table, capacity, after):
    groups, size = len(asked) + 1, len(table)
    smem, vmem = pl.BlockSpec(memory_space=pltpu.SMEM), pl.BlockSpec(memory_space=pltpu.VMEM)
    shape = (capacity,) + table[0].shape[1:]
    return pl.pallas_call(
        functools.partial(serve_kernel, groups, size),
        in_specs=[smem] * (groups - 1) + [vmem] * size + [pl.BlockSpec(memory_space=pl.ANY)],
        out_specs=[vmem] * (groups - 1),
        out_shape=[jax.ShapeDtypeStruct(shape, table[0].dtype)] * (groups - 1),
        compiler_params=params(),
        cost_estimate=cost(0, 4 * 10**6),
        name="serve",
    )(*asked, *table, after)


def near_kernel(size, leaf, slabs, *refs):
    table, (factors, out, held) = refs[:-3], refs[-3:]
    count, width, points = factors.shape
    chunk = table[0].shape[1]

    def gather(b, carry):
        for c in range(len(table) // size):

            def store(value, c=c):
                held[b, c * chunk : (c + 1) * chunk, :] = value

            pick(table[c * size : (c + 1) * size], leaf[b], store)
        return carry

    lax.fori_loop(0, count, gather, 0)
    row = lax.broadcasted_iota(jnp.int32, (width, out.shape[1]), 0)
    for b in range(count):
        value = dot(factors[b], held[b], NN)
        value = jnp.where(row < slabs[b] * SLAB, value, 0.0)
        out[b] = value.T.astype(out.dtype)


def near_stage(row_leaf, rank_slabs, tables, factors):
    count, width, points = factors.shape
    size, rank = len(tables[0]), tables[0][0].shape[2]
    smem, vmem = pl.BlockSpec(memory_space=pltpu.SMEM), pl.BlockSpec(memory_space=pltpu.VMEM)
    flat = [piece for table in tables for piece in table]
    return pl.pallas_call(
        functools.partial(near_kernel, size),
        in_specs=[smem, smem] + [vmem] * len(flat) + [vmem],
        out_specs=vmem,
        out_shape=jax.ShapeDtypeStruct((count, rank, width), jnp.bfloat16),
        scratch_shapes=[pltpu.VMEM((count, points, rank), flat[0].dtype)],
        compiler_params=params(),
        cost_estimate=cost(2 * 10**8, 2 * 10**7),
        name="near",
    )(row_leaf, rank_slabs, *flat, factors)


def far_kernel(groups, size, chunks, code, slabs, near, *refs):
    table, refs = refs[: chunks * size], refs[chunks * size :]
    fetched, (factors, out, held, tally) = refs[: chunks * (groups - 1)], refs[chunks * (groups - 1) :]
    count, width, points = factors.shape
    leaves = size * table[0].shape[0]
    chunk = table[0].shape[1]
    me = lax.axis_index("clus")
    for g in range(groups):
        tally[g] = 0

    def gather(b, carry):
        group, leaf = lax.div(code[b], leaves), lax.rem(code[b], leaves)
        position = tally[group]
        tally[group] = position + 1
        away = group ^ me

        @pl.when(away == 0)
        def _():
            for c in range(chunks):

                def store(value, c=c):
                    held[b, c * chunk : (c + 1) * chunk, :] = value

                pick(table[c * size : (c + 1) * size], leaf, store)

        for d in range(1, groups):

            @pl.when(away == d)
            def _(d=d):
                for c in range(chunks):
                    piece = fetched[c * (groups - 1) + d - 1]
                    held[b, c * chunk : (c + 1) * chunk, :] = piece[position]

        return carry

    lax.fori_loop(0, count, gather, 0)
    row = lax.broadcasted_iota(jnp.int32, (width, near.shape[1]), 0)
    for b in range(count):
        value = dot(factors[b], held[b], NN)
        value = jnp.where(row < slabs[b] * SLAB, value, 0.0).astype(near.dtype)
        out[b] = dot(near[b], value, NN)


def far_stage(code, rank_slabs, near, tables, fetched, factors):
    count, width, points = factors.shape
    size, rank = len(tables[0]), tables[0][0].shape[2]
    groups = len(fetched[0]) + 1
    smem, vmem = pl.BlockSpec(memory_space=pltpu.SMEM), pl.BlockSpec(memory_space=pltpu.VMEM)
    flat = [piece for table in tables for piece in table] + [piece for part in fetched for piece in part]
    return pl.pallas_call(
        functools.partial(far_kernel, groups, size, len(tables)),
        in_specs=[smem, smem, vmem] + [vmem] * len(flat) + [vmem],
        out_specs=vmem,
        out_shape=jax.ShapeDtypeStruct((count, rank, rank), jnp.float32),
        scratch_shapes=[
            pltpu.VMEM((count, points, rank), flat[0].dtype),
            pltpu.SMEM((groups,), jnp.int32),
        ],
        compiler_params=params(),
        cost_estimate=cost(3 * 10**8, 2 * 10**7),
        name="far",
    )(code, rank_slabs, near, *flat, factors)


def per_device(
    leaf_basis, transfer, block_rows, block_cols, rank_slabs, row_leaf, col_group, col_leaf
):
    groups = lax.axis_size("clus")
    block_count = block_rows.shape[0]
    capacity = max(2, 2 * block_count // groups)
    leaves = leaf_basis.shape[0] * lax.axis_size("blk")
    code = col_group[:, 0] * leaves + col_leaf
    asked = [shift(code, "clus", d) for d in range(1, groups)]
    far_basis = shift(leaf_basis, "blk", 1)
    far_transfer = shift(transfer, "blk", 1)
    pieces = leaf_stage(leaf_basis)
    leaf_work = pieces[-1]
    tables = [exchange(piece) for piece in pieces[:-1]]
    halves = parent_top(leaf_basis, transfer, far_basis, far_transfer)
    transfer_new = parent_low(transfer, leaf_work, halves)
    fetched = []
    for table, after in zip(tables, (halves[-1], transfer_new)):
        served = serve(asked, table, capacity, after)
        fetched.append([shift(value, "clus", d + 1) for d, value in enumerate(served)])
    near = near_stage(row_leaf, rank_slabs, tables, jnp.swapaxes(block_rows, 1, 2))
    coupling = far_stage(code, rank_slabs, near, tables, fetched, jnp.swapaxes(block_cols, 1, 2))
    return (coupling, transfer_new)


def solution(mesh):
    placed = (
        P(("clus", "blk"), None, None),
        P(("clus", "blk"), None, None),
        P(("clus", "blk"), None, None),
        P(("clus", "blk"), None, None),
        P(("clus", "blk")),
        P(("clus", "blk")),
        P(("clus", "blk"), None),
        P(("clus", "blk")),
    )
    return jax.shard_map(
        per_device,
        mesh=mesh,
        in_specs=placed,
        out_specs=(P(("clus", "blk"), None, None), P(("clus", "blk"), None, None)),
        check_vma=False,
    )
```

```python
import functools

import jax
import jax.numpy as jnp
from jax import lax
from jax.experimental import pallas as pl
from jax.experimental.pallas import tpu as pltpu
from jax.sharding import PartitionSpec as P

SLAB = 64
PANEL = 8
STRIP = 32
CHUNKS = 2
VMEM_LIMIT = 40 * 1024 * 1024

NN = (((1,), (0,)), ((), ()))
NT = (((1,), (1,)), ((), ()))
TN = (((0,), (0,)), ((), ()))


def params():
    return pltpu.CompilerParams(vmem_limit_bytes=VMEM_LIMIT)


def cost(flops, moved):
    return pl.CostEstimate(flops=flops, bytes_accessed=moved, transcendentals=0)


def dot(left, right, dims):
    return lax.dot_general(left, right, dims, preferred_element_type=jnp.float32)


def split(value):
    high = value.astype(jnp.bfloat16)
    low = (value - high.astype(jnp.float32)).astype(jnp.bfloat16)
    return high, low


def dot_split(left, right, dims):
    (lh, ll), (rh, rl) = left, right
    return dot(lh, rh, dims) + (dot(lh, rl, dims) + dot(ll, rh, dims))


def lower_part(value):
    rows = lax.broadcasted_iota(jnp.int32, value.shape, 0)
    cols = lax.broadcasted_iota(jnp.int32, value.shape, 1)
    return jnp.where(cols <= rows, value, 0.0)


def factor(work, batch, size):
    lane = lax.broadcasted_iota(jnp.int32, (batch, size), 1)

    def spread(row, column):
        return jnp.broadcast_to(row[:, column : column + 1], (batch, size))

    for top in range(0, size, STRIP):
        rows = [work[pl.ds(top + i, batch, stride=size), :] for i in range(STRIP)]
        for q in range(0, STRIP, PANEL):
            first = top + q
            inside = (lane >= first) & (lane < first + PANEL)
            diag = {
                (i, j): spread(rows[q + i], first + j) for i in range(PANEL) for j in range(i, PANEL)
            }
            scale, upper = [], {}
            for k in range(PANEL):
                inv = lax.rsqrt(diag[k, k])
                scale.append(inv)
                for j in range(k + 1, PANEL):
                    upper[k, j] = diag[k, j] * inv
                for i in range(k + 1, PANEL):
                    for j in range(i, PANEL):
                        diag[i, j] = diag[i, j] - upper[k, i] * upper[k, j]
            done = []
            for k in range(PANEL):
                row = jnp.where(inside, jnp.where(lane == first + k, 1.0, 0.0), rows[q + k])
                for m in range(k):
                    row = row - upper[m, k] * done[m]
                done.append(row * scale[k])
            rows[q : q + PANEL] = done
            for i in range(q + PANEL, STRIP):
                row = jnp.where(inside, 0.0, rows[i])
                for k in range(PANEL):
                    row = row - spread(done[k], top + i) * done[k]
                rows[i] = row
        for i in range(STRIP):
            work[pl.ds(top + i, batch, stride=size), :] = rows[i]
        below = top + STRIP
        if below < size:
            for b in range(batch):
                strip = work[b * size + top : b * size + below, :]
                row = lax.broadcasted_iota(jnp.int32, strip.shape, 0) + top
                column = lax.broadcasted_iota(jnp.int32, strip.shape, 1)
                keep = (column <= row) | (column >= below)
                high, low = split(strip)
                left = jnp.concatenate([high, high, low], axis=0)
                high, low = split(jnp.where(keep, strip, 0.0))
                right = jnp.concatenate([high, low, high], axis=0)
                rest = work[b * size + below : (b + 1) * size, :]
                column = lax.broadcasted_iota(jnp.int32, rest.shape, 1)
                rest = jnp.where((column >= top) & (column < below), 0.0, rest)
                work[b * size + below : (b + 1) * size, :] = rest - dot(left, right, TN)[below:]


def leaf_kernel(basis, *outs):
    pieces, work = outs[:-1], outs[-1]
    count, points, rank = basis.shape
    chunk = points // len(pieces)
    for b in range(count):
        leaf = basis[b]
        work[b * rank : (b + 1) * rank, :] = dot(leaf, leaf, TN)
    factor(work, count, rank)
    for b in range(count):
        high, low = split(lower_part(work[b * rank : (b + 1) * rank, :]))
        for c, piece in enumerate(pieces):
            leaf = basis[b, c * chunk : (c + 1) * chunk, :]
            piece[b] = (dot(leaf, high, NT) + dot(leaf, low, NT)).astype(piece.dtype)


def parent_top_kernel(own_basis, own_transfer, far_basis, far_transfer, weighted, top, cross, corner):
    count, points, rank = own_basis.shape
    half = own_transfer.shape[2] // 2
    for j in range(count):
        other = (j + count // 2) % count
        total = None
        for basis, transfer, c in ((own_basis, own_transfer, j), (far_basis, far_transfer, other)):
            leaf = basis[c]
            gram = split(dot(leaf, leaf, TN))
            value = transfer[c]
            moved = dot_split(gram, split(value), NN)
            if basis is own_basis:
                weighted[c] = moved
            left, right = split(value[:, :half]), split(value[:, half:])
            moved_left, moved_right = split(moved[:, :half]), split(moved[:, half:])
            parts = (
                dot_split(left, moved_left, TN),
                dot_split(right, moved_left, TN),
                dot_split(right, moved_right, TN),
            )
            total = parts if total is None else tuple(a + b for a, b in zip(total, parts))
        top[j * half : (j + 1) * half, :] = total[0]
        cross[j] = total[1]
        corner[j] = total[2]
    factor(top, count, half)


def parent_low_kernel(leaf_work, weighted, top, cross, corner, out, work, coupled):
    count, rank, columns = weighted.shape
    half = columns // 2
    for j in range(count):
        inverse = split(lower_part(top[j * half : (j + 1) * half, :]))
        lower = dot_split(split(cross[j]), inverse, NT)
        coupled[j] = lower
        lower = split(lower)
        work[j * half : (j + 1) * half, :] = corner[j] - dot_split(lower, lower, NT)
    factor(work, count, half)
    for j in range(count):
        leaf_inverse = split(lower_part(leaf_work[j * rank : (j + 1) * rank, :]))
        stacked = dot_split(leaf_inverse, split(weighted[j]), NN)
        inverse = split(lower_part(top[j * half : (j + 1) * half, :]))
        first = dot_split(split(stacked[:, :half]), inverse, NT)
        rest = stacked[:, half:] - dot_split(split(first), split(coupled[j]), NT)
        inverse = split(lower_part(work[j * half : (j + 1) * half, :]))
        out[j, :, :half] = first
        out[j, :, half:] = dot_split(split(rest), inverse, NT)


def leaf_stage(leaf_basis):
    count, points, rank = leaf_basis.shape
    piece = jax.ShapeDtypeStruct((count, points // CHUNKS, rank), jnp.bfloat16)
    return pl.pallas_call(
        leaf_kernel,
        out_shape=[piece] * CHUNKS + [jax.ShapeDtypeStruct((count * rank, rank), jnp.float32)],
        compiler_params=params(),
        cost_estimate=cost(10**9, 25 * 10**6),
        name="leaf_factor",
    )(leaf_basis)


def parent_top(leaf_basis, transfer, far_basis, far_transfer):
    count, points, rank = leaf_basis.shape
    half = transfer.shape[2] // 2
    square = jax.ShapeDtypeStruct((count, half, half), jnp.float32)
    return pl.pallas_call(
        parent_top_kernel,
        out_shape=(
            jax.ShapeDtypeStruct(transfer.shape, jnp.float32),
            jax.ShapeDtypeStruct((count * half, half), jnp.float32),
            square,
            square,
        ),
        compiler_params=params(),
        cost_estimate=cost(10**9, 50 * 10**6),
        name="parent_top",
    )(leaf_basis, transfer, far_basis, far_transfer)


def parent_low(transfer, leaf_work, halves):
    count, rank, columns = transfer.shape
    half = columns // 2
    return pl.pallas_call(
        parent_low_kernel,
        out_shape=jax.ShapeDtypeStruct(transfer.shape, jnp.float32),
        scratch_shapes=[
            pltpu.VMEM((count * half, half), jnp.float32),
            pltpu.VMEM((count, half, half), jnp.float32),
        ],
        compiler_params=params(),
        cost_estimate=cost(10**9, 40 * 10**6),
        name="parent_low",
    )(leaf_work, *halves)


def shift(value, axis, d):
    pairs = [(index ^ d, index) for index in range(lax.axis_size(axis))]
    return lax.ppermute(value, axis, pairs)


def gather_same_core(value):
    size = lax.axis_size("blk")
    same = [[index for index in range(size) if index % 2 == core] for core in range(2)]
    return lax.all_gather(value, "blk", axis=0, tiled=True, axis_index_groups=same)


def pick(table, leaf, count, store):
    owner = lax.div(leaf, count)
    core = (owner ^ lax.axis_index("blk")) & 1
    place = lax.div(owner, 2) * count + lax.rem(leaf, count)
    for c in range(2):

        @pl.when(core == c)
        def _():
            store(table[c][place])


def serve_kernel(groups, count, *refs):
    asked, table, outs = refs[: groups - 1], refs[groups - 1 : groups + 1], refs[1 - groups :]
    me = lax.axis_index("clus")
    leaves = 2 * table[0].shape[0]
    for d in range(1, groups):

        def place(b, position, d=d):
            code = asked[d - 1][b]
            mine = lax.div(code, leaves) == me

            @pl.when(mine)
            def _():
                def store(value):
                    outs[d - 1][position] = value

                pick(table, lax.rem(code, leaves), count, store)

            return position + mine.astype(jnp.int32)

        lax.fori_loop(0, asked[0].shape[0], place, jnp.int32(0))


def serve(asked, table, capacity, count):
    groups = len(asked) + 1
    smem, vmem = pl.BlockSpec(memory_space=pltpu.SMEM), pl.BlockSpec(memory_space=pltpu.VMEM)
    shape = (capacity,) + table[0].shape[1:]
    return pl.pallas_call(
        functools.partial(serve_kernel, groups, count),
        in_specs=[smem] * (groups - 1) + [vmem] * 2,
        out_specs=[vmem] * (groups - 1),
        out_shape=[jax.ShapeDtypeStruct(shape, table[0].dtype)] * (groups - 1),
        compiler_params=params(),
        cost_estimate=cost(0, 4 * 10**6),
        name="serve",
    )(*asked, *table)


def near_kernel(leaf_count, leaf, slabs, *refs):
    table, (factors, out, held) = refs[:-3], refs[-3:]
    count, width, points = factors.shape
    chunk = table[0].shape[1]

    def gather(b, carry):
        for c in range(len(table) // 2):

            def store(value, c=c):
                held[b, c * chunk : (c + 1) * chunk, :] = value

            pick(table[2 * c : 2 * c + 2], leaf[b], leaf_count, store)
        return carry

    lax.fori_loop(0, count, gather, 0)
    row = lax.broadcasted_iota(jnp.int32, (width, out.shape[1]), 0)
    for b in range(count):
        value = dot(factors[b], held[b], NN)
        value = jnp.where(row < slabs[b] * SLAB, value, 0.0)
        out[b] = value.T.astype(out.dtype)


def near_stage(row_leaf, rank_slabs, tables, leaf_count, factors):
    count, width, points = factors.shape
    rank = tables[0][0].shape[2]
    smem, vmem = pl.BlockSpec(memory_space=pltpu.SMEM), pl.BlockSpec(memory_space=pltpu.VMEM)
    flat = [piece for table in tables for piece in table]
    return pl.pallas_call(
        functools.partial(near_kernel, leaf_count),
        in_specs=[smem, smem] + [vmem] * len(flat) + [vmem],
        out_specs=vmem,
        out_shape=jax.ShapeDtypeStruct((count, rank, width), jnp.bfloat16),
        scratch_shapes=[pltpu.VMEM((count, points, rank), flat[0].dtype)],
        compiler_params=params(),
        cost_estimate=cost(2 * 10**8, 2 * 10**7),
        name="near",
    )(row_leaf, rank_slabs, *flat, factors)


def far_kernel(groups, leaf_count, chunks, code, slabs, near, *refs):
    table, refs = refs[: chunks * 2], refs[chunks * 2 :]
    fetched, (factors, out, held, tally) = refs[: chunks * (groups - 1)], refs[chunks * (groups - 1) :]
    count, width, points = factors.shape
    leaves = 2 * table[0].shape[0]
    chunk = table[0].shape[1]
    me = lax.axis_index("clus")
    for g in range(groups):
        tally[g] = 0

    def gather(b, carry):
        group, leaf = lax.div(code[b], leaves), lax.rem(code[b], leaves)
        position = tally[group]
        tally[group] = position + 1
        away = group ^ me

        @pl.when(away == 0)
        def _():
            for c in range(chunks):

                def store(value, c=c):
                    held[b, c * chunk : (c + 1) * chunk, :] = value

                pick(table[2 * c : 2 * c + 2], leaf, leaf_count, store)

        for d in range(1, groups):

            @pl.when(away == d)
            def _(d=d):
                for c in range(chunks):
                    piece = fetched[c * (groups - 1) + d - 1]
                    held[b, c * chunk : (c + 1) * chunk, :] = piece[position]

        return carry

    lax.fori_loop(0, count, gather, 0)
    row = lax.broadcasted_iota(jnp.int32, (width, near.shape[1]), 0)
    for b in range(count):
        value = dot(factors[b], held[b], NN)
        value = jnp.where(row < slabs[b] * SLAB, value, 0.0).astype(near.dtype)
        out[b] = dot(near[b], value, NN)


def far_stage(code, rank_slabs, near, tables, leaf_count, fetched, factors):
    count, width, points = factors.shape
    rank = tables[0][0].shape[2]
    groups = len(fetched[0]) + 1
    smem, vmem = pl.BlockSpec(memory_space=pltpu.SMEM), pl.BlockSpec(memory_space=pltpu.VMEM)
    flat = [piece for table in tables for piece in table] + [piece for part in fetched for piece in part]
    return pl.pallas_call(
        functools.partial(far_kernel, groups, leaf_count, len(tables)),
        in_specs=[smem, smem, vmem] + [vmem] * len(flat) + [vmem],
        out_specs=vmem,
        out_shape=jax.ShapeDtypeStruct((count, rank, rank), jnp.float32),
        scratch_shapes=[
            pltpu.VMEM((count, points, rank), flat[0].dtype),
            pltpu.SMEM((groups,), jnp.int32),
        ],
        compiler_params=params(),
        cost_estimate=cost(3 * 10**8, 2 * 10**7),
        name="far",
    )(code, rank_slabs, near, *flat, factors)


def per_device(
    leaf_basis, transfer, block_rows, block_cols, rank_slabs, row_leaf, col_group, col_leaf
):
    groups = lax.axis_size("clus")
    block_count = block_rows.shape[0]
    capacity = max(2, 2 * block_count // groups)
    leaf_count = leaf_basis.shape[0]
    leaves = leaf_count * lax.axis_size("blk")
    code = col_group[:, 0] * leaves + col_leaf
    asked = [shift(code, "clus", d) for d in range(1, groups)]
    far_basis = shift(leaf_basis, "blk", 1)
    far_transfer = shift(transfer, "blk", 1)
    pieces = leaf_stage(leaf_basis)
    leaf_work = pieces[-1]
    gathered = [gather_same_core(piece) for piece in pieces[:-1]]
    halves = parent_top(leaf_basis, transfer, far_basis, far_transfer)
    gathered[0], asked, halves = lax.optimization_barrier((gathered[0], asked, halves))
    swapped = shift(gathered[0], "blk", 1)
    transfer_new = parent_low(transfer, leaf_work, halves)
    swapped, transfer_new = lax.optimization_barrier((swapped, transfer_new))
    tables, fetched = [], []
    for c in range(CHUNKS):
        if c > 0:
            gathered[c], fetched[c - 1] = lax.optimization_barrier((gathered[c], fetched[c - 1]))
            swapped = shift(gathered[c], "blk", 1)
        tables.append([gathered[c], swapped])
        served = serve(asked, tables[c], capacity, leaf_count)
        fetched.append([shift(value, "clus", d + 1) for d, value in enumerate(served)])
    near = near_stage(row_leaf, rank_slabs, tables, leaf_count, jnp.swapaxes(block_rows, 1, 2))
    coupling = far_stage(code, rank_slabs, near, tables, leaf_count, fetched, jnp.swapaxes(block_cols, 1, 2))
    return (coupling, transfer_new)


def solution(mesh):
    placed = (
        P(("clus", "blk"), None, None),
        P(("clus", "blk"), None, None),
        P(("clus", "blk"), None, None),
        P(("clus", "blk"), None, None),
        P(("clus", "blk")),
        P(("clus", "blk")),
        P(("clus", "blk"), None),
        P(("clus", "blk")),
    )
    return jax.shard_map(
        per_device,
        mesh=mesh,
        in_specs=placed,
        out_specs=(P(("clus", "blk"), None, None), P(("clus", "blk"), None, None)),
        check_vma=False,
    )
```

```python
import functools

import jax
import jax.numpy as jnp
from jax import lax
from jax.experimental import pallas as pl
from jax.experimental.pallas import tpu as pltpu
from jax.sharding import PartitionSpec as P

SLAB = 64
PANEL = 8
STRIP = 32
FIRST = 10
AHEAD = 4
VMEM_LIMIT = 40 * 1024 * 1024

NN = (((1,), (0,)), ((), ()))
NT = (((1,), (1,)), ((), ()))
TN = (((0,), (0,)), ((), ()))


def params():
    return pltpu.CompilerParams(vmem_limit_bytes=VMEM_LIMIT)


def cost(flops, moved):
    return pl.CostEstimate(flops=flops, bytes_accessed=moved, transcendentals=0)


def dot(left, right, dims):
    return lax.dot_general(left, right, dims, preferred_element_type=jnp.float32)


def split(value):
    high = value.astype(jnp.bfloat16)
    low = (value - high.astype(jnp.float32)).astype(jnp.bfloat16)
    return high, low


def dot_split(left, right, dims):
    (lh, ll), (rh, rl) = left, right
    return dot(lh, rh, dims) + (dot(lh, rl, dims) + dot(ll, rh, dims))


def lower_part(value):
    rows = lax.broadcasted_iota(jnp.int32, value.shape, 0)
    cols = lax.broadcasted_iota(jnp.int32, value.shape, 1)
    return jnp.where(cols <= rows, value, 0.0)


def factor(work, batch, size):
    lane = lax.broadcasted_iota(jnp.int32, (batch, size), 1)

    def spread(row, column):
        return jnp.broadcast_to(row[:, column : column + 1], (batch, size))

    for top in range(0, size, STRIP):
        rows = [work[pl.ds(top + i, batch, stride=size), :] for i in range(STRIP)]
        for q in range(0, STRIP, PANEL):
            first = top + q
            inside = (lane >= first) & (lane < first + PANEL)
            diag = {
                (i, j): spread(rows[q + i], first + j) for i in range(PANEL) for j in range(i, PANEL)
            }
            scale, upper = [], {}
            for k in range(PANEL):
                inv = lax.rsqrt(diag[k, k])
                scale.append(inv)
                for j in range(k + 1, PANEL):
                    upper[k, j] = diag[k, j] * inv
                for i in range(k + 1, PANEL):
                    for j in range(i, PANEL):
                        diag[i, j] = diag[i, j] - upper[k, i] * upper[k, j]
            done = []
            for k in range(PANEL):
                row = jnp.where(inside, jnp.where(lane == first + k, 1.0, 0.0), rows[q + k])
                for m in range(k):
                    row = row - upper[m, k] * done[m]
                done.append(row * scale[k])
            rows[q : q + PANEL] = done
            for i in range(q + PANEL, STRIP):
                row = jnp.where(inside, 0.0, rows[i])
                for k in range(PANEL):
                    row = row - spread(done[k], top + i) * done[k]
                rows[i] = row
        for i in range(STRIP):
            work[pl.ds(top + i, batch, stride=size), :] = rows[i]
        below = top + STRIP
        if below < size:
            for b in range(batch):
                strip = work[b * size + top : b * size + below, :]
                row = lax.broadcasted_iota(jnp.int32, strip.shape, 0) + top
                column = lax.broadcasted_iota(jnp.int32, strip.shape, 1)
                keep = (column <= row) | (column >= below)
                high, low = split(strip)
                left = jnp.concatenate([high, high, low], axis=0)
                high, low = split(jnp.where(keep, strip, 0.0))
                right = jnp.concatenate([high, low, high], axis=0)
                rest = work[b * size + below : (b + 1) * size, :]
                column = lax.broadcasted_iota(jnp.int32, rest.shape, 1)
                rest = jnp.where((column >= top) & (column < below), 0.0, rest)
                work[b * size + below : (b + 1) * size, :] = rest - dot(left, right, TN)[below:]


def leaf_kernel(basis, *outs):
    pieces, work = outs[:-1], outs[-1]
    count, points, rank = basis.shape
    spans = chunk_spans(pieces)
    for b in range(count):
        leaf = basis[b]
        work[b * rank : (b + 1) * rank, :] = dot(leaf, leaf, TN)
    factor(work, count, rank)
    for b in range(count):
        high, low = split(lower_part(work[b * rank : (b + 1) * rank, :]))
        for span, piece in zip(spans, pieces):
            leaf = basis[b, span, :]
            piece[b] = (dot(leaf, high, NT) + dot(leaf, low, NT)).astype(piece.dtype)


def parent_top_kernel(own_basis, own_transfer, far_basis, far_transfer, weighted, top, cross, corner):
    count, points, rank = own_basis.shape
    half = own_transfer.shape[2] // 2
    for j in range(count):
        other = (j + count // 2) % count
        total = None
        for basis, transfer, c in ((own_basis, own_transfer, j), (far_basis, far_transfer, other)):
            leaf = basis[c]
            gram = split(dot(leaf, leaf, TN))
            value = transfer[c]
            moved = dot_split(gram, split(value), NN)
            if basis is own_basis:
                weighted[c] = moved
            left, right = split(value[:, :half]), split(value[:, half:])
            moved_left, moved_right = split(moved[:, :half]), split(moved[:, half:])
            parts = (
                dot_split(left, moved_left, TN),
                dot_split(right, moved_left, TN),
                dot_split(right, moved_right, TN),
            )
            total = parts if total is None else tuple(a + b for a, b in zip(total, parts))
        top[j * half : (j + 1) * half, :] = total[0]
        cross[j] = total[1]
        corner[j] = total[2]
    factor(top, count, half)


def parent_low_kernel(leaf_work, weighted, top, cross, corner, out, work, coupled):
    count, rank, columns = weighted.shape
    half = columns // 2
    for j in range(count):
        inverse = split(lower_part(top[j * half : (j + 1) * half, :]))
        lower = dot_split(split(cross[j]), inverse, NT)
        coupled[j] = lower
        lower = split(lower)
        work[j * half : (j + 1) * half, :] = corner[j] - dot_split(lower, lower, NT)
    factor(work, count, half)
    for j in range(count):
        leaf_inverse = split(lower_part(leaf_work[j * rank : (j + 1) * rank, :]))
        stacked = dot_split(leaf_inverse, split(weighted[j]), NN)
        inverse = split(lower_part(top[j * half : (j + 1) * half, :]))
        first = dot_split(split(stacked[:, :half]), inverse, NT)
        rest = stacked[:, half:] - dot_split(split(first), split(coupled[j]), NT)
        inverse = split(lower_part(work[j * half : (j + 1) * half, :]))
        out[j, :, :half] = first
        out[j, :, half:] = dot_split(split(rest), inverse, NT)


def leaf_stage(leaf_basis):
    count, points, rank = leaf_basis.shape
    first = points * FIRST // 16
    pieces = [
        jax.ShapeDtypeStruct((count, part, rank), jnp.bfloat16) for part in (first, points - first)
    ]
    return pl.pallas_call(
        leaf_kernel,
        out_shape=pieces + [jax.ShapeDtypeStruct((count * rank, rank), jnp.float32)],
        compiler_params=params(),
        cost_estimate=cost(10**9, 25 * 10**6),
        name="leaf_factor",
    )(leaf_basis)


def parent_top(leaf_basis, transfer, far_basis, far_transfer):
    count, points, rank = leaf_basis.shape
    half = transfer.shape[2] // 2
    square = jax.ShapeDtypeStruct((count, half, half), jnp.float32)
    return pl.pallas_call(
        parent_top_kernel,
        out_shape=(
            jax.ShapeDtypeStruct(transfer.shape, jnp.float32),
            jax.ShapeDtypeStruct((count * half, half), jnp.float32),
            square,
            square,
        ),
        compiler_params=params(),
        cost_estimate=cost(10**9, 50 * 10**6),
        name="parent_top",
    )(leaf_basis, transfer, far_basis, far_transfer)


def parent_low(transfer, leaf_work, halves):
    count, rank, columns = transfer.shape
    half = columns // 2
    return pl.pallas_call(
        parent_low_kernel,
        out_shape=jax.ShapeDtypeStruct(transfer.shape, jnp.float32),
        scratch_shapes=[
            pltpu.VMEM((count * half, half), jnp.float32),
            pltpu.VMEM((count, half, half), jnp.float32),
        ],
        compiler_params=params(),
        cost_estimate=cost(10**9, 40 * 10**6),
        name="parent_low",
    )(leaf_work, *halves)


def shift(value, axis, d):
    pairs = [(index ^ d, index) for index in range(lax.axis_size(axis))]
    return lax.ppermute(value, axis, pairs)


def in_order(table):
    return [table[d] for d in range(len(table))]


def chunk_spans(pieces):
    spans, start = [], 0
    for piece in pieces:
        spans.append(slice(start, start + piece.shape[1]))
        start += piece.shape[1]
    return spans


def pick(table, leaf, store):
    count = table[0].shape[0]
    place = lax.div(leaf, count) ^ lax.axis_index("blk")
    for d in range(len(table)):

        @pl.when(place == d)
        def _():
            store(table[d][lax.rem(leaf, count)])


def serve_kernel(groups, size, *refs):
    asked, table, outs = refs[: groups - 1], refs[groups - 1 : groups - 1 + size], refs[1 - groups :]
    me = lax.axis_index("clus")
    leaves = size * table[0].shape[0]
    for d in range(1, groups):

        def place(b, position, d=d):
            code = asked[d - 1][b]
            mine = lax.div(code, leaves) == me

            @pl.when(mine)
            def _():
                def store(value):
                    outs[d - 1][position] = value

                pick(table, lax.rem(code, leaves), store)

            return position + mine.astype(jnp.int32)

        lax.fori_loop(0, asked[0].shape[0], place, jnp.int32(0))


def serve(asked, table, capacity):
    groups, size = len(asked) + 1, len(table)
    smem, vmem = pl.BlockSpec(memory_space=pltpu.SMEM), pl.BlockSpec(memory_space=pltpu.VMEM)
    shape = (capacity,) + table[0].shape[1:]
    return pl.pallas_call(
        functools.partial(serve_kernel, groups, size),
        in_specs=[smem] * (groups - 1) + [vmem] * size,
        out_specs=[vmem] * (groups - 1),
        out_shape=[jax.ShapeDtypeStruct(shape, table[0].dtype)] * (groups - 1),
        compiler_params=params(),
        cost_estimate=cost(0, 4 * 10**6),
        name="serve",
    )(*asked, *table)


def near_kernel(size, leaf, slabs, *refs):
    table, (factors, out, held) = refs[:-3], refs[-3:]
    count, width, points = factors.shape
    spans = chunk_spans(table[::size])

    def gather(b, carry):
        for c in range(len(spans)):

            def store(value, c=c):
                held[b, spans[c], :] = value

            pick(table[c * size : (c + 1) * size], leaf[b], store)
        return carry

    lax.fori_loop(0, count, gather, 0)
    row = lax.broadcasted_iota(jnp.int32, (width, out.shape[1]), 0)
    for b in range(count):
        value = dot(factors[b], held[b], NN)
        value = jnp.where(row < slabs[b] * SLAB, value, 0.0)
        out[b] = value.T.astype(out.dtype)


def near_stage(row_leaf, rank_slabs, tables, factors):
    count, width, points = factors.shape
    size, rank = len(tables[0]), tables[0][0].shape[2]
    smem, vmem = pl.BlockSpec(memory_space=pltpu.SMEM), pl.BlockSpec(memory_space=pltpu.VMEM)
    flat = [piece for table in tables for piece in table]
    return pl.pallas_call(
        functools.partial(near_kernel, size),
        in_specs=[smem, smem] + [vmem] * len(flat) + [vmem],
        out_specs=vmem,
        out_shape=jax.ShapeDtypeStruct((count, rank, width), jnp.bfloat16),
        scratch_shapes=[pltpu.VMEM((count, points, rank), flat[0].dtype)],
        compiler_params=params(),
        cost_estimate=cost(2 * 10**8, 2 * 10**7),
        name="near",
    )(row_leaf, rank_slabs, *flat, factors)


def far_kernel(groups, size, chunks, code, slabs, near, *refs):
    table, refs = refs[: chunks * size], refs[chunks * size :]
    fetched, (factors, out, held, tally) = refs[: chunks * (groups - 1)], refs[chunks * (groups - 1) :]
    count, width, points = factors.shape
    leaves = size * table[0].shape[0]
    spans = chunk_spans(table[::size])
    me = lax.axis_index("clus")
    for g in range(groups):
        tally[g] = 0

    def gather(b, carry):
        group, leaf = lax.div(code[b], leaves), lax.rem(code[b], leaves)
        position = tally[group]
        tally[group] = position + 1
        away = group ^ me

        @pl.when(away == 0)
        def _():
            for c in range(chunks):

                def store(value, c=c):
                    held[b, spans[c], :] = value

                pick(table[c * size : (c + 1) * size], leaf, store)

        for d in range(1, groups):

            @pl.when(away == d)
            def _(d=d):
                for c in range(chunks):
                    piece = fetched[c * (groups - 1) + d - 1]
                    held[b, spans[c], :] = piece[position]

        return carry

    lax.fori_loop(0, count, gather, 0)
    row = lax.broadcasted_iota(jnp.int32, (width, near.shape[1]), 0)
    for first in range(0, count, AHEAD):
        values = [dot(factors[b], held[b], NN) for b in range(first, first + AHEAD)]
        for b in range(first, first + AHEAD):
            value = jnp.where(row < slabs[b] * SLAB, values[b - first], 0.0).astype(near.dtype)
            out[b] = dot(near[b], value, NN)


def far_stage(code, rank_slabs, near, tables, fetched, factors):
    count, width, points = factors.shape
    size, rank = len(tables[0]), tables[0][0].shape[2]
    groups = len(fetched[0]) + 1
    smem, vmem = pl.BlockSpec(memory_space=pltpu.SMEM), pl.BlockSpec(memory_space=pltpu.VMEM)
    flat = [piece for table in tables for piece in table] + [piece for part in fetched for piece in part]
    return pl.pallas_call(
        functools.partial(far_kernel, groups, size, len(tables)),
        in_specs=[smem, smem, vmem] + [vmem] * len(flat) + [vmem],
        out_specs=vmem,
        out_shape=jax.ShapeDtypeStruct((count, rank, rank), jnp.float32),
        scratch_shapes=[
            pltpu.VMEM((count, points, rank), flat[0].dtype),
            pltpu.SMEM((groups,), jnp.int32),
        ],
        compiler_params=params(),
        cost_estimate=cost(3 * 10**8, 2 * 10**7),
        name="far",
    )(code, rank_slabs, near, *flat, factors)


def per_device(
    leaf_basis, transfer, block_rows, block_cols, rank_slabs, row_leaf, col_group, col_leaf
):
    groups = lax.axis_size("clus")
    block_count = block_rows.shape[0]
    capacity = max(2, 2 * block_count // groups)
    leaf_count = leaf_basis.shape[0]
    leaves = leaf_count * lax.axis_size("blk")
    code = col_group[:, 0] * leaves + col_leaf
    asked = [shift(code, "clus", d) for d in range(1, groups)]
    far_basis = shift(leaf_basis, "blk", 1)
    far_transfer = shift(transfer, "blk", 1)
    first, second, leaf_work = leaf_stage(leaf_basis)
    barrier = lax.optimization_barrier
    first, second, far_basis, far_transfer, asked = barrier(
        (first, second, far_basis, far_transfer, asked)
    )
    chips = range(2, lax.axis_size("blk"), 2)
    table, later = {0: first}, {0: second}
    for d in reversed(chips):
        table[d] = shift(first, "blk", d)
    table[1], later[1] = shift(first, "blk", 1), shift(second, "blk", 1)
    halves = parent_top(leaf_basis, transfer, far_basis, far_transfer)
    table[1], later[1], table[2], later[0], halves = barrier(
        (table[1], later[1], table[2], later[0], halves)
    )
    table[3] = shift(table[2], "blk", 1)
    later[2] = shift(later[0], "blk", 2)
    transfer_new = parent_low(transfer, leaf_work, halves)
    table, later, transfer_new = barrier((table, later, transfer_new))
    for d in reversed(chips[1:]):
        later[d] = shift(later[0], "blk", d)
    for d in chips[1:]:
        table[d + 1] = shift(table[d], "blk", 1)
    later[3] = shift(later[2], "blk", 1)
    served = serve(asked, in_order(table), capacity)
    fetched = [[shift(value, "clus", d + 1) for d, value in enumerate(served)]]
    for d in chips[1:]:
        later[d + 1] = shift(later[d], "blk", 1)
    later, fetched[0] = barrier((later, fetched[0]))
    served = serve(asked, in_order(later), capacity)
    fetched.append([shift(value, "clus", d + 1) for d, value in enumerate(served)])
    tables = [in_order(table), in_order(later)]
    near = near_stage(row_leaf, rank_slabs, tables, jnp.swapaxes(block_rows, 1, 2))
    coupling = far_stage(code, rank_slabs, near, tables, fetched, jnp.swapaxes(block_cols, 1, 2))
    return (coupling, transfer_new)


def solution(mesh):
    placed = (
        P(("clus", "blk"), None, None),
        P(("clus", "blk"), None, None),
        P(("clus", "blk"), None, None),
        P(("clus", "blk"), None, None),
        P(("clus", "blk")),
        P(("clus", "blk")),
        P(("clus", "blk"), None),
        P(("clus", "blk")),
    )
    return jax.shard_map(
        per_device,
        mesh=mesh,
        in_specs=placed,
        out_specs=(P(("clus", "blk"), None, None), P(("clus", "blk"), None, None)),
        check_vma=False,
    )
```

```python
import functools

import jax
import jax.numpy as jnp
from jax import lax
from jax.experimental import pallas as pl
from jax.experimental.pallas import tpu as pltpu
from jax.sharding import PartitionSpec as P

SLAB = 64
PANEL = 8
STRIP = 32
FIRST = 8
AHEAD = 4
VMEM_LIMIT = 40 * 1024 * 1024

NN = (((1,), (0,)), ((), ()))
NT = (((1,), (1,)), ((), ()))
TN = (((0,), (0,)), ((), ()))


def params():
    return pltpu.CompilerParams(vmem_limit_bytes=VMEM_LIMIT)


def cost(flops, moved):
    return pl.CostEstimate(flops=flops, bytes_accessed=moved, transcendentals=0)


def dot(left, right, dims):
    return lax.dot_general(left, right, dims, preferred_element_type=jnp.float32)


def split(value):
    high = value.astype(jnp.bfloat16)
    low = (value - high.astype(jnp.float32)).astype(jnp.bfloat16)
    return high, low


def dot_split(left, right, dims):
    (lh, ll), (rh, rl) = left, right
    return dot(lh, rh, dims) + (dot(lh, rl, dims) + dot(ll, rh, dims))


def lower_part(value):
    rows = lax.broadcasted_iota(jnp.int32, value.shape, 0)
    cols = lax.broadcasted_iota(jnp.int32, value.shape, 1)
    return jnp.where(cols <= rows, value, 0.0)


def factor(work, batch, size):
    lane = lax.broadcasted_iota(jnp.int32, (batch, size), 1)

    def spread(row, column):
        return jnp.broadcast_to(row[:, column : column + 1], (batch, size))

    for top in range(0, size, STRIP):
        rows = [work[pl.ds(top + i, batch, stride=size), :] for i in range(STRIP)]
        for q in range(0, STRIP, PANEL):
            first = top + q
            inside = (lane >= first) & (lane < first + PANEL)
            diag = {
                (i, j): spread(rows[q + i], first + j) for i in range(PANEL) for j in range(i, PANEL)
            }
            scale, upper = [], {}
            for k in range(PANEL):
                inv = lax.rsqrt(diag[k, k])
                scale.append(inv)
                for j in range(k + 1, PANEL):
                    upper[k, j] = diag[k, j] * inv
                for i in range(k + 1, PANEL):
                    for j in range(i, PANEL):
                        diag[i, j] = diag[i, j] - upper[k, i] * upper[k, j]
            done = []
            for k in range(PANEL):
                row = jnp.where(inside, jnp.where(lane == first + k, 1.0, 0.0), rows[q + k])
                for m in range(k):
                    row = row - upper[m, k] * done[m]
                done.append(row * scale[k])
            rows[q : q + PANEL] = done
            for i in range(q + PANEL, STRIP):
                row = jnp.where(inside, 0.0, rows[i])
                for k in range(PANEL):
                    row = row - spread(done[k], top + i) * done[k]
                rows[i] = row
        for i in range(STRIP):
            work[pl.ds(top + i, batch, stride=size), :] = rows[i]
        below = top + STRIP
        if below < size:
            for b in range(batch):
                strip = work[b * size + top : b * size + below, :]
                row = lax.broadcasted_iota(jnp.int32, strip.shape, 0) + top
                column = lax.broadcasted_iota(jnp.int32, strip.shape, 1)
                keep = (column <= row) | (column >= below)
                high, low = split(strip)
                left = jnp.concatenate([high, high, low], axis=0)
                high, low = split(jnp.where(keep, strip, 0.0))
                right = jnp.concatenate([high, low, high], axis=0)
                rest = work[b * size + below : (b + 1) * size, :]
                column = lax.broadcasted_iota(jnp.int32, rest.shape, 1)
                rest = jnp.where((column >= top) & (column < below), 0.0, rest)
                work[b * size + below : (b + 1) * size, :] = rest - dot(left, right, TN)[below:]


def leaf_kernel(basis, rows_out, work):
    count, points, rank = basis.shape
    for b in range(count):
        leaf = basis[b]
        work[b * rank : (b + 1) * rank, :] = dot(leaf, leaf, TN)
    factor(work, count, rank)
    for b in range(count):
        high, low = split(lower_part(work[b * rank : (b + 1) * rank, :]))
        leaf = basis[b]
        rows_out[b] = (dot(leaf, high, NT) + dot(leaf, low, NT)).astype(rows_out.dtype)


def parent_top_kernel(own_basis, own_transfer, far_basis, far_transfer, weighted, top, cross, corner):
    count, points, rank = own_basis.shape
    half = own_transfer.shape[2] // 2
    for j in range(count):
        other = (j + count // 2) % count
        total = None
        for basis, transfer, c in ((own_basis, own_transfer, j), (far_basis, far_transfer, other)):
            leaf = basis[c]
            gram = split(dot(leaf, leaf, TN))
            value = transfer[c]
            moved = dot_split(gram, split(value), NN)
            if basis is own_basis:
                weighted[c] = moved
            left, right = split(value[:, :half]), split(value[:, half:])
            moved_left, moved_right = split(moved[:, :half]), split(moved[:, half:])
            parts = (
                dot_split(left, moved_left, TN),
                dot_split(right, moved_left, TN),
                dot_split(right, moved_right, TN),
            )
            total = parts if total is None else tuple(a + b for a, b in zip(total, parts))
        top[j * half : (j + 1) * half, :] = total[0]
        cross[j] = total[1]
        corner[j] = total[2]
    factor(top, count, half)


def parent_low_kernel(leaf_work, weighted, top, cross, corner, out, work, coupled):
    count, rank, columns = weighted.shape
    half = columns // 2
    for j in range(count):
        inverse = split(lower_part(top[j * half : (j + 1) * half, :]))
        lower = dot_split(split(cross[j]), inverse, NT)
        coupled[j] = lower
        lower = split(lower)
        work[j * half : (j + 1) * half, :] = corner[j] - dot_split(lower, lower, NT)
    factor(work, count, half)
    for j in range(count):
        leaf_inverse = split(lower_part(leaf_work[j * rank : (j + 1) * rank, :]))
        stacked = dot_split(leaf_inverse, split(weighted[j]), NN)
        inverse = split(lower_part(top[j * half : (j + 1) * half, :]))
        first = dot_split(split(stacked[:, :half]), inverse, NT)
        rest = stacked[:, half:] - dot_split(split(first), split(coupled[j]), NT)
        inverse = split(lower_part(work[j * half : (j + 1) * half, :]))
        out[j, :, :half] = first
        out[j, :, half:] = dot_split(split(rest), inverse, NT)


def leaf_stage(leaf_basis):
    count, points, rank = leaf_basis.shape
    return pl.pallas_call(
        leaf_kernel,
        out_shape=(
            jax.ShapeDtypeStruct(leaf_basis.shape, jnp.bfloat16),
            jax.ShapeDtypeStruct((count * rank, rank), jnp.float32),
        ),
        compiler_params=params(),
        cost_estimate=cost(10**6, 10**5),
        name="leaf_factor",
    )(leaf_basis)


def parent_top(leaf_basis, transfer, far_basis, far_transfer):
    count, points, rank = leaf_basis.shape
    half = transfer.shape[2] // 2
    square = jax.ShapeDtypeStruct((count, half, half), jnp.float32)
    return pl.pallas_call(
        parent_top_kernel,
        out_shape=(
            jax.ShapeDtypeStruct(transfer.shape, jnp.float32),
            jax.ShapeDtypeStruct((count * half, half), jnp.float32),
            square,
            square,
        ),
        compiler_params=params(),
        cost_estimate=cost(10**6, 10**5),
        name="parent_top",
    )(leaf_basis, transfer, far_basis, far_transfer)


def parent_low(transfer, leaf_work, halves):
    count, rank, columns = transfer.shape
    half = columns // 2
    return pl.pallas_call(
        parent_low_kernel,
        out_shape=jax.ShapeDtypeStruct(transfer.shape, jnp.float32),
        scratch_shapes=[
            pltpu.VMEM((count * half, half), jnp.float32),
            pltpu.VMEM((count, half, half), jnp.float32),
        ],
        compiler_params=params(),
        cost_estimate=cost(10**6, 10**5),
        name="parent_low",
    )(leaf_work, *halves)


def quotient(value, size):
    return value >> (size.bit_length() - 1) if size & (size - 1) == 0 else lax.div(value, size)


def remainder(value, size):
    return value & (size - 1) if size & (size - 1) == 0 else lax.rem(value, size)


def shift(value, axis, d):
    pairs = [(index ^ d, index) for index in range(lax.axis_size(axis))]
    return lax.ppermute(value, axis, pairs)


def send(value, moves):
    pairs = [(2 * source + core, 2 * target + core) for source, target in moves for core in range(2)]
    return lax.ppermute(value, "blk", pairs)


def in_order(table):
    return [table[d] for d in range(len(table))]


def points_split(points):
    first = points * FIRST // 16
    return (slice(0, first), slice(first, points))


def pick(table, leaf, span, store):
    count = table[0].shape[0]
    place = quotient(leaf, count) ^ lax.axis_index("blk")
    for d in range(len(table)):

        @pl.when(place == d)
        def _():
            rows = span if table[d].shape[1] > span.stop - span.start else slice(None)
            store(table[d][remainder(leaf, count), rows, :])


def serve_kernel(groups, size, span, *refs):
    asked, table, outs = refs[: groups - 1], refs[groups - 1 : groups - 1 + size], refs[1 - groups :]
    me = lax.axis_index("clus")
    leaves = size * table[0].shape[0]
    for d in range(1, groups):

        def place(b, position, d=d):
            code = asked[d - 1][b]
            mine = quotient(code, leaves) == me

            @pl.when(mine)
            def _():
                def store(value):
                    outs[d - 1][position] = value

                pick(table, remainder(code, leaves), span, store)

            return position + mine.astype(jnp.int32)

        lax.fori_loop(0, asked[0].shape[0], place, jnp.int32(0))


def serve(asked, table, span, capacity):
    groups, size = len(asked) + 1, len(table)
    smem, vmem = pl.BlockSpec(memory_space=pltpu.SMEM), pl.BlockSpec(memory_space=pltpu.VMEM)
    shape = (capacity, span.stop - span.start, table[0].shape[2])
    return pl.pallas_call(
        functools.partial(serve_kernel, groups, size, span),
        in_specs=[smem] * (groups - 1) + [vmem] * size,
        out_specs=[vmem] * (groups - 1),
        out_shape=[jax.ShapeDtypeStruct(shape, table[0].dtype)] * (groups - 1),
        compiler_params=params(),
        cost_estimate=cost(10**6, 10**5),
        name="serve",
    )(*asked, *table)


def near_kernel(size, leaf, slabs, *refs):
    table, (factors, out, held) = refs[:-3], refs[-3:]
    count, width, points = factors.shape
    spans = points_split(points)

    def gather(b, carry):
        for c in range(len(spans)):

            def store(value, c=c):
                held[b, spans[c], :] = value

            pick(table[c * size : (c + 1) * size], leaf[b], spans[c], store)
        return carry

    lax.fori_loop(0, count, gather, 0)
    row = lax.broadcasted_iota(jnp.int32, (width, out.shape[1]), 0)
    for b in range(count):
        value = dot(factors[b], held[b], NN)
        value = jnp.where(row < slabs[b] * SLAB, value, 0.0)
        out[b] = value.T.astype(out.dtype)


def near_stage(row_leaf, rank_slabs, tables, factors):
    count, width, points = factors.shape
    size, rank = len(tables[0]), tables[0][0].shape[2]
    smem, vmem = pl.BlockSpec(memory_space=pltpu.SMEM), pl.BlockSpec(memory_space=pltpu.VMEM)
    flat = [piece for table in tables for piece in table]
    return pl.pallas_call(
        functools.partial(near_kernel, size),
        in_specs=[smem, smem] + [vmem] * len(flat) + [vmem],
        out_specs=vmem,
        out_shape=jax.ShapeDtypeStruct((count, rank, width), jnp.bfloat16),
        scratch_shapes=[pltpu.VMEM((count, points, rank), flat[0].dtype)],
        compiler_params=params(),
        cost_estimate=cost(10**6, 10**5),
        name="near",
    )(row_leaf, rank_slabs, *flat, factors)


def far_kernel(groups, size, chunks, code, slabs, near, *refs):
    table, refs = refs[: chunks * size], refs[chunks * size :]
    fetched, (factors, out, held, tally) = refs[: chunks * (groups - 1)], refs[chunks * (groups - 1) :]
    count, width, points = factors.shape
    leaves = size * table[0].shape[0]
    spans = points_split(points)
    me = lax.axis_index("clus")
    for g in range(groups):
        tally[g] = 0

    def gather(b, carry):
        group, leaf = quotient(code[b], leaves), remainder(code[b], leaves)
        position = tally[group]
        tally[group] = position + 1
        away = group ^ me

        @pl.when(away == 0)
        def _():
            for c in range(chunks):

                def store(value, c=c):
                    held[b, spans[c], :] = value

                pick(table[c * size : (c + 1) * size], leaf, spans[c], store)

        for d in range(1, groups):

            @pl.when(away == d)
            def _(d=d):
                for c in range(chunks):
                    piece = fetched[c * (groups - 1) + d - 1]
                    held[b, spans[c], :] = piece[position]

        return carry

    lax.fori_loop(0, count, gather, 0)
    row = lax.broadcasted_iota(jnp.int32, (width, near.shape[1]), 0)
    for first in range(0, count, AHEAD):
        values = [dot(factors[b], held[b], NN) for b in range(first, first + AHEAD)]
        for b in range(first, first + AHEAD):
            value = jnp.where(row < slabs[b] * SLAB, values[b - first], 0.0).astype(near.dtype)
            out[b] = dot(near[b], value, NN)


def far_stage(code, rank_slabs, near, tables, fetched, factors):
    count, width, points = factors.shape
    size, rank = len(tables[0]), tables[0][0].shape[2]
    groups = len(fetched[0]) + 1
    smem, vmem = pl.BlockSpec(memory_space=pltpu.SMEM), pl.BlockSpec(memory_space=pltpu.VMEM)
    flat = [piece for table in tables for piece in table] + [piece for part in fetched for piece in part]
    return pl.pallas_call(
        functools.partial(far_kernel, groups, size, len(tables)),
        in_specs=[smem, smem, vmem] + [vmem] * len(flat) + [vmem],
        out_specs=vmem,
        out_shape=jax.ShapeDtypeStruct((count, rank, rank), jnp.float32),
        scratch_shapes=[
            pltpu.VMEM((count, points, rank), flat[0].dtype),
            pltpu.SMEM((groups,), jnp.int32),
        ],
        compiler_params=params(),
        cost_estimate=cost(10**6, 10**5),
        name="far",
    )(code, rank_slabs, near, *flat, factors)


def per_device(
    leaf_basis, transfer, block_rows, block_cols, rank_slabs, row_leaf, col_group, col_leaf
):
    groups = lax.axis_size("clus")
    block_count = block_rows.shape[0]
    capacity = max(2, 2 * block_count // groups)
    leaf_count = leaf_basis.shape[0]
    leaves = leaf_count * lax.axis_size("blk")
    code = col_group[:, 0] * leaves + col_leaf
    size = lax.axis_size("blk")
    spans = points_split(leaf_basis.shape[1])
    barrier = lax.optimization_barrier
    far_basis = shift(leaf_basis, "blk", 1)
    far_transfer = shift(transfer, "blk", 1)
    rows, leaf_work = leaf_stage(leaf_basis)
    rows, far_basis, far_transfer, code = barrier((rows, far_basis, far_transfer, code))
    forward = size == 8
    table = {0: rows}
    asked = [shift(code, "clus", d) for d in range(1, groups)]
    if forward:
        table[2] = shift(rows, "blk", 2)
        middle = send(rows, [(1, 2), (2, 1)])
    else:
        middle = rows
        for d in range(2, size, 2):
            table[d] = shift(rows, "blk", d)
    halves = parent_top(leaf_basis, transfer, far_basis, far_transfer)
    table, middle, asked, halves = barrier((table, middle, asked, halves))
    if forward:
        inner = send(table[2], [(1, 2), (2, 1)])
        outer = send(middle, [(1, 0), (2, 3)])
    for d in list(table):
        table[d + 1] = shift(table[d], "blk", 1)
    transfer_new = parent_low(transfer, leaf_work, halves)
    if forward:
        inner, outer, table, transfer_new = barrier((inner, outer, table, transfer_new))
    else:
        table, transfer_new = barrier((table, transfer_new))
    if forward:
        last = send(inner[:, spans[0]], [(1, 0), (2, 3)])
        table[4] = inner + outer
        table[5] = shift(table[4], "blk", 1)
    if forward:
        last, inner, table = barrier((last, inner, table))
    tables, fetched = [], []
    for c, span in enumerate(spans):
        if forward:
            part = middle[:, span] + last
            table = {**table, 6: part, 7: shift(part, "blk", 1)}
            if c == 0:
                last = send(inner[:, spans[1]], [(1, 0), (2, 3)])
        if c > 0:
            table, fetched[0] = barrier((table, fetched[0]))
        tables.append(in_order(table))
        served = serve(asked, tables[c], span, capacity)
        if forward and c == 0:
            last, _ = barrier((last, served))
        fetched.append([shift(value, "clus", d + 1) for d, value in enumerate(served)])
    near = near_stage(row_leaf, rank_slabs, tables, jnp.swapaxes(block_rows, 1, 2))
    coupling = far_stage(code, rank_slabs, near, tables, fetched, jnp.swapaxes(block_cols, 1, 2))
    return (coupling, transfer_new)


def solution(mesh):
    placed = (
        P(("clus", "blk"), None, None),
        P(("clus", "blk"), None, None),
        P(("clus", "blk"), None, None),
        P(("clus", "blk"), None, None),
        P(("clus", "blk")),
        P(("clus", "blk")),
        P(("clus", "blk"), None),
        P(("clus", "blk")),
    )
    return jax.shard_map(
        per_device,
        mesh=mesh,
        in_specs=placed,
        out_specs=(P(("clus", "blk"), None, None), P(("clus", "blk"), None, None)),
        check_vma=False,
    )
```

```python
import functools

import jax
import jax.numpy as jnp
from jax import lax
from jax.experimental import pallas as pl
from jax.experimental.pallas import tpu as pltpu
from jax.sharding import PartitionSpec as P

SLAB = 64
PANEL = 8
STRIP = 32
FIRST = 10
AHEAD = 4
VMEM_LIMIT = 24 * 1024 * 1024

NN = (((1,), (0,)), ((), ()))
NT = (((1,), (1,)), ((), ()))
TN = (((0,), (0,)), ((), ()))


def params():
    return pltpu.CompilerParams(vmem_limit_bytes=VMEM_LIMIT)


def cost(flops, moved):
    return pl.CostEstimate(flops=flops, bytes_accessed=moved, transcendentals=0)


def dot(left, right, dims):
    return lax.dot_general(left, right, dims, preferred_element_type=jnp.float32)


def split(value):
    high = value.astype(jnp.bfloat16)
    low = (value - high.astype(jnp.float32)).astype(jnp.bfloat16)
    return high, low


def dot_split(left, right, dims):
    (lh, ll), (rh, rl) = left, right
    return dot(lh, rh, dims) + (dot(lh, rl, dims) + dot(ll, rh, dims))


def lower_part(value):
    rows = lax.broadcasted_iota(jnp.int32, value.shape, 0)
    cols = lax.broadcasted_iota(jnp.int32, value.shape, 1)
    return jnp.where(cols <= rows, value, 0.0)


def factor(work, batch, size):
    lane = lax.broadcasted_iota(jnp.int32, (batch, size), 1)

    def spread(row, column):
        return jnp.broadcast_to(row[:, column : column + 1], (batch, size))

    for top in range(0, size, STRIP):
        rows = [work[pl.ds(top + i, batch, stride=size), :] for i in range(STRIP)]
        for q in range(0, STRIP, PANEL):
            first = top + q
            inside = (lane >= first) & (lane < first + PANEL)
            diag = {
                (i, j): spread(rows[q + i], first + j) for i in range(PANEL) for j in range(i, PANEL)
            }
            scale, upper = [], {}
            for k in range(PANEL):
                inv = lax.rsqrt(diag[k, k])
                scale.append(inv)
                for j in range(k + 1, PANEL):
                    upper[k, j] = diag[k, j] * inv
                for i in range(k + 1, PANEL):
                    for j in range(i, PANEL):
                        diag[i, j] = diag[i, j] - upper[k, i] * upper[k, j]
            done = []
            for k in range(PANEL):
                row = jnp.where(inside, jnp.where(lane == first + k, 1.0, 0.0), rows[q + k])
                for m in range(k):
                    row = row - upper[m, k] * done[m]
                done.append(row * scale[k])
            rows[q : q + PANEL] = done
            for i in range(q + PANEL, STRIP):
                row = jnp.where(inside, 0.0, rows[i])
                for k in range(PANEL):
                    row = row - spread(done[k], top + i) * done[k]
                rows[i] = row
        for i in range(STRIP):
            work[pl.ds(top + i, batch, stride=size), :] = rows[i]
        below = top + STRIP
        if below < size:
            for b in range(batch):
                strip = work[b * size + top : b * size + below, :]
                row = lax.broadcasted_iota(jnp.int32, strip.shape, 0) + top
                column = lax.broadcasted_iota(jnp.int32, strip.shape, 1)
                keep = (column <= row) | (column >= below)
                high, low = split(strip)
                left = jnp.concatenate([high, high, low], axis=0)
                high, low = split(jnp.where(keep, strip, 0.0))
                right = jnp.concatenate([high, low, high], axis=0)
                rest = work[b * size + below : (b + 1) * size, :]
                column = lax.broadcasted_iota(jnp.int32, rest.shape, 1)
                rest = jnp.where((column >= top) & (column < below), 0.0, rest)
                work[b * size + below : (b + 1) * size, :] = rest - dot(left, right, TN)[below:]


def leaf_kernel(leaves, group, leaf_of, basis, code, rows_out, *rest):
    pieces, work = rest[:-1], rest[-1]
    count, points, rank = basis.shape

    def pack(b, carry):
        code[b] = group[b] * leaves + leaf_of[b]
        return carry

    lax.fori_loop(0, code.shape[0], pack, 0)
    for b in range(count):
        leaf = basis[b]
        work[b * rank : (b + 1) * rank, :] = dot(leaf, leaf, TN)
    factor(work, count, rank)
    for b in range(count):
        high, low = split(lower_part(work[b * rank : (b + 1) * rank, :]))
        leaf = basis[b]
        value = (dot(leaf, high, NT) + dot(leaf, low, NT)).astype(rows_out.dtype)
        rows_out[b] = value
        for span, piece in zip(points_split(points), pieces):
            piece[b] = value[span]


def parent_top_kernel(own_basis, own_transfer, far_basis, far_transfer, weighted, top, cross, corner):
    count, points, rank = own_basis.shape
    half = own_transfer.shape[2] // 2
    for j in range(count):
        other = (j + count // 2) % count
        total = None
        for basis, transfer, c in ((own_basis, own_transfer, j), (far_basis, far_transfer, other)):
            leaf = basis[c]
            gram = split(dot(leaf, leaf, TN))
            value = transfer[c]
            moved = dot_split(gram, split(value), NN)
            if basis is own_basis:
                weighted[c] = moved
            left, right = split(value[:, :half]), split(value[:, half:])
            moved_left, moved_right = split(moved[:, :half]), split(moved[:, half:])
            parts = (
                dot_split(left, moved_left, TN),
                dot_split(right, moved_left, TN),
                dot_split(right, moved_right, TN),
            )
            total = parts if total is None else tuple(a + b for a, b in zip(total, parts))
        top[j * half : (j + 1) * half, :] = total[0]
        cross[j] = total[1]
        corner[j] = total[2]
    factor(top, count, half)


def parent_low_kernel(leaf_work, weighted, top, cross, corner, out, work, coupled):
    count, rank, columns = weighted.shape
    half = columns // 2
    for j in range(count):
        inverse = split(lower_part(top[j * half : (j + 1) * half, :]))
        lower = dot_split(split(cross[j]), inverse, NT)
        coupled[j] = lower
        lower = split(lower)
        work[j * half : (j + 1) * half, :] = corner[j] - dot_split(lower, lower, NT)
    factor(work, count, half)
    for j in range(count):
        leaf_inverse = split(lower_part(leaf_work[j * rank : (j + 1) * rank, :]))
        stacked = dot_split(leaf_inverse, split(weighted[j]), NN)
        inverse = split(lower_part(top[j * half : (j + 1) * half, :]))
        first = dot_split(split(stacked[:, :half]), inverse, NT)
        rest = stacked[:, half:] - dot_split(split(first), split(coupled[j]), NT)
        inverse = split(lower_part(work[j * half : (j + 1) * half, :]))
        out[j, :, :half] = first
        out[j, :, half:] = dot_split(split(rest), inverse, NT)


def leaf_stage(leaf_basis, leaves, group, leaf_of):
    count, points, rank = leaf_basis.shape
    smem, vmem = pl.BlockSpec(memory_space=pltpu.SMEM), pl.BlockSpec(memory_space=pltpu.VMEM)
    parts = [points] + [span.stop - span.start for span in points_split(points)]
    return pl.pallas_call(
        functools.partial(leaf_kernel, leaves),
        in_specs=[smem, smem, vmem],
        out_specs=[smem] + [vmem] * (len(parts) + 1),
        out_shape=[jax.ShapeDtypeStruct(leaf_of.shape, jnp.int32)]
        + [jax.ShapeDtypeStruct((count, part, rank), jnp.bfloat16) for part in parts]
        + [jax.ShapeDtypeStruct((count * rank, rank), jnp.float32)],
        compiler_params=params(),
        cost_estimate=cost(10**6, 10**5),
        name="leaf_factor",
    )(group, leaf_of, leaf_basis)


def parent_top(leaf_basis, transfer, far_basis, far_transfer):
    count, points, rank = leaf_basis.shape
    half = transfer.shape[2] // 2
    square = jax.ShapeDtypeStruct((count, half, half), jnp.float32)
    return pl.pallas_call(
        parent_top_kernel,
        out_shape=(
            jax.ShapeDtypeStruct(transfer.shape, jnp.float32),
            jax.ShapeDtypeStruct((count * half, half), jnp.float32),
            square,
            square,
        ),
        compiler_params=params(),
        cost_estimate=cost(10**6, 10**5),
        name="parent_top",
    )(leaf_basis, transfer, far_basis, far_transfer)


def parent_low(transfer, leaf_work, halves):
    count, rank, columns = transfer.shape
    half = columns // 2
    return pl.pallas_call(
        parent_low_kernel,
        out_shape=jax.ShapeDtypeStruct(transfer.shape, jnp.float32),
        scratch_shapes=[
            pltpu.VMEM((count * half, half), jnp.float32),
            pltpu.VMEM((count, half, half), jnp.float32),
        ],
        compiler_params=params(),
        cost_estimate=cost(10**6, 10**5),
        name="parent_low",
    )(leaf_work, *halves)


def quotient(value, size):
    return value >> (size.bit_length() - 1) if size & (size - 1) == 0 else lax.div(value, size)


def remainder(value, size):
    return value & (size - 1) if size & (size - 1) == 0 else lax.rem(value, size)


def shift(value, axis, d):
    pairs = [(index ^ d, index) for index in range(lax.axis_size(axis))]
    return lax.ppermute(value, axis, pairs)


def joined(values, bit):
    return jnp.concatenate([values, shift(values, "clus", bit)], axis=0)


def in_order(table):
    return [table[d] for d in range(len(table))]


def points_split(points):
    first = points * FIRST // 16
    return (slice(0, first), slice(first, points))


def pick(table, leaf, span, store):
    count = table[0].shape[0]
    place = quotient(leaf, count) ^ lax.axis_index("blk")
    for d in range(len(table)):

        @pl.when(place == d)
        def _():
            rows = span if table[d].shape[1] > span.stop - span.start else slice(None)
            store(table[d][remainder(leaf, count), rows, :])


def serve_kernel(size, span, asked, *refs):
    table, outs = refs[:size], refs[size:]
    me = lax.axis_index("clus")
    leaves = size * table[0].shape[0]
    for d in range(1, asked.shape[0]):

        def place(b, position, d=d):
            code = asked[d, b]
            mine = quotient(code, leaves) == me

            @pl.when(mine)
            def _():
                def store(value):
                    outs[d - 1][position] = value

                pick(table, remainder(code, leaves), span, store)

            return position + mine.astype(jnp.int32)

        lax.fori_loop(0, asked.shape[1], place, jnp.int32(0))


def serve(asked, table, span, capacity):
    groups, size = asked.shape[0], len(table)
    smem, vmem = pl.BlockSpec(memory_space=pltpu.SMEM), pl.BlockSpec(memory_space=pltpu.VMEM)
    shape = (capacity, span.stop - span.start, table[0].shape[2])
    return pl.pallas_call(
        functools.partial(serve_kernel, size, span),
        in_specs=[smem] + [vmem] * size,
        out_specs=[vmem] * (groups - 1),
        out_shape=[jax.ShapeDtypeStruct(shape, table[0].dtype)] * (groups - 1),
        compiler_params=params(),
        cost_estimate=cost(10**6, 10**5),
        name="serve",
    )(asked, *table)


def near_kernel(size, leaf, slabs, *refs):
    table, (factors, out, held) = refs[:-3], refs[-3:]
    count, width, points = factors.shape
    spans = points_split(points)

    def gather(b, carry):
        for c in range(len(spans)):

            def store(value, c=c):
                held[b, spans[c], :] = value

            pick(table[c * size : (c + 1) * size], leaf[b], spans[c], store)
        return carry

    lax.fori_loop(0, count, gather, 0)
    row = lax.broadcasted_iota(jnp.int32, (width, out.shape[1]), 0)
    for b in range(count):
        value = dot(factors[b], held[b], NN)
        value = jnp.where(row < slabs[b] * SLAB, value, 0.0)
        out[b] = value.T.astype(out.dtype)


def near_stage(row_leaf, rank_slabs, tables, factors):
    count, width, points = factors.shape
    size, rank = len(tables[0]), tables[0][0].shape[2]
    smem, vmem = pl.BlockSpec(memory_space=pltpu.SMEM), pl.BlockSpec(memory_space=pltpu.VMEM)
    flat = [piece for table in tables for piece in table]
    return pl.pallas_call(
        functools.partial(near_kernel, size),
        in_specs=[smem, smem] + [vmem] * len(flat) + [vmem],
        out_specs=vmem,
        out_shape=jax.ShapeDtypeStruct((count, rank, width), jnp.bfloat16),
        scratch_shapes=[pltpu.VMEM((count, points, rank), flat[0].dtype)],
        compiler_params=params(),
        cost_estimate=cost(10**6, 10**5),
        name="near",
    )(row_leaf, rank_slabs, *flat, factors)


def far_kernel(groups, size, chunks, code, slabs, near, *refs):
    table, refs = refs[: chunks * size], refs[chunks * size :]
    fetched, (factors, out, held, tally) = refs[: chunks * (groups - 1)], refs[chunks * (groups - 1) :]
    count, width, points = factors.shape
    leaves = size * table[0].shape[0]
    spans = points_split(points)
    me = lax.axis_index("clus")
    for g in range(groups):
        tally[g] = 0

    def gather(b, carry):
        group, leaf = quotient(code[b], leaves), remainder(code[b], leaves)
        position = tally[group]
        tally[group] = position + 1
        away = group ^ me

        @pl.when(away == 0)
        def _():
            for c in range(chunks):

                def store(value, c=c):
                    held[b, spans[c], :] = value

                pick(table[c * size : (c + 1) * size], leaf, spans[c], store)

        for d in range(1, groups):

            @pl.when(away == d)
            def _(d=d):
                for c in range(chunks):
                    piece = fetched[c * (groups - 1) + d - 1]
                    held[b, spans[c], :] = piece[position]

        return carry

    lax.fori_loop(0, count, gather, 0)
    row = lax.broadcasted_iota(jnp.int32, (width, near.shape[1]), 0)
    for first in range(0, count, AHEAD):
        values = [dot(factors[b], held[b], NN) for b in range(first, first + AHEAD)]
        for b in range(first, first + AHEAD):
            value = jnp.where(row < slabs[b] * SLAB, values[b - first], 0.0).astype(near.dtype)
            out[b] = dot(near[b], value, NN)


def far_stage(code, rank_slabs, near, tables, fetched, factors):
    count, width, points = factors.shape
    size, rank = len(tables[0]), tables[0][0].shape[2]
    groups = len(fetched[0]) + 1
    smem, vmem = pl.BlockSpec(memory_space=pltpu.SMEM), pl.BlockSpec(memory_space=pltpu.VMEM)
    flat = [piece for table in tables for piece in table] + [piece for part in fetched for piece in part]
    return pl.pallas_call(
        functools.partial(far_kernel, groups, size, len(tables)),
        in_specs=[smem, smem, vmem] + [vmem] * len(flat) + [vmem],
        out_specs=vmem,
        out_shape=jax.ShapeDtypeStruct((count, rank, rank), jnp.float32),
        scratch_shapes=[
            pltpu.VMEM((count, points, rank), flat[0].dtype),
            pltpu.SMEM((groups,), jnp.int32),
        ],
        compiler_params=params(),
        cost_estimate=cost(10**6, 10**5),
        name="far",
    )(code, rank_slabs, near, *flat, factors)


def per_device(
    leaf_basis, transfer, block_rows, block_cols, rank_slabs, row_leaf, col_group, col_leaf
):
    groups, size = lax.axis_size("clus"), lax.axis_size("blk")
    capacity = max(2, 2 * block_rows.shape[0] // groups)
    spans = points_split(leaf_basis.shape[1])
    barrier = lax.optimization_barrier
    far_basis = shift(leaf_basis, "blk", 1)
    far_transfer = shift(transfer, "blk", 1)
    code, rows, first, second, leaf_work = leaf_stage(
        leaf_basis, leaf_basis.shape[0] * size, col_group[:, 0], col_leaf
    )
    code, rows, first, second, far_basis, far_transfer = barrier(
        (code, rows, first, second, far_basis, far_transfer)
    )
    chips = range(4, size, 2)
    table = {d: shift(first, "blk", d) for d in reversed(chips)}
    close = {0: rows, 2: shift(rows, "blk", 2)}
    asked = joined(code[None], 1)
    halves = parent_top(leaf_basis, transfer, far_basis, far_transfer)
    asked, close, second, halves = barrier((asked, close, second, halves))
    close[1] = shift(close[0], "blk", 1)
    later = {d: shift(second, "blk", d) for d in reversed(chips)}
    bit = 2
    while bit < groups:
        asked = joined(asked, bit)
        bit *= 2
    transfer_new = parent_low(transfer, leaf_work, halves)
    table, close, asked, transfer_new = barrier((table, close, asked, transfer_new))
    for d in chips:
        table[d + 1] = shift(table[d], "blk", 1)
    close[3] = shift(close[2], "blk", 1)
    served = serve(asked, in_order(close | table), spans[0], capacity)
    fetched = [[shift(value, "clus", d + 1) for d, value in enumerate(served)]]
    later, fetched[0][0] = barrier((later, fetched[0][0]))
    for d in chips:
        later[d + 1] = shift(later[d], "blk", 1)
    later, fetched[0] = barrier((later, fetched[0]))
    served = serve(asked, in_order(close | later), spans[1], capacity)
    fetched.append([shift(value, "clus", d + 1) for d, value in enumerate(served)])
    tables = [in_order(close | table), in_order(close | later)]
    near = near_stage(row_leaf, rank_slabs, tables, jnp.swapaxes(block_rows, 1, 2))
    coupling = far_stage(asked[0], rank_slabs, near, tables, fetched, jnp.swapaxes(block_cols, 1, 2))
    return (coupling, transfer_new)


def solution(mesh):
    placed = (
        P(("clus", "blk"), None, None),
        P(("clus", "blk"), None, None),
        P(("clus", "blk"), None, None),
        P(("clus", "blk"), None, None),
        P(("clus", "blk")),
        P(("clus", "blk")),
        P(("clus", "blk"), None),
        P(("clus", "blk")),
    )
    return jax.shard_map(
        per_device,
        mesh=mesh,
        in_specs=placed,
        out_specs=(P(("clus", "blk"), None, None), P(("clus", "blk"), None, None)),
        check_vma=False,
    )
```

```python
import functools

import jax
import jax.numpy as jnp
from jax import lax
from jax.experimental import pallas as pl
from jax.experimental.pallas import tpu as pltpu
from jax.sharding import PartitionSpec as P

SLAB = 64
PANEL = 8
STRIP = 32
FIRST = 10
AHEAD = 4
VMEM_LIMIT = 24 * 1024 * 1024

NN = (((1,), (0,)), ((), ()))
NT = (((1,), (1,)), ((), ()))
TN = (((0,), (0,)), ((), ()))


def params():
    return pltpu.CompilerParams(vmem_limit_bytes=VMEM_LIMIT)


def cost(flops, moved):
    return pl.CostEstimate(flops=flops, bytes_accessed=moved, transcendentals=0)


def dot(left, right, dims):
    return lax.dot_general(left, right, dims, preferred_element_type=jnp.float32)


def split(value):
    high = value.astype(jnp.bfloat16)
    low = (value - high.astype(jnp.float32)).astype(jnp.bfloat16)
    return high, low


def dot_split(left, right, dims):
    (lh, ll), (rh, rl) = left, right
    return dot(lh, rh, dims) + (dot(lh, rl, dims) + dot(ll, rh, dims))


def lower_part(value):
    rows = lax.broadcasted_iota(jnp.int32, value.shape, 0)
    cols = lax.broadcasted_iota(jnp.int32, value.shape, 1)
    return jnp.where(cols <= rows, value, 0.0)


def factor(work, batch, size):
    lane = lax.broadcasted_iota(jnp.int32, (batch, size), 1)

    def spread(row, column):
        return jnp.broadcast_to(row[:, column : column + 1], (batch, size))

    for top in range(0, size, STRIP):
        rows = [work[pl.ds(top + i, batch, stride=size), :] for i in range(STRIP)]
        for q in range(0, STRIP, PANEL):
            first = top + q
            inside = (lane >= first) & (lane < first + PANEL)
            diag = {
                (i, j): spread(rows[q + i], first + j) for i in range(PANEL) for j in range(i, PANEL)
            }
            scale, upper = [], {}
            for k in range(PANEL):
                inv = lax.rsqrt(diag[k, k])
                scale.append(inv)
                for j in range(k + 1, PANEL):
                    upper[k, j] = diag[k, j] * inv
                for i in range(k + 1, PANEL):
                    for j in range(i, PANEL):
                        diag[i, j] = diag[i, j] - upper[k, i] * upper[k, j]
            done = []
            for k in range(PANEL):
                row = jnp.where(inside, jnp.where(lane == first + k, 1.0, 0.0), rows[q + k])
                for m in range(k):
                    row = row - upper[m, k] * done[m]
                done.append(row * scale[k])
            rows[q : q + PANEL] = done
            for i in range(q + PANEL, STRIP):
                row = jnp.where(inside, 0.0, rows[i])
                for k in range(PANEL):
                    row = row - spread(done[k], top + i) * done[k]
                rows[i] = row
        for i in range(STRIP):
            work[pl.ds(top + i, batch, stride=size), :] = rows[i]
        below = top + STRIP
        if below < size:
            for b in range(batch):
                strip = work[b * size + top : b * size + below, :]
                row = lax.broadcasted_iota(jnp.int32, strip.shape, 0) + top
                column = lax.broadcasted_iota(jnp.int32, strip.shape, 1)
                keep = (column <= row) | (column >= below)
                high, low = split(strip)
                left = jnp.concatenate([high, high, low], axis=0)
                high, low = split(jnp.where(keep, strip, 0.0))
                right = jnp.concatenate([high, low, high], axis=0)
                rest = work[b * size + below : (b + 1) * size, :]
                column = lax.broadcasted_iota(jnp.int32, rest.shape, 1)
                rest = jnp.where((column >= top) & (column < below), 0.0, rest)
                work[b * size + below : (b + 1) * size, :] = rest - dot(left, right, TN)[below:]


def leaf_kernel(leaves, group, leaf_of, basis, code, rows_out, *rest):
    pieces, work = rest[:-1], rest[-1]
    count, points, rank = basis.shape

    def pack(b, carry):
        code[b] = group[b] * leaves + leaf_of[b]
        return carry

    lax.fori_loop(0, code.shape[0], pack, 0)
    for b in range(count):
        leaf = basis[b]
        work[b * rank : (b + 1) * rank, :] = dot(leaf, leaf, TN)
    factor(work, count, rank)
    for b in range(count):
        high, low = split(lower_part(work[b * rank : (b + 1) * rank, :]))
        leaf = basis[b]
        value = (dot(leaf, high, NT) + dot(leaf, low, NT)).astype(rows_out.dtype)
        rows_out[b] = value
        for span, piece in zip(points_split(points), pieces):
            piece[b] = value[span]


def parent_top_kernel(own_basis, own_transfer, far_basis, far_transfer, weighted, top, cross, corner):
    count, points, rank = own_basis.shape
    half = own_transfer.shape[2] // 2
    for j in range(count):
        other = (j + count // 2) % count
        total = None
        for basis, transfer, c in ((own_basis, own_transfer, j), (far_basis, far_transfer, other)):
            leaf = basis[c]
            gram = split(dot(leaf, leaf, TN))
            value = transfer[c]
            moved = dot_split(gram, split(value), NN)
            if basis is own_basis:
                weighted[c] = moved
            left, right = split(value[:, :half]), split(value[:, half:])
            moved_left, moved_right = split(moved[:, :half]), split(moved[:, half:])
            parts = (
                dot_split(left, moved_left, TN),
                dot_split(right, moved_left, TN),
                dot_split(right, moved_right, TN),
            )
            total = parts if total is None else tuple(a + b for a, b in zip(total, parts))
        top[j * half : (j + 1) * half, :] = total[0]
        cross[j] = total[1]
        corner[j] = total[2]
    factor(top, count, half)


def parent_low_kernel(leaf_work, weighted, top, cross, corner, out, work, coupled):
    count, rank, columns = weighted.shape
    half = columns // 2
    for j in range(count):
        inverse = split(lower_part(top[j * half : (j + 1) * half, :]))
        lower = dot_split(split(cross[j]), inverse, NT)
        coupled[j] = lower
        lower = split(lower)
        work[j * half : (j + 1) * half, :] = corner[j] - dot_split(lower, lower, NT)
    factor(work, count, half)
    for j in range(count):
        leaf_inverse = split(lower_part(leaf_work[j * rank : (j + 1) * rank, :]))
        stacked = dot_split(leaf_inverse, split(weighted[j]), NN)
        inverse = split(lower_part(top[j * half : (j + 1) * half, :]))
        first = dot_split(split(stacked[:, :half]), inverse, NT)
        rest = stacked[:, half:] - dot_split(split(first), split(coupled[j]), NT)
        inverse = split(lower_part(work[j * half : (j + 1) * half, :]))
        out[j, :, :half] = first
        out[j, :, half:] = dot_split(split(rest), inverse, NT)


def leaf_stage(leaf_basis, leaves, group, leaf_of):
    count, points, rank = leaf_basis.shape
    smem, vmem = pl.BlockSpec(memory_space=pltpu.SMEM), pl.BlockSpec(memory_space=pltpu.VMEM)
    parts = [points] + [span.stop - span.start for span in points_split(points)]
    return pl.pallas_call(
        functools.partial(leaf_kernel, leaves),
        in_specs=[smem, smem, vmem],
        out_specs=[smem] + [vmem] * (len(parts) + 1),
        out_shape=[jax.ShapeDtypeStruct(leaf_of.shape, jnp.int32)]
        + [jax.ShapeDtypeStruct((count, part, rank), jnp.bfloat16) for part in parts]
        + [jax.ShapeDtypeStruct((count * rank, rank), jnp.float32)],
        compiler_params=params(),
        cost_estimate=cost(10**9, 25 * 10**6),
        name="leaf_factor",
    )(group, leaf_of, leaf_basis)


def parent_top(leaf_basis, transfer, far_basis, far_transfer):
    count, points, rank = leaf_basis.shape
    half = transfer.shape[2] // 2
    square = jax.ShapeDtypeStruct((count, half, half), jnp.float32)
    return pl.pallas_call(
        parent_top_kernel,
        out_shape=(
            jax.ShapeDtypeStruct(transfer.shape, jnp.float32),
            jax.ShapeDtypeStruct((count * half, half), jnp.float32),
            square,
            square,
        ),
        compiler_params=params(),
        cost_estimate=cost(10**9, 46 * 10**6),
        name="parent_top",
    )(leaf_basis, transfer, far_basis, far_transfer)


def parent_low(transfer, leaf_work, halves):
    count, rank, columns = transfer.shape
    half = columns // 2
    return pl.pallas_call(
        parent_low_kernel,
        out_shape=jax.ShapeDtypeStruct(transfer.shape, jnp.float32),
        scratch_shapes=[
            pltpu.VMEM((count * half, half), jnp.float32),
            pltpu.VMEM((count, half, half), jnp.float32),
        ],
        compiler_params=params(),
        cost_estimate=cost(10**9, 40 * 10**6),
        name="parent_low",
    )(leaf_work, *halves)


def quotient(value, size):
    return value >> (size.bit_length() - 1) if size & (size - 1) == 0 else lax.div(value, size)


def remainder(value, size):
    return value & (size - 1) if size & (size - 1) == 0 else lax.rem(value, size)


def shift(value, axis, d):
    pairs = [(index ^ d, index) for index in range(lax.axis_size(axis))]
    return lax.ppermute(value, axis, pairs)


def joined(values, bit):
    return jnp.concatenate([values, shift(values, "clus", bit)], axis=0)


def in_order(table):
    return [table[d] for d in range(len(table))]


def points_split(points):
    first = points * FIRST // 16
    return (slice(0, first), slice(first, points))


def pick(table, leaf, span, store):
    count = table[0].shape[0]
    place = quotient(leaf, count) ^ lax.axis_index("blk")
    for d in range(len(table)):

        @pl.when(place == d)
        def _():
            rows = span if table[d].shape[1] > span.stop - span.start else slice(None)
            store(table[d][remainder(leaf, count), rows, :])


def serve_kernel(size, span, asked, *refs):
    table, outs = refs[:size], refs[size:]
    me = lax.axis_index("clus")
    leaves = size * table[0].shape[0]
    for d in range(1, asked.shape[0]):

        def place(b, position, d=d):
            code = asked[d, b]
            mine = quotient(code, leaves) == me

            @pl.when(mine)
            def _():
                def store(value):
                    outs[d - 1][position] = value

                pick(table, remainder(code, leaves), span, store)

            return position + mine.astype(jnp.int32)

        lax.fori_loop(0, asked.shape[1], place, jnp.int32(0))


def serve(asked, table, span, capacity):
    groups, size = asked.shape[0], len(table)
    smem, vmem = pl.BlockSpec(memory_space=pltpu.SMEM), pl.BlockSpec(memory_space=pltpu.VMEM)
    shape = (capacity, span.stop - span.start, table[0].shape[2])
    return pl.pallas_call(
        functools.partial(serve_kernel, size, span),
        in_specs=[smem] + [vmem] * size,
        out_specs=[vmem] * (groups - 1),
        out_shape=[jax.ShapeDtypeStruct(shape, table[0].dtype)] * (groups - 1),
        compiler_params=params(),
        cost_estimate=cost(10**9, 6 * 10**6),
        name="serve",
    )(asked, *table)


def near_kernel(size, leaf, slabs, *refs):
    table, (factors, out, held) = refs[:-3], refs[-3:]
    count, width, points = factors.shape
    spans = points_split(points)

    def gather(b, carry):
        for c in range(len(spans)):

            def store(value, c=c):
                held[b, spans[c], :] = value

            pick(table[c * size : (c + 1) * size], leaf[b], spans[c], store)
        return carry

    lax.fori_loop(0, count, gather, 0)
    row = lax.broadcasted_iota(jnp.int32, (width, out.shape[1]), 0)
    for b in range(count):
        value = dot(factors[b], held[b], NN)
        value = jnp.where(row < slabs[b] * SLAB, value, 0.0)
        out[b] = value.T.astype(out.dtype)


def near_stage(row_leaf, rank_slabs, tables, factors):
    count, width, points = factors.shape
    size, rank = len(tables[0]), tables[0][0].shape[2]
    smem, vmem = pl.BlockSpec(memory_space=pltpu.SMEM), pl.BlockSpec(memory_space=pltpu.VMEM)
    flat = [piece for table in tables for piece in table]
    return pl.pallas_call(
        functools.partial(near_kernel, size),
        in_specs=[smem, smem] + [vmem] * len(flat) + [vmem],
        out_specs=vmem,
        out_shape=jax.ShapeDtypeStruct((count, rank, width), jnp.bfloat16),
        scratch_shapes=[pltpu.VMEM((count, points, rank), flat[0].dtype)],
        compiler_params=params(),
        cost_estimate=cost(10**9, 10 * 10**6),
        name="near",
    )(row_leaf, rank_slabs, *flat, factors)


def far_kernel(groups, size, chunks, code, slabs, near, *refs):
    table, refs = refs[: chunks * size], refs[chunks * size :]
    fetched, (factors, out, held, tally) = refs[: chunks * (groups - 1)], refs[chunks * (groups - 1) :]
    count, width, points = factors.shape
    leaves = size * table[0].shape[0]
    spans = points_split(points)
    me = lax.axis_index("clus")
    for g in range(groups):
        tally[g] = 0

    def gather(b, carry):
        group, leaf = quotient(code[b], leaves), remainder(code[b], leaves)
        position = tally[group]
        tally[group] = position + 1
        away = group ^ me

        @pl.when(away == 0)
        def _():
            for c in range(chunks):

                def store(value, c=c):
                    held[b, spans[c], :] = value

                pick(table[c * size : (c + 1) * size], leaf, spans[c], store)

        for d in range(1, groups):

            @pl.when(away == d)
            def _(d=d):
                for c in range(chunks):
                    piece = fetched[c * (groups - 1) + d - 1]
                    held[b, spans[c], :] = piece[position]

        return carry

    lax.fori_loop(0, count, gather, 0)
    row = lax.broadcasted_iota(jnp.int32, (width, near.shape[1]), 0)
    for first in range(0, count, AHEAD):
        values = [dot(factors[b], held[b], NN) for b in range(first, first + AHEAD)]
        for b in range(first, first + AHEAD):
            value = jnp.where(row < slabs[b] * SLAB, values[b - first], 0.0).astype(near.dtype)
            out[b] = dot(near[b], value, NN)


def far_stage(code, rank_slabs, near, tables, fetched, factors):
    count, width, points = factors.shape
    size, rank = len(tables[0]), tables[0][0].shape[2]
    groups = len(fetched[0]) + 1
    smem, vmem = pl.BlockSpec(memory_space=pltpu.SMEM), pl.BlockSpec(memory_space=pltpu.VMEM)
    flat = [piece for table in tables for piece in table] + [piece for part in fetched for piece in part]
    return pl.pallas_call(
        functools.partial(far_kernel, groups, size, len(tables)),
        in_specs=[smem, smem, vmem] + [vmem] * len(flat) + [vmem],
        out_specs=vmem,
        out_shape=jax.ShapeDtypeStruct((count, rank, rank), jnp.float32),
        scratch_shapes=[
            pltpu.VMEM((count, points, rank), flat[0].dtype),
            pltpu.SMEM((groups,), jnp.int32),
        ],
        compiler_params=params(),
        cost_estimate=cost(10**9, 13 * 10**6),
        name="far",
    )(code, rank_slabs, near, *flat, factors)


def per_device(
    leaf_basis, transfer, block_rows, block_cols, rank_slabs, row_leaf, col_group, col_leaf
):
    groups, size = lax.axis_size("clus"), lax.axis_size("blk")
    capacity = max(2, 2 * block_rows.shape[0] // groups)
    spans = points_split(leaf_basis.shape[1])
    barrier = lax.optimization_barrier
    far_basis = shift(leaf_basis, "blk", 1)
    far_transfer = shift(transfer, "blk", 1)
    code, rows, first, second, leaf_work = leaf_stage(
        leaf_basis, leaf_basis.shape[0] * size, col_group[:, 0], col_leaf
    )
    code, rows, first, second, far_basis, far_transfer = barrier(
        (code, rows, first, second, far_basis, far_transfer)
    )
    chips = range(4, size, 2)
    table = {d: shift(first, "blk", d) for d in reversed(chips)}
    close = {0: rows, 1: shift(rows, "blk", 1), 2: shift(rows, "blk", 2)}
    asked = joined(code[None], 1)
    halves = parent_top(leaf_basis, transfer, far_basis, far_transfer)
    asked, close, second, halves = barrier((asked, close, second, halves))
    later = {d: shift(second, "blk", d) for d in reversed(chips)}
    bit = 2
    while bit < groups:
        asked = joined(asked, bit)
        bit *= 2
    transfer_new = parent_low(transfer, leaf_work, halves)
    table, close, asked, transfer_new = barrier((table, close, asked, transfer_new))
    for d in chips:
        table[d + 1] = shift(table[d], "blk", 1)
    close[3] = shift(close[2], "blk", 1)
    served = serve(asked, in_order(close | table), spans[0], capacity)
    fetched = [[shift(value, "clus", d + 1) for d, value in enumerate(served)]]
    for d in chips:
        later[d + 1] = shift(later[d], "blk", 1)
    later, fetched[0] = barrier((later, fetched[0]))
    served = serve(asked, in_order(close | later), spans[1], capacity)
    fetched.append([shift(value, "clus", d + 1) for d, value in enumerate(served)])
    tables = [in_order(close | table), in_order(close | later)]
    near = near_stage(row_leaf, rank_slabs, tables, jnp.swapaxes(block_rows, 1, 2))
    coupling = far_stage(asked[0], rank_slabs, near, tables, fetched, jnp.swapaxes(block_cols, 1, 2))
    return (coupling, transfer_new)


def solution(mesh):
    placed = (
        P(("clus", "blk"), None, None),
        P(("clus", "blk"), None, None),
        P(("clus", "blk"), None, None),
        P(("clus", "blk"), None, None),
        P(("clus", "blk")),
        P(("clus", "blk")),
        P(("clus", "blk"), None),
        P(("clus", "blk")),
    )
    return jax.shard_map(
        per_device,
        mesh=mesh,
        in_specs=placed,
        out_specs=(P(("clus", "blk"), None, None), P(("clus", "blk"), None, None)),
        check_vma=False,
    )
```

```python
import functools

import jax
import jax.numpy as jnp
from jax import lax
from jax.experimental import pallas as pl
from jax.experimental.pallas import tpu as pltpu
from jax.sharding import PartitionSpec as P

SLAB = 64
PANEL = 8
STRIP = 32
FIRST = 10
AHEAD = 4
VMEM_LIMIT = 24 * 1024 * 1024

NN = (((1,), (0,)), ((), ()))
NT = (((1,), (1,)), ((), ()))
TN = (((0,), (0,)), ((), ()))


def params():
    return pltpu.CompilerParams(vmem_limit_bytes=VMEM_LIMIT)


def cost(flops, moved):
    return pl.CostEstimate(flops=flops, bytes_accessed=moved, transcendentals=0)


def dot(left, right, dims):
    return lax.dot_general(left, right, dims, preferred_element_type=jnp.float32)


def split(value):
    high = value.astype(jnp.bfloat16)
    low = (value - high.astype(jnp.float32)).astype(jnp.bfloat16)
    return high, low


def dot_split(left, right, dims):
    (lh, ll), (rh, rl) = left, right
    return dot(lh, rh, dims) + (dot(lh, rl, dims) + dot(ll, rh, dims))


def lower_part(value):
    rows = lax.broadcasted_iota(jnp.int32, value.shape, 0)
    cols = lax.broadcasted_iota(jnp.int32, value.shape, 1)
    return jnp.where(cols <= rows, value, 0.0)


def factor(work, batch, size):
    lane = lax.broadcasted_iota(jnp.int32, (batch, size), 1)

    def spread(row, column):
        return jnp.broadcast_to(row[:, column : column + 1], (batch, size))

    for top in range(0, size, STRIP):
        rows = [work[pl.ds(top + i, batch, stride=size), :] for i in range(STRIP)]
        for q in range(0, STRIP, PANEL):
            first = top + q
            inside = (lane >= first) & (lane < first + PANEL)
            diag = {
                (i, j): spread(rows[q + i], first + j) for i in range(PANEL) for j in range(i, PANEL)
            }
            scale, upper = [], {}
            for k in range(PANEL):
                inv = lax.rsqrt(diag[k, k])
                scale.append(inv)
                for j in range(k + 1, PANEL):
                    upper[k, j] = diag[k, j] * inv
                for i in range(k + 1, PANEL):
                    for j in range(i, PANEL):
                        diag[i, j] = diag[i, j] - upper[k, i] * upper[k, j]
            done = []
            for k in range(PANEL):
                row = jnp.where(inside, jnp.where(lane == first + k, 1.0, 0.0), rows[q + k])
                for m in range(k):
                    row = row - upper[m, k] * done[m]
                done.append(row * scale[k])
            rows[q : q + PANEL] = done
            for i in range(q + PANEL, STRIP):
                row = jnp.where(inside, 0.0, rows[i])
                for k in range(PANEL):
                    row = row - spread(done[k], top + i) * done[k]
                rows[i] = row
        for i in range(STRIP):
            work[pl.ds(top + i, batch, stride=size), :] = rows[i]
        below = top + STRIP
        if below < size:
            for b in range(batch):
                strip = work[b * size + top : b * size + below, :]
                row = lax.broadcasted_iota(jnp.int32, strip.shape, 0) + top
                column = lax.broadcasted_iota(jnp.int32, strip.shape, 1)
                keep = (column <= row) | (column >= below)
                high, low = split(strip)
                left = jnp.concatenate([high, high, low], axis=0)
                high, low = split(jnp.where(keep, strip, 0.0))
                right = jnp.concatenate([high, low, high], axis=0)
                rest = work[b * size + below : (b + 1) * size, :]
                column = lax.broadcasted_iota(jnp.int32, rest.shape, 1)
                rest = jnp.where((column >= top) & (column < below), 0.0, rest)
                work[b * size + below : (b + 1) * size, :] = rest - dot(left, right, TN)[below:]


def leaf_kernel(leaves, group, leaf_of, basis, code, rows_out, *rest):
    pieces, work = rest[:-1], rest[-1]
    count, points, rank = basis.shape

    def pack(b, carry):
        code[b] = group[b] * leaves + leaf_of[b]
        return carry

    lax.fori_loop(0, code.shape[0], pack, 0)
    for b in range(count):
        leaf = basis[b]
        work[b * rank : (b + 1) * rank, :] = dot(leaf, leaf, TN)
    factor(work, count, rank)
    for b in range(count):
        high, low = split(lower_part(work[b * rank : (b + 1) * rank, :]))
        leaf = basis[b]
        value = (dot(leaf, high, NT) + dot(leaf, low, NT)).astype(rows_out.dtype)
        rows_out[b] = value
        for span, piece in zip(points_split(points), pieces):
            piece[b] = value[span]


def parent_top_kernel(own_basis, own_transfer, far_basis, far_transfer, weighted, top, cross, corner):
    count, points, rank = own_basis.shape
    half = own_transfer.shape[2] // 2
    for j in range(count):
        other = (j + count // 2) % count
        total = None
        for basis, transfer, c in ((own_basis, own_transfer, j), (far_basis, far_transfer, other)):
            leaf = basis[c]
            gram = split(dot(leaf, leaf, TN))
            value = transfer[c]
            moved = dot_split(gram, split(value), NN)
            if basis is own_basis:
                weighted[c] = moved
            left, right = split(value[:, :half]), split(value[:, half:])
            moved_left, moved_right = split(moved[:, :half]), split(moved[:, half:])
            parts = (
                dot_split(left, moved_left, TN),
                dot_split(right, moved_left, TN),
                dot_split(right, moved_right, TN),
            )
            total = parts if total is None else tuple(a + b for a, b in zip(total, parts))
        top[j * half : (j + 1) * half, :] = total[0]
        cross[j] = total[1]
        corner[j] = total[2]
    factor(top, count, half)


def parent_low_kernel(leaf_work, weighted, top, cross, corner, out, work, coupled):
    count, rank, columns = weighted.shape
    half = columns // 2
    for j in range(count):
        inverse = split(lower_part(top[j * half : (j + 1) * half, :]))
        lower = dot_split(split(cross[j]), inverse, NT)
        coupled[j] = lower
        lower = split(lower)
        work[j * half : (j + 1) * half, :] = corner[j] - dot_split(lower, lower, NT)
    factor(work, count, half)
    for j in range(count):
        leaf_inverse = split(lower_part(leaf_work[j * rank : (j + 1) * rank, :]))
        stacked = dot_split(leaf_inverse, split(weighted[j]), NN)
        inverse = split(lower_part(top[j * half : (j + 1) * half, :]))
        first = dot_split(split(stacked[:, :half]), inverse, NT)
        rest = stacked[:, half:] - dot_split(split(first), split(coupled[j]), NT)
        inverse = split(lower_part(work[j * half : (j + 1) * half, :]))
        out[j, :, :half] = first
        out[j, :, half:] = dot_split(split(rest), inverse, NT)


def leaf_stage(leaf_basis, leaves, group, leaf_of):
    count, points, rank = leaf_basis.shape
    smem, vmem = pl.BlockSpec(memory_space=pltpu.SMEM), pl.BlockSpec(memory_space=pltpu.VMEM)
    parts = [points] + [span.stop - span.start for span in points_split(points)]
    return pl.pallas_call(
        functools.partial(leaf_kernel, leaves),
        in_specs=[smem, smem, vmem],
        out_specs=[smem] + [vmem] * (len(parts) + 1),
        out_shape=[jax.ShapeDtypeStruct(leaf_of.shape, jnp.int32)]
        + [jax.ShapeDtypeStruct((count, part, rank), jnp.bfloat16) for part in parts]
        + [jax.ShapeDtypeStruct((count * rank, rank), jnp.float32)],
        compiler_params=params(),
        cost_estimate=cost(10**9, 25 * 10**6),
        name="leaf_factor",
    )(group, leaf_of, leaf_basis)


def parent_top(leaf_basis, transfer, far_basis, far_transfer):
    count, points, rank = leaf_basis.shape
    half = transfer.shape[2] // 2
    square = jax.ShapeDtypeStruct((count, half, half), jnp.float32)
    return pl.pallas_call(
        parent_top_kernel,
        out_shape=(
            jax.ShapeDtypeStruct(transfer.shape, jnp.float32),
            jax.ShapeDtypeStruct((count * half, half), jnp.float32),
            square,
            square,
        ),
        compiler_params=params(),
        cost_estimate=cost(10**9, 46 * 10**6),
        name="parent_top",
    )(leaf_basis, transfer, far_basis, far_transfer)


def parent_low(transfer, leaf_work, halves):
    count, rank, columns = transfer.shape
    half = columns // 2
    return pl.pallas_call(
        parent_low_kernel,
        out_shape=jax.ShapeDtypeStruct(transfer.shape, jnp.float32),
        scratch_shapes=[
            pltpu.VMEM((count * half, half), jnp.float32),
            pltpu.VMEM((count, half, half), jnp.float32),
        ],
        compiler_params=params(),
        cost_estimate=cost(10**9, 40 * 10**6),
        name="parent_low",
    )(leaf_work, *halves)


def quotient(value, size):
    return value >> (size.bit_length() - 1) if size & (size - 1) == 0 else lax.div(value, size)


def remainder(value, size):
    return value & (size - 1) if size & (size - 1) == 0 else lax.rem(value, size)


def shift(value, axis, d):
    pairs = [(index ^ d, index) for index in range(lax.axis_size(axis))]
    return lax.ppermute(value, axis, pairs)


def joined(values, bit):
    return jnp.concatenate([values, shift(values, "clus", bit)], axis=0)


def in_order(table):
    return [table[d] for d in range(len(table))]


def points_split(points):
    first = points * FIRST // 16
    return (slice(0, first), slice(first, points))


def pick(table, leaf, span, store):
    count = table[0].shape[0]
    place = quotient(leaf, count) ^ lax.axis_index("blk")
    for d in range(len(table)):

        @pl.when(place == d)
        def _():
            rows = span if table[d].shape[1] > span.stop - span.start else slice(None)
            store(table[d][remainder(leaf, count), rows, :])


def serve_kernel(size, span, asked, *refs):
    table, outs = refs[:size], refs[size:]
    me = lax.axis_index("clus")
    leaves = size * table[0].shape[0]
    for d in range(1, asked.shape[0]):

        def place(b, position, d=d):
            code = asked[d, b]
            mine = quotient(code, leaves) == me

            @pl.when(mine)
            def _():
                def store(value):
                    outs[d - 1][position] = value

                pick(table, remainder(code, leaves), span, store)

            return position + mine.astype(jnp.int32)

        lax.fori_loop(0, asked.shape[1], place, jnp.int32(0))


def serve(asked, table, span, capacity):
    groups, size = asked.shape[0], len(table)
    smem, vmem = pl.BlockSpec(memory_space=pltpu.SMEM), pl.BlockSpec(memory_space=pltpu.VMEM)
    shape = (capacity, span.stop - span.start, table[0].shape[2])
    return pl.pallas_call(
        functools.partial(serve_kernel, size, span),
        in_specs=[smem] + [vmem] * size,
        out_specs=[vmem] * (groups - 1),
        out_shape=[jax.ShapeDtypeStruct(shape, table[0].dtype)] * (groups - 1),
        compiler_params=params(),
        cost_estimate=cost(10**9, 6 * 10**6),
        name="serve",
    )(asked, *table)


def near_kernel(size, leaf, slabs, *refs):
    table, (factors, out, held) = refs[:-3], refs[-3:]
    count, width, points = factors.shape
    spans = points_split(points)

    def gather(b, carry):
        for c in range(len(spans)):

            def store(value, c=c):
                held[b, spans[c], :] = value

            pick(table[c * size : (c + 1) * size], leaf[b], spans[c], store)
        return carry

    lax.fori_loop(0, count, gather, 0)
    row = lax.broadcasted_iota(jnp.int32, (width, out.shape[1]), 0)
    for b in range(count):
        value = dot(factors[b], held[b], NN)
        value = jnp.where(row < slabs[b] * SLAB, value, 0.0)
        out[b] = value.T.astype(out.dtype)


def near_stage(row_leaf, rank_slabs, tables, factors):
    count, width, points = factors.shape
    size, rank = len(tables[0]), tables[0][0].shape[2]
    smem, vmem = pl.BlockSpec(memory_space=pltpu.SMEM), pl.BlockSpec(memory_space=pltpu.VMEM)
    flat = [piece for table in tables for piece in table]
    return pl.pallas_call(
        functools.partial(near_kernel, size),
        in_specs=[smem, smem] + [vmem] * len(flat) + [vmem],
        out_specs=vmem,
        out_shape=jax.ShapeDtypeStruct((count, rank, width), jnp.bfloat16),
        scratch_shapes=[pltpu.VMEM((count, points, rank), flat[0].dtype)],
        compiler_params=params(),
        cost_estimate=cost(10**9, 10 * 10**6),
        name="near",
    )(row_leaf, rank_slabs, *flat, factors)


def far_kernel(groups, size, chunks, code, slabs, near, *refs):
    table, refs = refs[: chunks * size], refs[chunks * size :]
    fetched, (factors, out, held, tally) = refs[: chunks * (groups - 1)], refs[chunks * (groups - 1) :]
    count, width, points = factors.shape
    leaves = size * table[0].shape[0]
    spans = points_split(points)
    me = lax.axis_index("clus")
    for g in range(groups):
        tally[g] = 0

    def gather(b, carry):
        group, leaf = quotient(code[b], leaves), remainder(code[b], leaves)
        position = tally[group]
        tally[group] = position + 1
        away = group ^ me

        @pl.when(away == 0)
        def _():
            for c in range(chunks):

                def store(value, c=c):
                    held[b, spans[c], :] = value

                pick(table[c * size : (c + 1) * size], leaf, spans[c], store)

        for d in range(1, groups):

            @pl.when(away == d)
            def _(d=d):
                for c in range(chunks):
                    piece = fetched[c * (groups - 1) + d - 1]
                    held[b, spans[c], :] = piece[position]

        return carry

    lax.fori_loop(0, count, gather, 0)
    row = lax.broadcasted_iota(jnp.int32, (width, near.shape[1]), 0)
    for first in range(0, count, AHEAD):
        values = [dot(factors[b], held[b], NN) for b in range(first, first + AHEAD)]
        for b in range(first, first + AHEAD):
            value = jnp.where(row < slabs[b] * SLAB, values[b - first], 0.0).astype(near.dtype)
            out[b] = dot(near[b], value, NN)


def far_stage(code, rank_slabs, near, tables, fetched, factors):
    count, width, points = factors.shape
    size, rank = len(tables[0]), tables[0][0].shape[2]
    groups = len(fetched[0]) + 1
    smem, vmem = pl.BlockSpec(memory_space=pltpu.SMEM), pl.BlockSpec(memory_space=pltpu.VMEM)
    flat = [piece for table in tables for piece in table] + [piece for part in fetched for piece in part]
    return pl.pallas_call(
        functools.partial(far_kernel, groups, size, len(tables)),
        in_specs=[smem, smem, vmem] + [vmem] * len(flat) + [vmem],
        out_specs=vmem,
        out_shape=jax.ShapeDtypeStruct((count, rank, rank), jnp.float32),
        scratch_shapes=[
            pltpu.VMEM((count, points, rank), flat[0].dtype),
            pltpu.SMEM((groups,), jnp.int32),
        ],
        compiler_params=params(),
        cost_estimate=cost(10**9, 13 * 10**6),
        name="far",
    )(code, rank_slabs, near, *flat, factors)


def per_device(
    leaf_basis, transfer, block_rows, block_cols, rank_slabs, row_leaf, col_group, col_leaf
):
    groups, size = lax.axis_size("clus"), lax.axis_size("blk")
    capacity = max(2, 2 * block_rows.shape[0] // groups)
    spans = points_split(leaf_basis.shape[1])
    barrier = lax.optimization_barrier
    far_basis = shift(leaf_basis, "blk", 1)
    far_transfer = shift(transfer, "blk", 1)
    code, rows, first, second, leaf_work = leaf_stage(
        leaf_basis, leaf_basis.shape[0] * size, col_group[:, 0], col_leaf
    )
    code, rows, first, second, far_basis, far_transfer = barrier(
        (code, rows, first, second, far_basis, far_transfer)
    )
    chips = range(4, size, 2)
    table = {d: shift(first, "blk", d) for d in reversed(chips)}
    close = {0: rows, 1: shift(rows, "blk", 1), 2: shift(rows, "blk", 2)}
    asked = joined(code[None], 1)
    halves = parent_top(leaf_basis, transfer, far_basis, far_transfer)
    asked, close[1], second, halves = barrier((asked, close[1], second, halves))
    later = {d: shift(second, "blk", d) for d in reversed(chips)}
    bit = 2
    while bit < groups:
        asked = joined(asked, bit)
        bit *= 2
    transfer_new = parent_low(transfer, leaf_work, halves)
    table, close, asked, transfer_new = barrier((table, close, asked, transfer_new))
    for d in chips:
        table[d + 1] = shift(table[d], "blk", 1)
    close[3] = shift(close[2], "blk", 1)
    served = serve(asked, in_order(close | table), spans[0], capacity)
    fetched = [[shift(value, "clus", d + 1) for d, value in enumerate(served)]]
    for d in chips:
        later[d + 1] = shift(later[d], "blk", 1)
    later, fetched[0] = barrier((later, fetched[0]))
    served = serve(asked, in_order(close | later), spans[1], capacity)
    fetched.append([shift(value, "clus", d + 1) for d, value in enumerate(served)])
    tables = [in_order(close | table), in_order(close | later)]
    near = near_stage(row_leaf, rank_slabs, tables, jnp.swapaxes(block_rows, 1, 2))
    coupling = far_stage(asked[0], rank_slabs, near, tables, fetched, jnp.swapaxes(block_cols, 1, 2))
    return (coupling, transfer_new)


def solution(mesh):
    placed = (
        P(("clus", "blk"), None, None),
        P(("clus", "blk"), None, None),
        P(("clus", "blk"), None, None),
        P(("clus", "blk"), None, None),
        P(("clus", "blk")),
        P(("clus", "blk")),
        P(("clus", "blk"), None),
        P(("clus", "blk")),
    )
    return jax.shard_map(
        per_device,
        mesh=mesh,
        in_specs=placed,
        out_specs=(P(("clus", "blk"), None, None), P(("clus", "blk"), None, None)),
        check_vma=False,
    )
```

```python
import functools

import jax
import jax.numpy as jnp
from jax import lax
from jax.experimental import pallas as pl
from jax.experimental.pallas import tpu as pltpu
from jax.sharding import PartitionSpec as P

SLAB = 64
PANEL = 8
STRIP = 32
FIRST = 9
AHEAD = 4
VMEM_LIMIT = 24 * 1024 * 1024

NN = (((1,), (0,)), ((), ()))
NT = (((1,), (1,)), ((), ()))
TN = (((0,), (0,)), ((), ()))


def params():
    return pltpu.CompilerParams(vmem_limit_bytes=VMEM_LIMIT)


def cost(flops, moved):
    return pl.CostEstimate(flops=flops, bytes_accessed=moved, transcendentals=0)


def dot(left, right, dims):
    return lax.dot_general(left, right, dims, preferred_element_type=jnp.float32)


def split(value):
    high = value.astype(jnp.bfloat16)
    low = (value - high.astype(jnp.float32)).astype(jnp.bfloat16)
    return high, low


def dot_split(left, right, dims):
    (lh, ll), (rh, rl) = left, right
    return dot(lh, rh, dims) + (dot(lh, rl, dims) + dot(ll, rh, dims))


def lower_part(value):
    rows = lax.broadcasted_iota(jnp.int32, value.shape, 0)
    cols = lax.broadcasted_iota(jnp.int32, value.shape, 1)
    return jnp.where(cols <= rows, value, 0.0)


def factor(work, batch, size):
    lane = lax.broadcasted_iota(jnp.int32, (batch, size), 1)

    def spread(row, column):
        return jnp.broadcast_to(row[:, column : column + 1], (batch, size))

    for top in range(0, size, STRIP):
        rows = [work[pl.ds(top + i, batch, stride=size), :] for i in range(STRIP)]
        for q in range(0, STRIP, PANEL):
            first = top + q
            inside = (lane >= first) & (lane < first + PANEL)
            diag = {
                (i, j): spread(rows[q + i], first + j) for i in range(PANEL) for j in range(i, PANEL)
            }
            scale, upper = [], {}
            for k in range(PANEL):
                inv = lax.rsqrt(diag[k, k])
                scale.append(inv)
                for j in range(k + 1, PANEL):
                    upper[k, j] = diag[k, j] * inv
                for i in range(k + 1, PANEL):
                    for j in range(i, PANEL):
                        diag[i, j] = diag[i, j] - upper[k, i] * upper[k, j]
            done = []
            for k in range(PANEL):
                row = jnp.where(inside, jnp.where(lane == first + k, 1.0, 0.0), rows[q + k])
                for m in range(k):
                    row = row - upper[m, k] * done[m]
                done.append(row * scale[k])
            rows[q : q + PANEL] = done
            for i in range(q + PANEL, STRIP):
                row = jnp.where(inside, 0.0, rows[i])
                for k in range(PANEL):
                    row = row - spread(done[k], top + i) * done[k]
                rows[i] = row
        for i in range(STRIP):
            work[pl.ds(top + i, batch, stride=size), :] = rows[i]
        below = top + STRIP
        if below < size:
            for b in range(batch):
                strip = work[b * size + top : b * size + below, :]
                row = lax.broadcasted_iota(jnp.int32, strip.shape, 0) + top
                column = lax.broadcasted_iota(jnp.int32, strip.shape, 1)
                keep = (column <= row) | (column >= below)
                high, low = split(strip)
                left = jnp.concatenate([high, high, low], axis=0)
                high, low = split(jnp.where(keep, strip, 0.0))
                right = jnp.concatenate([high, low, high], axis=0)
                rest = work[b * size + below : (b + 1) * size, :]
                column = lax.broadcasted_iota(jnp.int32, rest.shape, 1)
                rest = jnp.where((column >= top) & (column < below), 0.0, rest)
                work[b * size + below : (b + 1) * size, :] = rest - dot(left, right, TN)[below:]


def leaf_kernel(basis, rows_out, kept_out, *rest):
    pieces, work = rest[:-1], rest[-1]
    count, points, rank = basis.shape
    for b in range(count):
        leaf = basis[b]
        work[b * rank : (b + 1) * rank, :] = dot(leaf, leaf, TN)
    factor(work, count, rank)
    for b in range(count):
        value = orthonormal(work[b * rank : (b + 1) * rank, :], basis[b]).astype(rows_out.dtype)
        rows_out[b] = value
        if b < kept_out.shape[0]:
            kept_out[b] = value
            for span, piece in zip(points_split(points), pieces):
                piece[b] = value[span]


def orthonormal(factored, leaf):
    high, low = split(lower_part(factored))
    return dot(leaf, high, NT) + dot(leaf, low, NT)


def extra_bases(batch, bases, rows, out, work):
    early, points, rank = bases[0].shape
    row = lax.broadcasted_iota(jnp.int32, (rank, rank), 0)
    column = lax.broadcasted_iota(jnp.int32, (rank, rank), 1)
    held = rows.shape[0]
    for b in range(held):
        out[b] = rows[b]
    for first in range(0, out.shape[0] - held, batch):
        last = min(first + batch, out.shape[0] - held)
        leaves = [bases[n // early][n % early] for n in range(first, last)]
        for b in range(batch):
            gram = dot(leaves[b], leaves[b], TN) if b < len(leaves) else jnp.where(row == column, 1.0, 0.0)
            work[b * rank : (b + 1) * rank, :] = gram
        factor(work, batch, rank)
        for b, leaf in enumerate(leaves):
            value = orthonormal(work[b * rank : (b + 1) * rank, :], leaf)
            out[held + first + b] = value.astype(out.dtype)


def parent_top_kernel(own_basis, own_transfer, far_basis, far_transfer, rows, *refs):
    bases, (weighted, top, cross, corner, combined, work) = refs[:-6], refs[-6:]
    count, points, rank = own_basis.shape
    half = own_transfer.shape[2] // 2
    extra_bases(count, bases, rows, combined, work)
    for j in range(count):
        other = (j + count // 2) % count
        total = None
        for basis, transfer, c in ((own_basis, own_transfer, j), (far_basis, far_transfer, other)):
            leaf = basis[c]
            gram = split(dot(leaf, leaf, TN))
            value = transfer[c]
            moved = dot_split(gram, split(value), NN)
            if basis is own_basis:
                weighted[c] = moved
            left, right = split(value[:, :half]), split(value[:, half:])
            moved_left, moved_right = split(moved[:, :half]), split(moved[:, half:])
            parts = (
                dot_split(left, moved_left, TN),
                dot_split(right, moved_left, TN),
                dot_split(right, moved_right, TN),
            )
            total = parts if total is None else tuple(a + b for a, b in zip(total, parts))
        top[j * half : (j + 1) * half, :] = total[0]
        cross[j] = total[1]
        corner[j] = total[2]
    factor(top, count, half)


def parent_low_kernel(leaf_work, weighted, top, cross, corner, out, work, coupled):
    count, rank, columns = weighted.shape
    half = columns // 2
    for j in range(count):
        inverse = split(lower_part(top[j * half : (j + 1) * half, :]))
        lower = dot_split(split(cross[j]), inverse, NT)
        coupled[j] = lower
        lower = split(lower)
        work[j * half : (j + 1) * half, :] = corner[j] - dot_split(lower, lower, NT)
    factor(work, count, half)
    for j in range(count):
        leaf_inverse = split(lower_part(leaf_work[j * rank : (j + 1) * rank, :]))
        stacked = dot_split(leaf_inverse, split(weighted[j]), NN)
        inverse = split(lower_part(top[j * half : (j + 1) * half, :]))
        first = dot_split(split(stacked[:, :half]), inverse, NT)
        rest = stacked[:, half:] - dot_split(split(first), split(coupled[j]), NT)
        inverse = split(lower_part(work[j * half : (j + 1) * half, :]))
        out[j, :, :half] = first
        out[j, :, half:] = dot_split(split(rest), inverse, NT)


def leaf_stage(leaf_basis, kept):
    count, points, rank = leaf_basis.shape
    shapes = [(count, points), (kept, points)]
    shapes += [(kept, span.stop - span.start) for span in points_split(points)]
    return pl.pallas_call(
        leaf_kernel,
        out_shape=[jax.ShapeDtypeStruct(shape + (rank,), jnp.bfloat16) for shape in shapes]
        + [jax.ShapeDtypeStruct((count * rank, rank), jnp.float32)],
        compiler_params=params(),
        cost_estimate=cost(10**9, 25 * 10**6),
        name="leaf_factor",
    )(leaf_basis)


def parent_top(leaf_basis, transfer, far_basis, far_transfer, rows, raw):
    count, points, rank = leaf_basis.shape
    half = transfer.shape[2] // 2
    square = jax.ShapeDtypeStruct((count, half, half), jnp.float32)
    combined = (count + len(raw) * raw[0].shape[0], points, rank)
    return pl.pallas_call(
        parent_top_kernel,
        out_shape=(
            jax.ShapeDtypeStruct(transfer.shape, jnp.float32),
            jax.ShapeDtypeStruct((count * half, half), jnp.float32),
            square,
            square,
            jax.ShapeDtypeStruct(combined, jnp.bfloat16),
        ),
        scratch_shapes=[pltpu.VMEM((count * rank, rank), jnp.float32)],
        compiler_params=params(),
        cost_estimate=cost(10**9, 70 * 10**6),
        name="parent_top",
    )(leaf_basis, transfer, far_basis, far_transfer, rows, *raw)


def parent_low(transfer, leaf_work, halves):
    count, rank, columns = transfer.shape
    half = columns // 2
    return pl.pallas_call(
        parent_low_kernel,
        out_shape=jax.ShapeDtypeStruct(transfer.shape, jnp.float32),
        scratch_shapes=[
            pltpu.VMEM((count * half, half), jnp.float32),
            pltpu.VMEM((count, half, half), jnp.float32),
        ],
        compiler_params=params(),
        cost_estimate=cost(10**9, 40 * 10**6),
        name="parent_low",
    )(leaf_work, *halves)


def quotient(value, size):
    return value >> (size.bit_length() - 1) if size & (size - 1) == 0 else lax.div(value, size)


def remainder(value, size):
    return value & (size - 1) if size & (size - 1) == 0 else lax.rem(value, size)


def shift(value, axis, d):
    pairs = [(index ^ d, index) for index in range(lax.axis_size(axis))]
    return lax.ppermute(value, axis, pairs)


def early_of(count):
    return count // 4


def joined(values, bit):
    return jnp.concatenate([values, shift(values, "clus", bit)], axis=0)


def in_order(table):
    return [table[d] for d in range(len(table))]


def points_split(points):
    first = points * FIRST // 16
    return (slice(0, first), slice(first, points))


def pick(table, leaf, span, store):
    size, kept = len(table), table[2].shape[0]
    early = (table[0].shape[0] - kept) // (size // 2)
    count = kept + early
    place = quotient(leaf, count) ^ lax.axis_index("blk")
    local = remainder(leaf, count)
    here = (place < 2) | (local >= kept)
    index = jnp.where(place < 2, local, count + ((place >> 1) - 1) * early + local - kept)
    for d in range(size):

        @pl.when((here & (place & 1 == d)) if d < 2 else (jnp.logical_not(here) & (place == d)))
        def _():
            rows = span if table[d].shape[1] > span.stop - span.start else slice(None)
            store(table[d][index if d < 2 else local, rows, :])


def leaves_of(table):
    size, kept = len(table), table[2].shape[0]
    return size * (kept + (table[0].shape[0] - kept) // (size // 2))


def serve_kernel(size, span, asked, *refs):
    table, outs = refs[:size], refs[size:]
    me = lax.axis_index("clus")
    leaves = leaves_of(table)
    for d in range(1, asked.shape[0]):

        def place(b, position, d=d):
            code = asked[d, b]
            mine = quotient(code, leaves) == me

            @pl.when(mine)
            def _():
                def store(value):
                    outs[d - 1][position] = value

                pick(table, remainder(code, leaves), span, store)

            return position + mine.astype(jnp.int32)

        lax.fori_loop(0, asked.shape[1], place, jnp.int32(0))


def serve(asked, table, span, capacity):
    groups, size = asked.shape[0], len(table)
    smem, vmem = pl.BlockSpec(memory_space=pltpu.SMEM), pl.BlockSpec(memory_space=pltpu.VMEM)
    shape = (capacity, span.stop - span.start, table[0].shape[2])
    return pl.pallas_call(
        functools.partial(serve_kernel, size, span),
        in_specs=[smem] + [vmem] * size,
        out_specs=[vmem] * (groups - 1),
        out_shape=[jax.ShapeDtypeStruct(shape, table[0].dtype)] * (groups - 1),
        compiler_params=params(),
        cost_estimate=cost(10**9, 6 * 10**6),
        name="serve",
    )(asked, *table)


def near_kernel(size, leaf, slabs, *refs):
    table, (factors, out, held) = refs[:-3], refs[-3:]
    count, width, points = factors.shape
    spans = points_split(points)

    def gather(b, carry):
        for c in range(len(spans)):

            def store(value, c=c):
                held[b, spans[c], :] = value

            pick(table[c * size : (c + 1) * size], leaf[b], spans[c], store)
        return carry

    lax.fori_loop(0, count, gather, 0)
    row = lax.broadcasted_iota(jnp.int32, (width, out.shape[1]), 0)
    for b in range(count):
        value = dot(factors[b], held[b], NN)
        value = jnp.where(row < slabs[b] * SLAB, value, 0.0)
        out[b] = value.T.astype(out.dtype)


def near_stage(row_leaf, rank_slabs, tables, factors):
    count, width, points = factors.shape
    size, rank = len(tables[0]), tables[0][0].shape[2]
    smem, vmem = pl.BlockSpec(memory_space=pltpu.SMEM), pl.BlockSpec(memory_space=pltpu.VMEM)
    flat = [piece for table in tables for piece in table]
    return pl.pallas_call(
        functools.partial(near_kernel, size),
        in_specs=[smem, smem] + [vmem] * len(flat) + [vmem],
        out_specs=vmem,
        out_shape=jax.ShapeDtypeStruct((count, rank, width), jnp.bfloat16),
        scratch_shapes=[pltpu.VMEM((count, points, rank), flat[0].dtype)],
        compiler_params=params(),
        cost_estimate=cost(10**9, 10 * 10**6),
        name="near",
    )(row_leaf, rank_slabs, *flat, factors)


def far_kernel(groups, size, chunks, code, slabs, near, *refs):
    table, refs = refs[: chunks * size], refs[chunks * size :]
    fetched, (factors, out, held, tally) = refs[: chunks * (groups - 1)], refs[chunks * (groups - 1) :]
    count, width, points = factors.shape
    leaves = leaves_of(table[:size])
    spans = points_split(points)
    me = lax.axis_index("clus")
    for g in range(groups):
        tally[g] = 0

    def gather(b, carry):
        group, leaf = quotient(code[b], leaves), remainder(code[b], leaves)
        position = tally[group]
        tally[group] = position + 1
        away = group ^ me

        @pl.when(away == 0)
        def _():
            for c in range(chunks):

                def store(value, c=c):
                    held[b, spans[c], :] = value

                pick(table[c * size : (c + 1) * size], leaf, spans[c], store)

        for d in range(1, groups):

            @pl.when(away == d)
            def _(d=d):
                for c in range(chunks):
                    piece = fetched[c * (groups - 1) + d - 1]
                    held[b, spans[c], :] = piece[position]

        return carry

    lax.fori_loop(0, count, gather, 0)
    row = lax.broadcasted_iota(jnp.int32, (width, near.shape[1]), 0)
    for first in range(0, count, AHEAD):
        values = [dot(factors[b], held[b], NN) for b in range(first, first + AHEAD)]
        for b in range(first, first + AHEAD):
            value = jnp.where(row < slabs[b] * SLAB, values[b - first], 0.0).astype(near.dtype)
            out[b] = dot(near[b], value, NN)


def far_stage(code, rank_slabs, near, tables, fetched, factors):
    count, width, points = factors.shape
    size, rank = len(tables[0]), tables[0][0].shape[2]
    groups = len(fetched[0]) + 1
    smem, vmem = pl.BlockSpec(memory_space=pltpu.SMEM), pl.BlockSpec(memory_space=pltpu.VMEM)
    flat = [piece for table in tables for piece in table] + [piece for part in fetched for piece in part]
    return pl.pallas_call(
        functools.partial(far_kernel, groups, size, len(tables)),
        in_specs=[smem, smem, vmem] + [vmem] * len(flat) + [vmem],
        out_specs=vmem,
        out_shape=jax.ShapeDtypeStruct((count, rank, rank), jnp.float32),
        scratch_shapes=[
            pltpu.VMEM((count, points, rank), flat[0].dtype),
            pltpu.SMEM((groups,), jnp.int32),
        ],
        compiler_params=params(),
        cost_estimate=cost(10**9, 13 * 10**6),
        name="far",
    )(code, rank_slabs, near, *flat, factors)


def per_device(
    leaf_basis, transfer, block_rows, block_cols, rank_slabs, row_leaf, col_group, col_leaf
):
    groups, size = lax.axis_size("clus"), lax.axis_size("blk")
    capacity = max(2, 2 * block_rows.shape[0] // groups)
    count, points, _ = leaf_basis.shape
    kept = count - early_of(count)
    spans = points_split(points)
    barrier = lax.optimization_barrier
    code = col_group[:, 0] * (count * size) + col_leaf
    far_transfer = shift(transfer, "blk", 1)
    far_basis = shift(leaf_basis, "blk", 1)
    raw = [shift(leaf_basis[kept:], "blk", d) for d in range(2, size, 2)]
    rows, kept_rows, first, second, leaf_work = leaf_stage(leaf_basis, kept)
    rows, kept_rows, first, second, far_basis, far_transfer, raw, code = barrier(
        (rows, kept_rows, first, second, far_basis, far_transfer, raw, code)
    )
    chips = range(4, size, 2)
    table = {d: shift(first, "blk", d) for d in reversed(chips)}
    table[2], table[3] = shift(kept_rows, "blk", 2), shift(kept_rows, "blk", 3)
    asked = joined(code[None], 1)
    *halves, own = parent_top(leaf_basis, transfer, far_basis, far_transfer, rows, raw)
    table, asked, halves, own, second = barrier((table, asked, halves, own, second))
    bit = 2
    while bit < groups:
        asked = joined(asked, bit)
        bit *= 2
    later = {d: shift(second, "blk", d) for d in reversed(chips)}
    for d in chips:
        table[d + 1] = shift(table[d], "blk", 1)
    table[0], table[1] = own, shift(own, "blk", 1)
    served = serve(asked, in_order(table), spans[0], capacity)
    served, halves = barrier((served, halves))
    fetched = [[shift(value, "clus", d + 1) for d, value in enumerate(served)]]
    transfer_new = parent_low(transfer, leaf_work, halves)
    later, transfer_new = barrier((later, transfer_new))
    for d in chips:
        later[d + 1] = shift(later[d], "blk", 1)
    later, fetched[0] = barrier((later, fetched[0]))
    later = {**table, **later}
    served = serve(asked, in_order(later), spans[1], capacity)
    fetched.append([shift(value, "clus", d + 1) for d, value in enumerate(served)])
    tables = [in_order(table), in_order(later)]
    near = near_stage(row_leaf, rank_slabs, tables, jnp.swapaxes(block_rows, 1, 2))
    coupling = far_stage(asked[0], rank_slabs, near, tables, fetched, jnp.swapaxes(block_cols, 1, 2))
    return (coupling, transfer_new)


def solution(mesh):
    placed = (
        P(("clus", "blk"), None, None),
        P(("clus", "blk"), None, None),
        P(("clus", "blk"), None, None),
        P(("clus", "blk"), None, None),
        P(("clus", "blk")),
        P(("clus", "blk")),
        P(("clus", "blk"), None),
        P(("clus", "blk")),
    )
    return jax.shard_map(
        per_device,
        mesh=mesh,
        in_specs=placed,
        out_specs=(P(("clus", "blk"), None, None), P(("clus", "blk"), None, None)),
        check_vma=False,
    )
```

```python
import functools

import jax
import jax.numpy as jnp
from jax import lax
from jax.experimental import pallas as pl
from jax.experimental.pallas import tpu as pltpu
from jax.sharding import PartitionSpec as P

SLAB = 64
PANEL = 8
STRIP = 32
FIRST = 10
AHEAD = 4
VMEM_LIMIT = 24 * 1024 * 1024

NN = (((1,), (0,)), ((), ()))
NT = (((1,), (1,)), ((), ()))
TN = (((0,), (0,)), ((), ()))


def params():
    return pltpu.CompilerParams(vmem_limit_bytes=VMEM_LIMIT)


def cost(flops, moved):
    return pl.CostEstimate(flops=flops, bytes_accessed=moved, transcendentals=0)


def dot(left, right, dims):
    return lax.dot_general(left, right, dims, preferred_element_type=jnp.float32)


def split(value):
    high = value.astype(jnp.bfloat16)
    low = (value - high.astype(jnp.float32)).astype(jnp.bfloat16)
    return high, low


def dot_split(left, right, dims):
    (lh, ll), (rh, rl) = left, right
    return dot(lh, rh, dims) + (dot(lh, rl, dims) + dot(ll, rh, dims))


def lower_part(value):
    rows = lax.broadcasted_iota(jnp.int32, value.shape, 0)
    cols = lax.broadcasted_iota(jnp.int32, value.shape, 1)
    return jnp.where(cols <= rows, value, 0.0)


def factor(work, batch, size):
    lane = lax.broadcasted_iota(jnp.int32, (batch, size), 1)

    def spread(row, column):
        return jnp.broadcast_to(row[:, column : column + 1], (batch, size))

    for top in range(0, size, STRIP):
        rows = [work[pl.ds(top + i, batch, stride=size), :] for i in range(STRIP)]
        for q in range(0, STRIP, PANEL):
            first = top + q
            inside = (lane >= first) & (lane < first + PANEL)
            diag = {
                (i, j): spread(rows[q + i], first + j) for i in range(PANEL) for j in range(i, PANEL)
            }
            scale, upper = [], {}
            for k in range(PANEL):
                inv = lax.rsqrt(diag[k, k])
                scale.append(inv)
                for j in range(k + 1, PANEL):
                    upper[k, j] = diag[k, j] * inv
                for i in range(k + 1, PANEL):
                    for j in range(i, PANEL):
                        diag[i, j] = diag[i, j] - upper[k, i] * upper[k, j]
            done = []
            for k in range(PANEL):
                row = jnp.where(inside, jnp.where(lane == first + k, 1.0, 0.0), rows[q + k])
                for m in range(k):
                    row = row - upper[m, k] * done[m]
                done.append(row * scale[k])
            rows[q : q + PANEL] = done
            for i in range(q + PANEL, STRIP):
                row = jnp.where(inside, 0.0, rows[i])
                for k in range(PANEL):
                    row = row - spread(done[k], top + i) * done[k]
                rows[i] = row
        for i in range(STRIP):
            work[pl.ds(top + i, batch, stride=size), :] = rows[i]
        below = top + STRIP
        if below < size:
            for b in range(batch):
                strip = work[b * size + top : b * size + below, :]
                row = lax.broadcasted_iota(jnp.int32, strip.shape, 0) + top
                column = lax.broadcasted_iota(jnp.int32, strip.shape, 1)
                keep = (column <= row) | (column >= below)
                high, low = split(strip)
                left = jnp.concatenate([high, high, low], axis=0)
                high, low = split(jnp.where(keep, strip, 0.0))
                right = jnp.concatenate([high, low, high], axis=0)
                rest = work[b * size + below : (b + 1) * size, :]
                column = lax.broadcasted_iota(jnp.int32, rest.shape, 1)
                rest = jnp.where((column >= top) & (column < below), 0.0, rest)
                work[b * size + below : (b + 1) * size, :] = rest - dot(left, right, TN)[below:]


def leaf_kernel(basis, rows_out, *rest):
    pieces, work = rest[:-1], rest[-1]
    count, points, rank = basis.shape
    for b in range(count):
        leaf = basis[b]
        work[b * rank : (b + 1) * rank, :] = dot(leaf, leaf, TN)
    factor(work, count, rank)
    for b in range(count):
        high, low = split(lower_part(work[b * rank : (b + 1) * rank, :]))
        leaf = basis[b]
        value = (dot(leaf, high, NT) + dot(leaf, low, NT)).astype(rows_out.dtype)
        rows_out[b] = value
        for span, piece in zip(points_split(points), pieces):
            piece[b] = value[span]


def parent_top_kernel(own_basis, own_transfer, far_basis, far_transfer, weighted, top, cross, corner):
    count, points, rank = own_basis.shape
    half = own_transfer.shape[2] // 2
    for j in range(count):
        other = (j + count // 2) % count
        total = None
        for basis, transfer, c in ((own_basis, own_transfer, j), (far_basis, far_transfer, other)):
            leaf = basis[c]
            gram = split(dot(leaf, leaf, TN))
            value = transfer[c]
            moved = dot_split(gram, split(value), NN)
            if basis is own_basis:
                weighted[c] = moved
            left, right = split(value[:, :half]), split(value[:, half:])
            moved_left, moved_right = split(moved[:, :half]), split(moved[:, half:])
            parts = (
                dot_split(left, moved_left, TN),
                dot_split(right, moved_left, TN),
                dot_split(right, moved_right, TN),
            )
            total = parts if total is None else tuple(a + b for a, b in zip(total, parts))
        top[j * half : (j + 1) * half, :] = total[0]
        cross[j] = total[1]
        corner[j] = total[2]
    factor(top, count, half)


def parent_low_kernel(leaf_work, weighted, top, cross, corner, out, work, coupled):
    count, rank, columns = weighted.shape
    half = columns // 2
    for j in range(count):
        inverse = split(lower_part(top[j * half : (j + 1) * half, :]))
        lower = dot_split(split(cross[j]), inverse, NT)
        coupled[j] = lower
        lower = split(lower)
        work[j * half : (j + 1) * half, :] = corner[j] - dot_split(lower, lower, NT)
    factor(work, count, half)
    for j in range(count):
        leaf_inverse = split(lower_part(leaf_work[j * rank : (j + 1) * rank, :]))
        stacked = dot_split(leaf_inverse, split(weighted[j]), NN)
        inverse = split(lower_part(top[j * half : (j + 1) * half, :]))
        first = dot_split(split(stacked[:, :half]), inverse, NT)
        rest = stacked[:, half:] - dot_split(split(first), split(coupled[j]), NT)
        inverse = split(lower_part(work[j * half : (j + 1) * half, :]))
        out[j, :, :half] = first
        out[j, :, half:] = dot_split(split(rest), inverse, NT)


def leaf_stage(leaf_basis):
    count, points, rank = leaf_basis.shape
    parts = [points] + [span.stop - span.start for span in points_split(points)]
    return pl.pallas_call(
        leaf_kernel,
        out_shape=[jax.ShapeDtypeStruct((count, part, rank), jnp.bfloat16) for part in parts]
        + [jax.ShapeDtypeStruct((count * rank, rank), jnp.float32)],
        compiler_params=params(),
        cost_estimate=cost(10**9, 25 * 10**6),
        name="leaf_factor",
    )(leaf_basis)


def parent_top(leaf_basis, transfer, far_basis, far_transfer):
    count, points, rank = leaf_basis.shape
    half = transfer.shape[2] // 2
    square = jax.ShapeDtypeStruct((count, half, half), jnp.float32)
    return pl.pallas_call(
        parent_top_kernel,
        out_shape=(
            jax.ShapeDtypeStruct(transfer.shape, jnp.float32),
            jax.ShapeDtypeStruct((count * half, half), jnp.float32),
            square,
            square,
        ),
        compiler_params=params(),
        cost_estimate=cost(10**9, 46 * 10**6),
        name="parent_top",
    )(leaf_basis, transfer, far_basis, far_transfer)


def parent_low(transfer, leaf_work, halves):
    count, rank, columns = transfer.shape
    half = columns // 2
    return pl.pallas_call(
        parent_low_kernel,
        out_shape=jax.ShapeDtypeStruct(transfer.shape, jnp.float32),
        scratch_shapes=[
            pltpu.VMEM((count * half, half), jnp.float32),
            pltpu.VMEM((count, half, half), jnp.float32),
        ],
        compiler_params=params(),
        cost_estimate=cost(10**9, 40 * 10**6),
        name="parent_low",
    )(leaf_work, *halves)


def quotient(value, size):
    return value >> (size.bit_length() - 1) if size & (size - 1) == 0 else lax.div(value, size)


def remainder(value, size):
    return value & (size - 1) if size & (size - 1) == 0 else lax.rem(value, size)


def shift(value, axis, d):
    pairs = [(index ^ d, index) for index in range(lax.axis_size(axis))]
    return lax.ppermute(value, axis, pairs)


def joined(values, bit):
    return jnp.concatenate([values, shift(values, "clus", bit)], axis=0)


def in_order(table):
    return [table[d] for d in range(len(table))]


def points_split(points):
    first = points * FIRST // 16
    return (slice(0, first), slice(first, points))


def pick(table, leaf, span, store):
    count = table[0].shape[0]
    place = quotient(leaf, count) ^ lax.axis_index("blk")
    for d in range(len(table)):

        @pl.when(place == d)
        def _():
            rows = span if table[d].shape[1] > span.stop - span.start else slice(None)
            store(table[d][remainder(leaf, count), rows, :])


def serve_kernel(size, span, asked, *refs):
    table, outs = refs[:size], refs[size:]
    me = lax.axis_index("clus")
    leaves = size * table[0].shape[0]
    for d in range(1, asked.shape[0]):

        def place(b, position, d=d):
            code = asked[d, b]
            mine = quotient(code, leaves) == me

            @pl.when(mine)
            def _():
                def store(value):
                    outs[d - 1][position] = value

                pick(table, remainder(code, leaves), span, store)

            return position + mine.astype(jnp.int32)

        lax.fori_loop(0, asked.shape[1], place, jnp.int32(0))


def serve(asked, table, span, capacity):
    groups, size = asked.shape[0], len(table)
    smem, vmem = pl.BlockSpec(memory_space=pltpu.SMEM), pl.BlockSpec(memory_space=pltpu.VMEM)
    shape = (capacity, span.stop - span.start, table[0].shape[2])
    return pl.pallas_call(
        functools.partial(serve_kernel, size, span),
        in_specs=[smem] + [vmem] * size,
        out_specs=[vmem] * (groups - 1),
        out_shape=[jax.ShapeDtypeStruct(shape, table[0].dtype)] * (groups - 1),
        compiler_params=params(),
        cost_estimate=cost(10**9, 6 * 10**6),
        name="serve",
    )(asked, *table)


def near_kernel(size, leaf, slabs, *refs):
    table, (factors, out, held) = refs[:-3], refs[-3:]
    count, width, points = factors.shape
    spans = points_split(points)

    def gather(b, carry):
        for c in range(len(spans)):

            def store(value, c=c):
                held[b, spans[c], :] = value

            pick(table[c * size : (c + 1) * size], leaf[b], spans[c], store)
        return carry

    lax.fori_loop(0, count, gather, 0)
    row = lax.broadcasted_iota(jnp.int32, (width, out.shape[1]), 0)
    for b in range(count):
        value = dot(factors[b], held[b], NN)
        value = jnp.where(row < slabs[b] * SLAB, value, 0.0)
        out[b] = value.T.astype(out.dtype)


def near_stage(row_leaf, rank_slabs, tables, factors):
    count, width, points = factors.shape
    size, rank = len(tables[0]), tables[0][0].shape[2]
    smem, vmem = pl.BlockSpec(memory_space=pltpu.SMEM), pl.BlockSpec(memory_space=pltpu.VMEM)
    flat = [piece for table in tables for piece in table]
    return pl.pallas_call(
        functools.partial(near_kernel, size),
        in_specs=[smem, smem] + [vmem] * len(flat) + [vmem],
        out_specs=vmem,
        out_shape=jax.ShapeDtypeStruct((count, rank, width), jnp.bfloat16),
        scratch_shapes=[pltpu.VMEM((count, points, rank), flat[0].dtype)],
        compiler_params=params(),
        cost_estimate=cost(10**9, 10 * 10**6),
        name="near",
    )(row_leaf, rank_slabs, *flat, factors)


def far_kernel(groups, size, chunks, code, slabs, near, *refs):
    table, refs = refs[: chunks * size], refs[chunks * size :]
    fetched, (factors, out, held, tally) = refs[: chunks * (groups - 1)], refs[chunks * (groups - 1) :]
    count, width, points = factors.shape
    leaves = size * table[0].shape[0]
    spans = points_split(points)
    me = lax.axis_index("clus")
    for g in range(groups):
        tally[g] = 0

    def gather(b, carry):
        group, leaf = quotient(code[b], leaves), remainder(code[b], leaves)
        position = tally[group]
        tally[group] = position + 1
        away = group ^ me

        @pl.when(away == 0)
        def _():
            for c in range(chunks):

                def store(value, c=c):
                    held[b, spans[c], :] = value

                pick(table[c * size : (c + 1) * size], leaf, spans[c], store)

        for d in range(1, groups):

            @pl.when(away == d)
            def _(d=d):
                for c in range(chunks):
                    piece = fetched[c * (groups - 1) + d - 1]
                    held[b, spans[c], :] = piece[position]

        return carry

    lax.fori_loop(0, count, gather, 0)
    row = lax.broadcasted_iota(jnp.int32, (width, near.shape[1]), 0)
    for first in range(0, count, AHEAD):
        values = [dot(factors[b], held[b], NN) for b in range(first, first + AHEAD)]
        for b in range(first, first + AHEAD):
            value = jnp.where(row < slabs[b] * SLAB, values[b - first], 0.0).astype(near.dtype)
            out[b] = dot(near[b], value, NN)


def far_stage(code, rank_slabs, near, tables, fetched, factors):
    count, width, points = factors.shape
    size, rank = len(tables[0]), tables[0][0].shape[2]
    groups = len(fetched[0]) + 1
    smem, vmem = pl.BlockSpec(memory_space=pltpu.SMEM), pl.BlockSpec(memory_space=pltpu.VMEM)
    flat = [piece for table in tables for piece in table] + [piece for part in fetched for piece in part]
    return pl.pallas_call(
        functools.partial(far_kernel, groups, size, len(tables)),
        in_specs=[smem, smem, vmem] + [vmem] * len(flat) + [vmem],
        out_specs=vmem,
        out_shape=jax.ShapeDtypeStruct((count, rank, rank), jnp.float32),
        scratch_shapes=[
            pltpu.VMEM((count, points, rank), flat[0].dtype),
            pltpu.SMEM((groups,), jnp.int32),
        ],
        compiler_params=params(),
        cost_estimate=cost(10**9, 13 * 10**6),
        name="far",
    )(code, rank_slabs, near, *flat, factors)


def per_device(
    leaf_basis, transfer, block_rows, block_cols, rank_slabs, row_leaf, col_group, col_leaf
):
    groups, size = lax.axis_size("clus"), lax.axis_size("blk")
    capacity = max(2, 2 * block_rows.shape[0] // groups)
    spans = points_split(leaf_basis.shape[1])
    barrier = lax.optimization_barrier
    far_basis = shift(leaf_basis, "blk", 1)
    far_transfer = shift(transfer, "blk", 1)
    code = col_group[:, 0] * (leaf_basis.shape[0] * size) + col_leaf
    rows, first, second, leaf_work = leaf_stage(leaf_basis)
    code, rows, first, second, far_basis, far_transfer = barrier(
        (code, rows, first, second, far_basis, far_transfer)
    )
    chips = range(4, size, 2)
    table = {d: shift(first, "blk", d) for d in reversed(chips)}
    close = {0: rows, 1: shift(rows, "blk", 1), 2: shift(rows, "blk", 2)}
    asked = joined(code[None], 1)
    halves = parent_top(leaf_basis, transfer, far_basis, far_transfer)
    asked, close[1], second, halves = barrier((asked, close[1], second, halves))
    later = {d: shift(second, "blk", d) for d in reversed(chips)}
    bit = 2
    while bit < groups:
        asked = joined(asked, bit)
        bit *= 2
    transfer_new = parent_low(transfer, leaf_work, halves)
    table, close, asked, transfer_new = barrier((table, close, asked, transfer_new))
    for d in chips:
        table[d + 1] = shift(table[d], "blk", 1)
    close[3] = shift(close[2], "blk", 1)
    served = serve(asked, in_order(close | table), spans[0], capacity)
    fetched = [[shift(value, "clus", d + 1) for d, value in enumerate(served)]]
    for d in chips:
        later[d + 1] = shift(later[d], "blk", 1)
    later, fetched[0] = barrier((later, fetched[0]))
    served = serve(asked, in_order(close | later), spans[1], capacity)
    fetched.append([shift(value, "clus", d + 1) for d, value in enumerate(served)])
    tables = [in_order(close | table), in_order(close | later)]
    near = near_stage(row_leaf, rank_slabs, tables, jnp.swapaxes(block_rows, 1, 2))
    coupling = far_stage(asked[0], rank_slabs, near, tables, fetched, jnp.swapaxes(block_cols, 1, 2))
    return (coupling, transfer_new)


def solution(mesh):
    placed = (
        P(("clus", "blk"), None, None),
        P(("clus", "blk"), None, None),
        P(("clus", "blk"), None, None),
        P(("clus", "blk"), None, None),
        P(("clus", "blk")),
        P(("clus", "blk")),
        P(("clus", "blk"), None),
        P(("clus", "blk")),
    )
    return jax.shard_map(
        per_device,
        mesh=mesh,
        in_specs=placed,
        out_specs=(P(("clus", "blk"), None, None), P(("clus", "blk"), None, None)),
        check_vma=False,
    )
```

```python
import functools

import jax
import jax.numpy as jnp
from jax import lax
from jax.experimental import pallas as pl
from jax.experimental.pallas import tpu as pltpu
from jax.sharding import PartitionSpec as P

SLAB = 64
PANEL = 8
STRIP = 32
FIRST = 10
AHEAD = 4
VMEM_LIMIT = 24 * 1024 * 1024

NN = (((1,), (0,)), ((), ()))
NT = (((1,), (1,)), ((), ()))
TN = (((0,), (0,)), ((), ()))


def params():
    return pltpu.CompilerParams(vmem_limit_bytes=VMEM_LIMIT)


def cost(flops, moved):
    return pl.CostEstimate(flops=flops, bytes_accessed=moved, transcendentals=0)


def dot(left, right, dims):
    return lax.dot_general(left, right, dims, preferred_element_type=jnp.float32)


def split(value):
    high = value.astype(jnp.bfloat16)
    low = (value - high.astype(jnp.float32)).astype(jnp.bfloat16)
    return high, low


def dot_split(left, right, dims):
    (lh, ll), (rh, rl) = left, right
    return dot(lh, rh, dims) + (dot(lh, rl, dims) + dot(ll, rh, dims))


def lower_part(value):
    rows = lax.broadcasted_iota(jnp.int32, value.shape, 0)
    cols = lax.broadcasted_iota(jnp.int32, value.shape, 1)
    return jnp.where(cols <= rows, value, 0.0)


def factor(work, batch, size):
    lane = lax.broadcasted_iota(jnp.int32, (batch, size), 1)

    def spread(row, column):
        return jnp.broadcast_to(row[:, column : column + 1], (batch, size))

    for top in range(0, size, STRIP):
        rows = [work[pl.ds(top + i, batch, stride=size), :] for i in range(STRIP)]
        for q in range(0, STRIP, PANEL):
            first = top + q
            inside = (lane >= first) & (lane < first + PANEL)
            diag = {
                (i, j): spread(rows[q + i], first + j) for i in range(PANEL) for j in range(i, PANEL)
            }
            scale, upper = [], {}
            for k in range(PANEL):
                inv = lax.rsqrt(diag[k, k])
                scale.append(inv)
                for j in range(k + 1, PANEL):
                    upper[k, j] = diag[k, j] * inv
                for i in range(k + 1, PANEL):
                    for j in range(i, PANEL):
                        diag[i, j] = diag[i, j] - upper[k, i] * upper[k, j]
            done = []
            for k in range(PANEL):
                row = jnp.where(inside, jnp.where(lane == first + k, 1.0, 0.0), rows[q + k])
                for m in range(k):
                    row = row - upper[m, k] * done[m]
                done.append(row * scale[k])
            rows[q : q + PANEL] = done
            for i in range(q + PANEL, STRIP):
                row = jnp.where(inside, 0.0, rows[i])
                for k in range(PANEL):
                    row = row - spread(done[k], top + i) * done[k]
                rows[i] = row
        for i in range(STRIP):
            work[pl.ds(top + i, batch, stride=size), :] = rows[i]
        below = top + STRIP
        if below < size:
            for b in range(batch):
                strip = work[b * size + top : b * size + below, :]
                row = lax.broadcasted_iota(jnp.int32, strip.shape, 0) + top
                column = lax.broadcasted_iota(jnp.int32, strip.shape, 1)
                keep = (column <= row) | (column >= below)
                high, low = split(strip)
                left = jnp.concatenate([high, high, low], axis=0)
                high, low = split(jnp.where(keep, strip, 0.0))
                right = jnp.concatenate([high, low, high], axis=0)
                rest = work[b * size + below : (b + 1) * size, :]
                column = lax.broadcasted_iota(jnp.int32, rest.shape, 1)
                rest = jnp.where((column >= top) & (column < below), 0.0, rest)
                work[b * size + below : (b + 1) * size, :] = rest - dot(left, right, TN)[below:]


def leaf_kernel(basis, rows_out, *rest):
    pieces, work = rest[:-1], rest[-1]
    count, points, rank = basis.shape
    for b in range(count):
        leaf = basis[b]
        work[b * rank : (b + 1) * rank, :] = dot(leaf, leaf, TN)
    factor(work, count, rank)
    for b in range(count):
        high, low = split(lower_part(work[b * rank : (b + 1) * rank, :]))
        leaf = basis[b]
        value = (dot(leaf, high, NT) + dot(leaf, low, NT)).astype(rows_out.dtype)
        rows_out[b] = value
        for span, piece in zip(points_split(points), pieces):
            piece[b] = value[span]


def parent_top_kernel(own_basis, own_transfer, far_basis, far_transfer, weighted, top, cross, corner):
    count, points, rank = own_basis.shape
    half = own_transfer.shape[2] // 2
    for j in range(count):
        other = (j + count // 2) % count
        total = None
        for basis, transfer, c in ((own_basis, own_transfer, j), (far_basis, far_transfer, other)):
            leaf = basis[c]
            gram = split(dot(leaf, leaf, TN))
            value = transfer[c]
            moved = dot_split(gram, split(value), NN)
            if basis is own_basis:
                weighted[c] = moved
            left, right = split(value[:, :half]), split(value[:, half:])
            moved_left, moved_right = split(moved[:, :half]), split(moved[:, half:])
            parts = (
                dot_split(left, moved_left, TN),
                dot_split(right, moved_left, TN),
                dot_split(right, moved_right, TN),
            )
            total = parts if total is None else tuple(a + b for a, b in zip(total, parts))
        top[j * half : (j + 1) * half, :] = total[0]
        cross[j] = total[1]
        corner[j] = total[2]
    factor(top, count, half)


def parent_low_kernel(leaf_work, weighted, top, cross, corner, out, work, coupled):
    count, rank, columns = weighted.shape
    half = columns // 2
    for j in range(count):
        inverse = split(lower_part(top[j * half : (j + 1) * half, :]))
        lower = dot_split(split(cross[j]), inverse, NT)
        coupled[j] = lower
        lower = split(lower)
        work[j * half : (j + 1) * half, :] = corner[j] - dot_split(lower, lower, NT)
    factor(work, count, half)
    for j in range(count):
        leaf_inverse = split(lower_part(leaf_work[j * rank : (j + 1) * rank, :]))
        stacked = dot_split(leaf_inverse, split(weighted[j]), NN)
        inverse = split(lower_part(top[j * half : (j + 1) * half, :]))
        first = dot_split(split(stacked[:, :half]), inverse, NT)
        rest = stacked[:, half:] - dot_split(split(first), split(coupled[j]), NT)
        inverse = split(lower_part(work[j * half : (j + 1) * half, :]))
        out[j, :, :half] = first
        out[j, :, half:] = dot_split(split(rest), inverse, NT)


def leaf_stage(leaf_basis):
    count, points, rank = leaf_basis.shape
    parts = [points] + [span.stop - span.start for span in points_split(points)]
    return pl.pallas_call(
        leaf_kernel,
        out_shape=[jax.ShapeDtypeStruct((count, part, rank), jnp.bfloat16) for part in parts]
        + [jax.ShapeDtypeStruct((count * rank, rank), jnp.float32)],
        compiler_params=params(),
        cost_estimate=cost(10**9, 25 * 10**6),
        name="leaf_factor",
    )(leaf_basis)


def parent_top(leaf_basis, transfer, far_basis, far_transfer):
    count, points, rank = leaf_basis.shape
    half = transfer.shape[2] // 2
    square = jax.ShapeDtypeStruct((count, half, half), jnp.float32)
    return pl.pallas_call(
        parent_top_kernel,
        out_shape=(
            jax.ShapeDtypeStruct(transfer.shape, jnp.float32),
            jax.ShapeDtypeStruct((count * half, half), jnp.float32),
            square,
            square,
        ),
        compiler_params=params(),
        cost_estimate=cost(10**9, 46 * 10**6),
        name="parent_top",
    )(leaf_basis, transfer, far_basis, far_transfer)


def parent_low(transfer, leaf_work, halves):
    count, rank, columns = transfer.shape
    half = columns // 2
    return pl.pallas_call(
        parent_low_kernel,
        out_shape=jax.ShapeDtypeStruct(transfer.shape, jnp.float32),
        scratch_shapes=[
            pltpu.VMEM((count * half, half), jnp.float32),
            pltpu.VMEM((count, half, half), jnp.float32),
        ],
        compiler_params=params(),
        cost_estimate=cost(10**9, 40 * 10**6),
        name="parent_low",
    )(leaf_work, *halves)


def quotient(value, size):
    return value >> (size.bit_length() - 1) if size & (size - 1) == 0 else lax.div(value, size)


def remainder(value, size):
    return value & (size - 1) if size & (size - 1) == 0 else lax.rem(value, size)


def shift(value, axis, d):
    pairs = [(index ^ d, index) for index in range(lax.axis_size(axis))]
    return lax.ppermute(value, axis, pairs)


def joined(values, bit):
    return jnp.concatenate([values, shift(values, "clus", bit)], axis=0)


def in_order(table):
    return [table[d] for d in range(len(table))]


def points_split(points):
    first = points * FIRST // 16
    return (slice(0, first), slice(first, points))


def choose(index, low, high, act):
    if high - low == 1:
        act(low)
        return
    middle = (low + high) // 2
    lax.cond(
        index < middle,
        lambda: choose(index, low, middle, act),
        lambda: choose(index, middle, high, act),
    )


def pick(table, leaf, span, store):
    count = table[0].shape[0]
    local = remainder(leaf, count)

    def take(d):
        rows = span if table[d].shape[1] > span.stop - span.start else slice(None)
        store(table[d][local, rows, :])

    choose(quotient(leaf, count) ^ lax.axis_index("blk"), 0, len(table), take)


def serve_kernel(size, span, asked, *refs):
    table, outs = refs[:size], refs[size:]
    me = lax.axis_index("clus")
    leaves = size * table[0].shape[0]
    for d in range(1, asked.shape[0]):

        def place(b, position, d=d):
            code = asked[d, b]
            mine = quotient(code, leaves) == me

            @pl.when(mine)
            def _():
                def store(value):
                    outs[d - 1][position] = value

                pick(table, remainder(code, leaves), span, store)

            return position + mine.astype(jnp.int32)

        lax.fori_loop(0, asked.shape[1], place, jnp.int32(0), unroll=4)


def serve(asked, table, span, capacity):
    groups, size = asked.shape[0], len(table)
    smem, vmem = pl.BlockSpec(memory_space=pltpu.SMEM), pl.BlockSpec(memory_space=pltpu.VMEM)
    shape = (capacity, span.stop - span.start, table[0].shape[2])
    return pl.pallas_call(
        functools.partial(serve_kernel, size, span),
        in_specs=[smem] + [vmem] * size,
        out_specs=[vmem] * (groups - 1),
        out_shape=[jax.ShapeDtypeStruct(shape, table[0].dtype)] * (groups - 1),
        compiler_params=params(),
        cost_estimate=cost(10**9, 6 * 10**6),
        name="serve",
    )(asked, *table)


def near_kernel(size, leaf, slabs, *refs):
    table, (factors, out, held) = refs[:-3], refs[-3:]
    count, width, points = factors.shape
    spans = points_split(points)

    def gather(b, carry):
        for c in range(len(spans)):

            def store(value, c=c):
                held[b, spans[c], :] = value

            pick(table[c * size : (c + 1) * size], leaf[b], spans[c], store)
        return carry

    lax.fori_loop(0, count, gather, 0)
    row = lax.broadcasted_iota(jnp.int32, (width, out.shape[1]), 0)
    for b in range(count):
        value = dot(factors[b], held[b], NN)
        value = jnp.where(row < slabs[b] * SLAB, value, 0.0)
        out[b] = value.T.astype(out.dtype)


def near_stage(row_leaf, rank_slabs, tables, factors):
    count, width, points = factors.shape
    size, rank = len(tables[0]), tables[0][0].shape[2]
    smem, vmem = pl.BlockSpec(memory_space=pltpu.SMEM), pl.BlockSpec(memory_space=pltpu.VMEM)
    flat = [piece for table in tables for piece in table]
    return pl.pallas_call(
        functools.partial(near_kernel, size),
        in_specs=[smem, smem] + [vmem] * len(flat) + [vmem],
        out_specs=vmem,
        out_shape=jax.ShapeDtypeStruct((count, rank, width), jnp.bfloat16),
        scratch_shapes=[pltpu.VMEM((count, points, rank), flat[0].dtype)],
        compiler_params=params(),
        cost_estimate=cost(10**9, 10 * 10**6),
        name="near",
    )(row_leaf, rank_slabs, *flat, factors)


def far_kernel(groups, size, chunks, code, slabs, near, *refs):
    table, refs = refs[: chunks * size], refs[chunks * size :]
    fetched, (factors, out, held, tally) = refs[: chunks * (groups - 1)], refs[chunks * (groups - 1) :]
    count, width, points = factors.shape
    leaves = size * table[0].shape[0]
    spans = points_split(points)
    me = lax.axis_index("clus")
    for g in range(groups):
        tally[g] = 0

    def gather(b, carry):
        group, leaf = quotient(code[b], leaves), remainder(code[b], leaves)
        position = tally[group]
        tally[group] = position + 1
        away = group ^ me

        def take(d):
            for c in range(chunks):
                if d == 0:

                    def store(value, c=c):
                        held[b, spans[c], :] = value

                    pick(table[c * size : (c + 1) * size], leaf, spans[c], store)
                else:
                    piece = fetched[c * (groups - 1) + d - 1]
                    held[b, spans[c], :] = piece[position]

        choose(away, 0, groups, take)
        return carry

    lax.fori_loop(0, count, gather, 0)
    row = lax.broadcasted_iota(jnp.int32, (width, near.shape[1]), 0)
    for first in range(0, count, AHEAD):
        values = [dot(factors[b], held[b], NN) for b in range(first, first + AHEAD)]
        for b in range(first, first + AHEAD):
            value = jnp.where(row < slabs[b] * SLAB, values[b - first], 0.0).astype(near.dtype)
            out[b] = dot(near[b], value, NN)


def far_stage(code, rank_slabs, near, tables, fetched, factors):
    count, width, points = factors.shape
    size, rank = len(tables[0]), tables[0][0].shape[2]
    groups = len(fetched[0]) + 1
    smem, vmem = pl.BlockSpec(memory_space=pltpu.SMEM), pl.BlockSpec(memory_space=pltpu.VMEM)
    flat = [piece for table in tables for piece in table] + [piece for part in fetched for piece in part]
    return pl.pallas_call(
        functools.partial(far_kernel, groups, size, len(tables)),
        in_specs=[smem, smem, vmem] + [vmem] * len(flat) + [vmem],
        out_specs=vmem,
        out_shape=jax.ShapeDtypeStruct((count, rank, rank), jnp.float32),
        scratch_shapes=[
            pltpu.VMEM((count, points, rank), flat[0].dtype),
            pltpu.SMEM((groups,), jnp.int32),
        ],
        compiler_params=params(),
        cost_estimate=cost(10**9, 13 * 10**6),
        name="far",
    )(code, rank_slabs, near, *flat, factors)


def per_device(
    leaf_basis, transfer, block_rows, block_cols, rank_slabs, row_leaf, col_group, col_leaf
):
    groups, size = lax.axis_size("clus"), lax.axis_size("blk")
    capacity = max(2, 2 * block_rows.shape[0] // groups)
    spans = points_split(leaf_basis.shape[1])
    barrier = lax.optimization_barrier
    far_basis = shift(leaf_basis, "blk", 1)
    far_transfer = shift(transfer, "blk", 1)
    code = col_group[:, 0] * (leaf_basis.shape[0] * size) + col_leaf
    rows, first, second, leaf_work = leaf_stage(leaf_basis)
    code, rows, first, second, far_basis, far_transfer = barrier(
        (code, rows, first, second, far_basis, far_transfer)
    )
    chips = range(4, size, 2)
    table = {d: shift(first, "blk", d) for d in reversed(chips)}
    close = {0: rows, 1: shift(rows, "blk", 1), 2: shift(rows, "blk", 2)}
    asked = joined(code[None], 1)
    halves = parent_top(leaf_basis, transfer, far_basis, far_transfer)
    asked, close[1], second, halves = barrier((asked, close[1], second, halves))
    later = {d: shift(second, "blk", d) for d in reversed(chips)}
    bit = 2
    while bit < groups:
        asked = joined(asked, bit)
        bit *= 2
    transfer_new = parent_low(transfer, leaf_work, halves)
    table, close, asked, transfer_new = barrier((table, close, asked, transfer_new))
    for d in chips:
        table[d + 1] = shift(table[d], "blk", 1)
    close[3] = shift(close[2], "blk", 1)
    served = serve(asked, in_order(close | table), spans[0], capacity)
    fetched = [[shift(value, "clus", d + 1) for d, value in enumerate(served)]]
    for d in chips:
        later[d + 1] = shift(later[d], "blk", 1)
    later, fetched[0] = barrier((later, fetched[0]))
    served = serve(asked, in_order(close | later), spans[1], capacity)
    fetched.append([shift(value, "clus", d + 1) for d, value in enumerate(served)])
    tables = [in_order(close | table), in_order(close | later)]
    near = near_stage(row_leaf, rank_slabs, tables, jnp.swapaxes(block_rows, 1, 2))
    coupling = far_stage(asked[0], rank_slabs, near, tables, fetched, jnp.swapaxes(block_cols, 1, 2))
    return (coupling, transfer_new)


def solution(mesh):
    placed = (
        P(("clus", "blk"), None, None),
        P(("clus", "blk"), None, None),
        P(("clus", "blk"), None, None),
        P(("clus", "blk"), None, None),
        P(("clus", "blk")),
        P(("clus", "blk")),
        P(("clus", "blk"), None),
        P(("clus", "blk")),
    )
    return jax.shard_map(
        per_device,
        mesh=mesh,
        in_specs=placed,
        out_specs=(P(("clus", "blk"), None, None), P(("clus", "blk"), None, None)),
        check_vma=False,
    )
```

```python
import functools

import jax
import jax.numpy as jnp
from jax import lax
from jax.experimental import pallas as pl
from jax.experimental.pallas import tpu as pltpu
from jax.sharding import PartitionSpec as P

SLAB = 64
PANEL = 8
STRIP = 16
FIRST = 10
AHEAD = 4
VMEM_LIMIT = 24 * 1024 * 1024

NN = (((1,), (0,)), ((), ()))
NT = (((1,), (1,)), ((), ()))
TN = (((0,), (0,)), ((), ()))


def params():
    return pltpu.CompilerParams(vmem_limit_bytes=VMEM_LIMIT)


def cost(flops, moved):
    return pl.CostEstimate(flops=flops, bytes_accessed=moved, transcendentals=0)


def dot(left, right, dims):
    return lax.dot_general(left, right, dims, preferred_element_type=jnp.float32)


def split(value):
    high = value.astype(jnp.bfloat16)
    low = (value - high.astype(jnp.float32)).astype(jnp.bfloat16)
    return high, low


def dot_split(left, right, dims):
    (lh, ll), (rh, rl) = left, right
    return dot(lh, rh, dims) + (dot(lh, rl, dims) + dot(ll, rh, dims))


def lower_part(value):
    rows = lax.broadcasted_iota(jnp.int32, value.shape, 0)
    cols = lax.broadcasted_iota(jnp.int32, value.shape, 1)
    return jnp.where(cols <= rows, value, 0.0)


def factor(work, batch, size):
    lane = lax.broadcasted_iota(jnp.int32, (batch, size), 1)

    def spread(row, column):
        return jnp.broadcast_to(row[:, column : column + 1], (batch, size))

    for top in range(0, size, STRIP):
        rows = [work[pl.ds(top + i, batch, stride=size), :] for i in range(STRIP)]
        for q in range(0, STRIP, PANEL):
            first = top + q
            inside = (lane >= first) & (lane < first + PANEL)
            diag = {
                (i, j): spread(rows[q + i], first + j) for i in range(PANEL) for j in range(i, PANEL)
            }
            scale, upper = [], {}
            for k in range(PANEL):
                inv = lax.rsqrt(diag[k, k])
                scale.append(inv)
                for j in range(k + 1, PANEL):
                    upper[k, j] = diag[k, j] * inv
                for i in range(k + 1, PANEL):
                    for j in range(i, PANEL):
                        diag[i, j] = diag[i, j] - upper[k, i] * upper[k, j]
            done = []
            for k in range(PANEL):
                row = jnp.where(inside, jnp.where(lane == first + k, 1.0, 0.0), rows[q + k])
                for m in range(k):
                    row = row - upper[m, k] * done[m]
                done.append(row * scale[k])
            rows[q : q + PANEL] = done
            for i in range(q + PANEL, STRIP):
                row = jnp.where(inside, 0.0, rows[i])
                for k in range(PANEL):
                    row = row - spread(done[k], top + i) * done[k]
                rows[i] = row
        for i in range(STRIP):
            work[pl.ds(top + i, batch, stride=size), :] = rows[i]
        below = top + STRIP
        if below < size:
            for b in range(batch):
                strip = work[b * size + top : b * size + below, :]
                row = lax.broadcasted_iota(jnp.int32, strip.shape, 0) + top
                column = lax.broadcasted_iota(jnp.int32, strip.shape, 1)
                keep = (column <= row) | (column >= below)
                high, low = split(strip)
                left = jnp.concatenate([high, high, low], axis=0)
                high, low = split(jnp.where(keep, strip, 0.0))
                right = jnp.concatenate([high, low, high], axis=0)
                rest = work[b * size + below : (b + 1) * size, :]
                column = lax.broadcasted_iota(jnp.int32, rest.shape, 1)
                rest = jnp.where((column >= top) & (column < below), 0.0, rest)
                work[b * size + below : (b + 1) * size, :] = rest - dot(left, right, TN)[below:]


def leaf_kernel(basis, rows_out, *rest):
    pieces, work = rest[:-1], rest[-1]
    count, points, rank = basis.shape
    for b in range(count):
        leaf = basis[b]
        work[b * rank : (b + 1) * rank, :] = dot(leaf, leaf, TN)
    factor(work, count, rank)
    for b in range(count):
        high, low = split(lower_part(work[b * rank : (b + 1) * rank, :]))
        leaf = basis[b]
        value = (dot(leaf, high, NT) + dot(leaf, low, NT)).astype(rows_out.dtype)
        rows_out[b] = value
        for span, piece in zip(points_split(points), pieces):
            piece[b] = value[span]


def parent_top_kernel(own_basis, own_transfer, far_basis, far_transfer, weighted, top, cross, corner):
    count, points, rank = own_basis.shape
    half = own_transfer.shape[2] // 2
    for j in range(count):
        other = (j + count // 2) % count
        total = None
        for basis, transfer, c in ((own_basis, own_transfer, j), (far_basis, far_transfer, other)):
            leaf = basis[c]
            gram = split(dot(leaf, leaf, TN))
            value = transfer[c]
            moved = dot_split(gram, split(value), NN)
            if basis is own_basis:
                weighted[c] = moved
            left, right = split(value[:, :half]), split(value[:, half:])
            moved_left, moved_right = split(moved[:, :half]), split(moved[:, half:])
            parts = (
                dot_split(left, moved_left, TN),
                dot_split(right, moved_left, TN),
                dot_split(right, moved_right, TN),
            )
            total = parts if total is None else tuple(a + b for a, b in zip(total, parts))
        top[j * half : (j + 1) * half, :] = total[0]
        cross[j] = total[1]
        corner[j] = total[2]
    factor(top, count, half)


def parent_low_kernel(leaf_work, weighted, top, cross, corner, out, work, coupled):
    count, rank, columns = weighted.shape
    half = columns // 2
    for j in range(count):
        inverse = split(lower_part(top[j * half : (j + 1) * half, :]))
        lower = dot_split(split(cross[j]), inverse, NT)
        coupled[j] = lower
        lower = split(lower)
        work[j * half : (j + 1) * half, :] = corner[j] - dot_split(lower, lower, NT)
    factor(work, count, half)
    for j in range(count):
        leaf_inverse = split(lower_part(leaf_work[j * rank : (j + 1) * rank, :]))
        stacked = dot_split(leaf_inverse, split(weighted[j]), NN)
        inverse = split(lower_part(top[j * half : (j + 1) * half, :]))
        first = dot_split(split(stacked[:, :half]), inverse, NT)
        rest = stacked[:, half:] - dot_split(split(first), split(coupled[j]), NT)
        inverse = split(lower_part(work[j * half : (j + 1) * half, :]))
        out[j, :, :half] = first
        out[j, :, half:] = dot_split(split(rest), inverse, NT)


def leaf_stage(leaf_basis):
    count, points, rank = leaf_basis.shape
    parts = [points] + [span.stop - span.start for span in points_split(points)]
    return pl.pallas_call(
        leaf_kernel,
        out_shape=[jax.ShapeDtypeStruct((count, part, rank), jnp.bfloat16) for part in parts]
        + [jax.ShapeDtypeStruct((count * rank, rank), jnp.float32)],
        compiler_params=params(),
        cost_estimate=cost(10**9, 25 * 10**6),
        name="leaf_factor",
    )(leaf_basis)


def parent_top(leaf_basis, transfer, far_basis, far_transfer):
    count, points, rank = leaf_basis.shape
    half = transfer.shape[2] // 2
    square = jax.ShapeDtypeStruct((count, half, half), jnp.float32)
    return pl.pallas_call(
        parent_top_kernel,
        out_shape=(
            jax.ShapeDtypeStruct(transfer.shape, jnp.float32),
            jax.ShapeDtypeStruct((count * half, half), jnp.float32),
            square,
            square,
        ),
        compiler_params=params(),
        cost_estimate=cost(10**9, 46 * 10**6),
        name="parent_top",
    )(leaf_basis, transfer, far_basis, far_transfer)


def parent_low(transfer, leaf_work, halves):
    count, rank, columns = transfer.shape
    half = columns // 2
    return pl.pallas_call(
        parent_low_kernel,
        out_shape=jax.ShapeDtypeStruct(transfer.shape, jnp.float32),
        scratch_shapes=[
            pltpu.VMEM((count * half, half), jnp.float32),
            pltpu.VMEM((count, half, half), jnp.float32),
        ],
        compiler_params=params(),
        cost_estimate=cost(10**9, 40 * 10**6),
        name="parent_low",
    )(leaf_work, *halves)


def quotient(value, size):
    return value >> (size.bit_length() - 1) if size & (size - 1) == 0 else lax.div(value, size)


def remainder(value, size):
    return value & (size - 1) if size & (size - 1) == 0 else lax.rem(value, size)


def shift(value, axis, d):
    pairs = [(index ^ d, index) for index in range(lax.axis_size(axis))]
    return lax.ppermute(value, axis, pairs)


def joined(values, bit):
    return jnp.concatenate([values, shift(values, "clus", bit)], axis=0)


def in_order(table):
    return [table[d] for d in range(len(table))]


def points_split(points):
    first = points * FIRST // 16
    return (slice(0, first), slice(first, points))


def choose(index, low, high, act):
    if high - low == 1:
        act(low)
        return
    middle = (low + high) // 2
    lax.cond(
        index < middle,
        lambda: choose(index, low, middle, act),
        lambda: choose(index, middle, high, act),
    )


def pick(table, leaf, span, store):
    count = table[0].shape[0]
    local = remainder(leaf, count)

    def take(d):
        rows = span if table[d].shape[1] > span.stop - span.start else slice(None)
        store(table[d][local, rows, :])

    choose(quotient(leaf, count) ^ lax.axis_index("blk"), 0, len(table), take)


def serve_kernel(size, span, asked, *refs):
    table, outs = refs[:size], refs[size:]
    me = lax.axis_index("clus")
    leaves = size * table[0].shape[0]
    for d in range(1, asked.shape[0]):

        def place(b, position, d=d):
            code = asked[d, b]
            mine = quotient(code, leaves) == me

            @pl.when(mine)
            def _():
                def store(value):
                    outs[d - 1][position] = value

                pick(table, remainder(code, leaves), span, store)

            return position + mine.astype(jnp.int32)

        lax.fori_loop(0, asked.shape[1], place, jnp.int32(0), unroll=4)


def serve(asked, table, span, capacity):
    groups, size = asked.shape[0], len(table)
    smem, vmem = pl.BlockSpec(memory_space=pltpu.SMEM), pl.BlockSpec(memory_space=pltpu.VMEM)
    shape = (capacity, span.stop - span.start, table[0].shape[2])
    return pl.pallas_call(
        functools.partial(serve_kernel, size, span),
        in_specs=[smem] + [vmem] * size,
        out_specs=[vmem] * (groups - 1),
        out_shape=[jax.ShapeDtypeStruct(shape, table[0].dtype)] * (groups - 1),
        compiler_params=params(),
        cost_estimate=cost(10**9, 6 * 10**6),
        name="serve",
    )(asked, *table)


def near_kernel(size, leaf, slabs, *refs):
    table, (factors, out, held) = refs[:-3], refs[-3:]
    count, width, points = factors.shape
    spans = points_split(points)

    def gather(b, carry):
        for c in range(len(spans)):

            def store(value, c=c):
                held[b, spans[c], :] = value

            pick(table[c * size : (c + 1) * size], leaf[b], spans[c], store)
        return carry

    lax.fori_loop(0, count, gather, 0)
    row = lax.broadcasted_iota(jnp.int32, (width, out.shape[1]), 0)
    for b in range(count):
        value = dot(factors[b], held[b], NN)
        value = jnp.where(row < slabs[b] * SLAB, value, 0.0)
        out[b] = value.T.astype(out.dtype)


def near_stage(row_leaf, rank_slabs, tables, factors):
    count, width, points = factors.shape
    size, rank = len(tables[0]), tables[0][0].shape[2]
    smem, vmem = pl.BlockSpec(memory_space=pltpu.SMEM), pl.BlockSpec(memory_space=pltpu.VMEM)
    flat = [piece for table in tables for piece in table]
    return pl.pallas_call(
        functools.partial(near_kernel, size),
        in_specs=[smem, smem] + [vmem] * len(flat) + [vmem],
        out_specs=vmem,
        out_shape=jax.ShapeDtypeStruct((count, rank, width), jnp.bfloat16),
        scratch_shapes=[pltpu.VMEM((count, points, rank), flat[0].dtype)],
        compiler_params=params(),
        cost_estimate=cost(10**9, 10 * 10**6),
        name="near",
    )(row_leaf, rank_slabs, *flat, factors)


def far_kernel(groups, size, chunks, code, slabs, near, *refs):
    table, refs = refs[: chunks * size], refs[chunks * size :]
    fetched, (factors, out, held, tally) = refs[: chunks * (groups - 1)], refs[chunks * (groups - 1) :]
    count, width, points = factors.shape
    leaves = size * table[0].shape[0]
    spans = points_split(points)
    me = lax.axis_index("clus")
    for g in range(groups):
        tally[g] = 0

    def gather(b, carry):
        group, leaf = quotient(code[b], leaves), remainder(code[b], leaves)
        position = tally[group]
        tally[group] = position + 1
        away = group ^ me

        def take(d):
            for c in range(chunks):
                if d == 0:

                    def store(value, c=c):
                        held[b, spans[c], :] = value

                    pick(table[c * size : (c + 1) * size], leaf, spans[c], store)
                else:
                    piece = fetched[c * (groups - 1) + d - 1]
                    held[b, spans[c], :] = piece[position]

        choose(away, 0, groups, take)
        return carry

    lax.fori_loop(0, count, gather, 0)
    row = lax.broadcasted_iota(jnp.int32, (width, near.shape[1]), 0)
    for first in range(0, count, AHEAD):
        values = [dot(factors[b], held[b], NN) for b in range(first, first + AHEAD)]
        for b in range(first, first + AHEAD):
            value = jnp.where(row < slabs[b] * SLAB, values[b - first], 0.0).astype(near.dtype)
            out[b] = dot(near[b], value, NN)


def far_stage(code, rank_slabs, near, tables, fetched, factors):
    count, width, points = factors.shape
    size, rank = len(tables[0]), tables[0][0].shape[2]
    groups = len(fetched[0]) + 1
    smem, vmem = pl.BlockSpec(memory_space=pltpu.SMEM), pl.BlockSpec(memory_space=pltpu.VMEM)
    flat = [piece for table in tables for piece in table] + [piece for part in fetched for piece in part]
    return pl.pallas_call(
        functools.partial(far_kernel, groups, size, len(tables)),
        in_specs=[smem, smem, vmem] + [vmem] * len(flat) + [vmem],
        out_specs=vmem,
        out_shape=jax.ShapeDtypeStruct((count, rank, rank), jnp.float32),
        scratch_shapes=[
            pltpu.VMEM((count, points, rank), flat[0].dtype),
            pltpu.SMEM((groups,), jnp.int32),
        ],
        compiler_params=params(),
        cost_estimate=cost(10**9, 13 * 10**6),
        name="far",
    )(code, rank_slabs, near, *flat, factors)


def per_device(
    leaf_basis, transfer, block_rows, block_cols, rank_slabs, row_leaf, col_group, col_leaf
):
    groups, size = lax.axis_size("clus"), lax.axis_size("blk")
    capacity = max(2, 2 * block_rows.shape[0] // groups)
    spans = points_split(leaf_basis.shape[1])
    barrier = lax.optimization_barrier
    far_basis = shift(leaf_basis, "blk", 1)
    far_transfer = shift(transfer, "blk", 1)
    code = col_group[:, 0] * (leaf_basis.shape[0] * size) + col_leaf
    rows, first, second, leaf_work = leaf_stage(leaf_basis)
    code, rows, first, second, far_basis, far_transfer = barrier(
        (code, rows, first, second, far_basis, far_transfer)
    )
    chips = range(4, size, 2)
    table = {d: shift(first, "blk", d) for d in reversed(chips)}
    close = {0: rows, 1: shift(rows, "blk", 1), 2: shift(rows, "blk", 2)}
    asked = joined(code[None], 1)
    halves = parent_top(leaf_basis, transfer, far_basis, far_transfer)
    asked, close[1], second, halves = barrier((asked, close[1], second, halves))
    later = {d: shift(second, "blk", d) for d in reversed(chips)}
    bit = 2
    while bit < groups:
        asked = joined(asked, bit)
        bit *= 2
    transfer_new = parent_low(transfer, leaf_work, halves)
    table, close, asked, transfer_new = barrier((table, close, asked, transfer_new))
    for d in chips:
        table[d + 1] = shift(table[d], "blk", 1)
    close[3] = shift(close[2], "blk", 1)
    served = serve(asked, in_order(close | table), spans[0], capacity)
    fetched = [[shift(value, "clus", d + 1) for d, value in enumerate(served)]]
    for d in chips:
        later[d + 1] = shift(later[d], "blk", 1)
    later, fetched[0] = barrier((later, fetched[0]))
    served = serve(asked, in_order(close | later), spans[1], capacity)
    fetched.append([shift(value, "clus", d + 1) for d, value in enumerate(served)])
    tables = [in_order(close | table), in_order(close | later)]
    near = near_stage(row_leaf, rank_slabs, tables, jnp.swapaxes(block_rows, 1, 2))
    coupling = far_stage(asked[0], rank_slabs, near, tables, fetched, jnp.swapaxes(block_cols, 1, 2))
    return (coupling, transfer_new)


def solution(mesh):
    placed = (
        P(("clus", "blk"), None, None),
        P(("clus", "blk"), None, None),
        P(("clus", "blk"), None, None),
        P(("clus", "blk"), None, None),
        P(("clus", "blk")),
        P(("clus", "blk")),
        P(("clus", "blk"), None),
        P(("clus", "blk")),
    )
    return jax.shard_map(
        per_device,
        mesh=mesh,
        in_specs=placed,
        out_specs=(P(("clus", "blk"), None, None), P(("clus", "blk"), None, None)),
        check_vma=False,
    )
```
